32 devices in a mesh: seq: 8 (over z, x), tensor: 4 (over y, core).
Axes of the slice: x: 2, y: 2, z: 4, core: 2. Of those that a mesh axis runs over, the one named last changes fastest.
Arguments:
- inputs: bfloat16 [2, 4096, 1024], P(None, 'seq'), may hold values from -6 to 6
- out_grad: bfloat16 [2, 4096, 1024], P(None, 'seq'), may hold values from -6 to 6
- lengths: int32 [2], replicated, may hold values from 2048 to 4096, as said below
- norm_gain: float32 [1024], replicated, may hold values from 0.5 to 1.5
- query_weight: bfloat16 [1024, 1024], P(None, 'tensor'), may hold values from -0.1875 to 0.1875
- key_weight: bfloat16 [1024, 1024], P(None, 'tensor'), may hold values from -0.1875 to 0.1875
- value_weight: bfloat16 [1024, 1024], P(None, 'tensor'), may hold values from -0.1875 to 0.1875
- out_weight: bfloat16 [1024, 1024], P('tensor'), may hold values from -1.5 to 1.5
- mlp_gain: float32 [1024], replicated, may hold values from 0.5 to 1.5
- up_weight: bfloat16 [1024, 4096], P(None, 'tensor'), may hold values from -0.1875 to 0.1875
- down_weight: bfloat16 [4096, 1024], P('tensor'), may hold values from -0.09375 to 0.09375
- decay_rate: float32 [16, 1024], P(None, 'tensor'), may hold values from 0.00012207031 to 0.03
- state_input: float32 [16, 1024], P(None, 'tensor'), may hold values from -4 to 4
- state_output: float32 [16, 1024], P(None, 'tensor'), may hold values from -1.5 to 1.5
- skip_gain: float32 [1024], P('tensor'), may hold values from -4 to 4
Outputs:
- outputs: bfloat16 [2, 4096, 1024], P(None, 'seq')
- input_grad: bfloat16 [2, 4096, 1024], P(None, 'seq', 'tensor')
- norm_gain_grad: float32 [1024], P('tensor')
- query_weight_grad: float32 [1024, 1024], P(None, 'tensor')
- key_weight_grad: float32 [1024, 1024], P(None, 'tensor')
- value_weight_grad: float32 [1024, 1024], P(None, 'tensor')
- out_weight_grad: float32 [1024, 1024], P('tensor')
- mlp_gain_grad: float32 [1024], replicated
- up_weight_grad: float32 [1024, 4096], P(None, 'tensor')
- down_weight_grad: float32 [4096, 1024], P('tensor')
- decay_rate_grad: float32 [16, 1024], P(None, 'tensor')
- state_input_grad: float32 [16, 1024], P(None, 'tensor')
- state_output_grad: float32 [16, 1024], P(None, 'tensor')
- skip_gain_grad: float32 [1024], P('tensor')
The draws below stay inside these ranges and needn't reach their ends.
Inputs may be any that keep to these rules, and one draw needn't show every extreme that they name: `lengths`: one sequence has length 4096 in every draw.
All inputs are finite; a program needn't handle non-finite values.
Results may differ from the reference program's by a relative error of at most 0.02.
Values may be sent and summed in bfloat16 or wider, within the bound.
No kernel may reach another device: no remote copies, remote signals or barrier semaphores. Data moves between devices by JAX's collectives and lax.ppermute only.
A program may use at most 320 MiB of HBM per device.

```python
import math
from functools import partial
import jax
import jax.numpy as jnp
from jax import lax

D = 1024
HD = 128
FF = 4096
NS = 16
BLK = 512
CTX = 128
MINLEN = 2048
SEQS = 2
L = 4096


def draw_lengths(key, part):
    first_key, second_key = jax.random.split(jax.random.fold_in(key, 17))
    drawn = jax.random.randint(first_key, (SEQS,), MINLEN, L + 1)
    chosen = jax.random.randint(second_key, (), 0, SEQS)
    return jnp.where(jnp.arange(SEQS) == chosen, L, drawn).astype(jnp.int32)


def level_of(own_key, shape, pieces, low, largest):
    level = 1.0
    for position, parts in pieces:
        steps = jax.random.uniform(jax.random.fold_in(jax.random.fold_in(own_key, 6), position), (parts,), jnp.float32, low / len(pieces), largest / len(pieces))
        level = level * jnp.repeat(jnp.exp(steps), shape[position] // parts).reshape((-1,) + (1,) * (len(shape) - 1 - position))
    return level


def bell_draw(key, shape, scale, most, shards=(), dtype=jnp.bfloat16):
    factor_of = level_of(key, shape, shards, -0.22, 0.18) if shards else 1.0
    array = jax.random.normal(key, shape, jnp.float32) * scale * factor_of
    return jnp.minimum(jnp.maximum(array, -most), most).astype(dtype)


def setup_inputs(seed: int = 0) -> dict:
    key_of = jax.random.split(jax.random.key(seed), 16)
    return {
        "inputs": bell_draw(key_of[0], (SEQS, L, D), 1.0, 6.0, ((1, 8),)),
        "out_grad": bell_draw(key_of[1], (SEQS, L, D), 1.0, 6.0, ((1, 8),)),
        "lengths": draw_lengths(jax.random.fold_in(key_of[15], 71), 0),
        "norm_gain": jnp.clip(1.0 + 0.1 * jax.random.normal(key_of[3], (D,), jnp.float32), 0.5, 1.5),
        "query_weight": bell_draw(key_of[4], (D, D), D ** -0.5, 0.1875, ((1, 4),)),
        "key_weight": bell_draw(key_of[5], (D, D), D ** -0.5, 0.1875, ((1, 4),)),
        "value_weight": bell_draw(key_of[6], (D, D), D ** -0.5, 0.1875, ((1, 4),)),
        "out_weight": bell_draw(key_of[7], (D, D), (D // 64) ** -0.5, 1.5, ((0, 4),)),
        "mlp_gain": jnp.clip(1.0 + 0.1 * jax.random.normal(key_of[8], (D,), jnp.float32), 0.5, 1.5),
        "up_weight": bell_draw(key_of[9], (D, FF), D ** -0.5, 0.1875, ((1, 4),)),
        "down_weight": bell_draw(key_of[10], (FF, D), FF ** -0.5, 0.09375, ((0, 4),)),
        "decay_rate": jnp.clip(jnp.exp(math.log(0.03) - 5.5043554 * jax.random.uniform(key_of[11], (NS, D), jnp.float32) ** level_of(key_of[11], (NS, D), ((1, 4),), -0.2, 0.2)), 0.00012207031, 0.03),
        "state_input": bell_draw(key_of[12], (NS, D), 1.0, 4.0, ((1, 4),), jnp.float32),
        "state_output": bell_draw(key_of[13], (NS, D), NS ** -0.5, 1.5, ((1, 4),), jnp.float32),
        "skip_gain": bell_draw(key_of[14], (D,), 1.0, 4.0, ((0, 4),), jnp.float32),
    }


epsilon = 1e-06
highest = lax.Precision.HIGHEST

@jax.custom_vjp
def low(v):
    return lax.optimization_barrier(v.astype(jnp.bfloat16)).astype(jnp.float32)

@jax.custom_vjp
def low_back(v):
    return v

def low_keep(v):
    return (low(v), None)

def low_pass(kept, grad):
    return (grad,)

def back_keep(v):
    return (v, None)

def back_low(kept, grad):
    return (low(grad),)
low.defvjp(low_keep, low_pass)
low_back.defvjp(back_keep, back_low)

def rounded_both(value):
    return low(low_back(value))

def product(left, right):
    return jnp.dot(left, right, precision=highest)

def rms_norm(value, gain):
    return value * lax.rsqrt(lax.optimization_barrier(jnp.mean(value * value, -1, keepdims=True)) + epsilon) * gain

def combine_pair(early, late):
    return (early[0] * late[0], late[0] * early[1] + late[1])

def exact_gelu(value):
    return jax.nn.gelu(value, approximate=False)

def state_block(decay, in_coeff, state_output, skip_gain, carry, chan_block):
    count = chan_block.shape[0]
    elements = (jnp.broadcast_to(decay, (count,) + decay.shape), in_coeff[None] * chan_block[:, None, :])
    cumul, local = lax.associative_scan(combine_pair, elements, axis=0)
    states = local + cumul * carry[None]
    return (states[-1], lax.optimization_barrier(jnp.sum(state_output[None] * states, 1)) + skip_gain * chan_block)

def attend_block(allowed, item):
    query, keys, values = item
    heads = query.shape[1] // HD
    query_heads = query.reshape(query.shape[0], heads, HD)
    key_heads = keys.reshape(keys.shape[0], heads, HD)
    value_heads = values.reshape(values.shape[0], heads, HD)
    scores = jnp.einsum('qhd,khd->hqk', query_heads, key_heads, precision=highest) * HD ** (-0.5)
    scores = jnp.where(allowed[None], low_back(scores), -1e+30)
    top = lax.optimization_barrier(jnp.max(scores, -1, keepdims=True))
    expo = jnp.exp(scores - top)
    probs = expo / lax.optimization_barrier(jnp.sum(expo, -1, keepdims=True))
    result = jnp.einsum('hqk,khd->qhd', low(probs), value_heads, precision=highest)
    return result.reshape(query.shape)

def layer(inputs, norm_gain, query_weight, key_weight, value_weight, out_weight, mlp_gain, up_weight, down_weight, decay_rate, state_input, state_output, skip_gain):
    length = inputs.shape[0]
    blocks = length // BLK
    stride = BLK // CTX
    normed1 = rms_norm(inputs, norm_gain)
    normed_low = low(normed1)
    decay = jnp.exp(-decay_rate)
    in_coeff = jnp.sqrt(-jnp.expm1(-2.0 * decay_rate)) * state_input
    stepper = jax.checkpoint(partial(state_block, decay, in_coeff, state_output, skip_gain))
    _, mixed = lax.scan(stepper, jnp.zeros(decay.shape, jnp.float32), normed1.reshape(blocks, BLK, -1))
    ctx_low = low(mixed.reshape(blocks, CTX, stride, -1)[:, :, stride - 1, :])
    query = rounded_both(product(normed_low, query_weight)).reshape(blocks, BLK, -1)
    key_self = rounded_both(product(normed_low, key_weight)).reshape(blocks, BLK, -1)
    value_self = rounded_both(product(normed_low, value_weight)).reshape(blocks, BLK, -1)
    key_ctx = rounded_both(jnp.einsum('bcd,de->bce', ctx_low, key_weight, precision=highest))
    value_ctx = rounded_both(jnp.einsum('bcd,de->bce', ctx_low, value_weight, precision=highest))
    keys = jnp.concatenate([key_ctx, key_self], 1)
    values = jnp.concatenate([value_ctx, value_self], 1)
    rows = jnp.arange(BLK)[:, None]
    ctx_cols = stride * jnp.arange(CTX) + stride - 1
    allowed = jnp.concatenate([ctx_cols[None, :] <= rows, jnp.arange(BLK)[None, :] <= rows], 1)
    attended = lax.map(jax.checkpoint(partial(attend_block, allowed)), (query, keys, values))
    attended = rounded_both(attended.reshape(length, -1))
    middle = inputs + low_back(product(attended, out_weight))
    normed2 = low(rms_norm(middle, mlp_gain))
    pre_act = low_back(product(normed2, up_weight))
    return middle + product(low(exact_gelu(pre_act)), down_weight)

def reference(inputs, out_grad, lengths, norm_gain, query_weight, key_weight, value_weight, out_weight, mlp_gain, up_weight, down_weight, decay_rate, state_input, state_output, skip_gain):
    weights = tuple((weight.astype(jnp.float32) for weight in (norm_gain, query_weight, key_weight, value_weight, out_weight, mlp_gain, up_weight, down_weight, decay_rate, state_input, state_output, skip_gain)))
    positions = jnp.arange(inputs.shape[1])

    def one_sequence(totals, item):
        seq_in, seq_cot, seq_len = item
        result, pullback = jax.vjp(layer, seq_in.astype(jnp.float32), *weights)
        valid = (positions < seq_len).astype(jnp.float32)[:, None]
        grads = pullback(seq_cot.astype(jnp.float32) * valid)
        totals = tuple((total + grad for total, grad in zip(totals, grads[1:])))
        return (totals, (result.astype(jnp.bfloat16), grads[0].astype(jnp.bfloat16)))
    zeros = tuple((jnp.zeros(weight.shape, jnp.float32) for weight in weights))
    totals, (outputs, input_grad) = lax.scan(one_sequence, zeros, (inputs, out_grad, lengths))
    return (outputs, input_grad, totals[0], totals[1], totals[2], totals[3], totals[4], totals[5], totals[6], totals[7], totals[8], totals[9], totals[10], totals[11])
```

```python
import functools

import jax
import jax.numpy as jnp
from jax import lax
from jax.experimental import pallas as pl
from jax.experimental.pallas import tpu as pltpu
from jax.sharding import PartitionSpec as P

HD = 128
NS = 16
CTX = 128
SUB = 8
EPS = 1e-06
F32 = jnp.float32
BF16 = jnp.bfloat16
MIB = 1 << 20


def nn(a, b):
    return lax.dot_general(a, b, (((1,), (0,)), ((), ())), preferred_element_type=F32)


def nt(a, b):
    return lax.dot_general(a, b, (((1,), (1,)), ((), ())), preferred_element_type=F32)


def tn(a, b):
    return lax.dot_general(a, b, (((0,), (0,)), ((), ())), preferred_element_type=F32)


def swap(value, axis, bit):
    count = lax.axis_size(axis)
    return lax.ppermute(value, axis, [(i, i ^ bit) for i in range(count)])


def low_bits(count):
    bit, out = 1, []
    while bit < count:
        out.append(bit)
        bit *= 2
    return out


def sds(shape, dtype):
    return jax.ShapeDtypeStruct(shape, dtype)


def vmem():
    return pl.BlockSpec(memory_space=pltpu.VMEM)


def smem():
    return pl.BlockSpec(memory_space=pltpu.SMEM)


def params(limit_mib, sems=None):
    return pltpu.CompilerParams(vmem_limit_bytes=limit_mib * MIB, dimension_semantics=sems)


def cost(flops, nbytes, trans=0):
    return pl.CostEstimate(flops=int(flops), bytes_accessed=int(nbytes), transcendentals=int(trans))


def lanes(tile):
    return slice(tile * HD, (tile + 1) * HD)


def spread(table, rows, factor=None):
    for n in range(NS):
        row = rows[n : n + 1, :]
        if factor is not None:
            row = jnp.exp(row * factor)
        table[n] = jnp.broadcast_to(row, table.shape[1:])


def scan_step(hat_ref, decay_tab, jump_tab, group, state, stride, seg):
    tiles = hat_ref.shape[0]
    taps = [[hat_ref[t, pl.ds(group * stride + i, SUB, stride=seg), :] for i in range(stride)] for t in range(tiles)]
    out = []
    for n in range(NS):
        for t in range(tiles):
            decay = decay_tab[n, :, lanes(t)]
            inner = taps[t][0]
            for tap in taps[t][1:]:
                inner = inner * decay + tap
            out.append(state[n * tiles + t] * jump_tab[n, :, lanes(t)] + inner)
    return tuple(out), taps


def segment_ends(state, rate, seg, seqs, seg_ref, end_ref, forward):
    per = SUB // seqs
    tiles = rate.shape[1] // HD
    place = lax.rem(lax.broadcasted_iota(jnp.int32, (SUB, HD), 0), per)
    away = ((per - 1 - place if forward else place) * seg).astype(F32)
    for n in range(NS):
        for t in range(tiles):
            now = state[n * tiles + t]
            seg_ref[n, :, lanes(t)] = now
            part = now * jnp.exp(-rate[n : n + 1, lanes(t)] * away)
            for s in range(seqs):
                end_ref[s, n : n + 1, lanes(t)] = jnp.sum(part[s * per : (s + 1) * per], 0, keepdims=True)


def entry_states(entry_ref, carry_ref, seg_ref, hop, seqs, forward):
    per = SUB // seqs
    for n in range(NS):
        step = hop[n : n + 1, :]
        for s in range(seqs):
            now = carry_ref[s, n : n + 1, :]
            for k in range(per):
                q = s * per + (k if forward else per - 1 - k)
                entry_ref[n, q : q + 1, :] = now
                if k < per - 1:
                    now = now * step + seg_ref[n, q : q + 1, :]


def read_state(ref):
    tiles = ref.shape[2] // HD
    return tuple(ref[n, :, lanes(t)] for n in range(NS) for t in range(tiles))


def enter_kernel(seqs, stride, x_ref, xc_ref, gain_ref, rate_ref, low_ref, hat_ref, inv_ref, seg_ref, fin_ref, decay_tab, jump_tab):
    rows, width = x_ref.shape
    seg = rows // SUB
    tiles = hat_ref.shape[0]
    step = 64
    gain = gain_ref[...]

    def norm(i, carry):
        at = pl.ds(pl.multiple_of(i * step, step), step)
        x = x_ref[at, :].astype(F32)
        inv = lax.rsqrt(jnp.sum(x * x, -1, keepdims=True) * (1.0 / width) + EPS)
        low_ref[at, :] = (x * inv * gain).astype(BF16)
        inv_ref[at, :] = inv
        for t in range(tiles):
            hat_ref[t, at, :] = xc_ref[at, lanes(t)].astype(F32) * inv
        return carry

    lax.fori_loop(0, rows // step, norm, 0)
    rate = rate_ref[...]
    spread(decay_tab, rate, -1.0)
    spread(jump_tab, rate, -float(stride))

    def group(g, state):
        return scan_step(hat_ref, decay_tab, jump_tab, g, state, stride, seg)[0]

    state = lax.fori_loop(0, seg // stride, group, (jnp.zeros((SUB, HD), F32),) * (NS * tiles))
    segment_ends(state, rate, seg, seqs, seg_ref, fin_ref, True)


def context_kernel(seqs, stride, hat_ref, seg_ref, carry_ref, rate_ref, coeff_ref, sout_ref, skip_ref, gain_ref, ctx_ref, entry_ref, decay_tab, jump_tab, out_tab, flat):
    tiles = hat_ref.shape[0]
    seg = hat_ref.shape[1] // SUB
    rate = rate_ref[...]
    spread(decay_tab, rate, -1.0)
    spread(jump_tab, rate, -float(stride))
    spread(out_tab, coeff_ref[...] * sout_ref[...] * gain_ref[...])
    entry_states(entry_ref, carry_ref, seg_ref, jnp.exp(rate * (-float(seg))), seqs, True)
    skip = skip_ref[...] * gain_ref[...]
    groups = seg // stride

    def group(g, state):
        state, taps = scan_step(hat_ref, decay_tab, jump_tab, g, state, stride, seg)
        for t in range(tiles):
            total = skip[:, lanes(t)] * taps[t][-1]
            for n in range(NS):
                total = total + out_tab[n, :, lanes(t)] * state[n * tiles + t]
            flat[t, pl.ds(g, SUB, stride=groups), :] = total
        return state

    lax.fori_loop(0, groups, group, read_state(entry_ref))
    for t in range(tiles):
        ctx_ref[:, lanes(t)] = flat[t].astype(BF16)


def lead_kernel(seqs, stride, near_ref, far_ref, rate_ref, grad_ref, segb_ref, lead_ref, jump_tab):
    tiles = grad_ref.shape[0]
    groups = grad_ref.shape[1] // SUB
    for t in range(tiles):
        grad_ref[t] = near_ref[:, lanes(t)].astype(F32) + far_ref[:, lanes(t)].astype(F32)
    rate = rate_ref[...]
    spread(jump_tab, rate, -float(stride))

    def group(i, state):
        g = groups - 1 - i
        grads = [grad_ref[t, pl.ds(g, SUB, stride=groups), :] for t in range(tiles)]
        return tuple(state[n * tiles + t] * jump_tab[n, :, lanes(t)] + grads[t] for n in range(NS) for t in range(tiles))

    state = lax.fori_loop(0, groups, group, (jnp.zeros((SUB, HD), F32),) * (NS * tiles))
    segment_ends(state, rate, groups * stride, seqs, segb_ref, lead_ref, False)


def state_back_kernel(
    seqs, stride, hat_ref, grad_ref, entry_ref, segb_ref, carryb_ref, rate_ref, root_ref, sin_ref, sout_ref, skip_ref, gain_ref,
    back_ref, rateg_ref, sing_ref, soutg_ref, skipg_ref,
    decay_tab, jump_tab, tap_tab, entryb, states, sums,
):
    tiles = hat_ref.shape[0]
    seg = hat_ref.shape[1] // SUB
    groups = seg // stride
    rate = rate_ref[...]
    root = root_ref[...]
    s_in = sin_ref[...]
    s_out = sout_ref[...]
    gain = gain_ref[...]
    coeff = root * s_in
    spread(decay_tab, rate, -1.0)
    spread(jump_tab, rate, -float(stride))
    both = coeff * s_out
    for i in range(stride):
        spread(tap_tab.at[i], both * jnp.exp(rate * (-float(stride - 1 - i))))
    entry_states(entryb, carryb_ref, segb_ref, jnp.exp(rate * (-float(seg))), seqs, False)
    skip = skip_ref[...]

    def forward(g, state):
        for n in range(NS):
            for t in range(tiles):
                states[g, n, :, lanes(t)] = state[n * tiles + t]
        return scan_step(hat_ref, decay_tab, jump_tab, g, state, stride, seg)[0]

    last = lax.fori_loop(0, groups, forward, read_state(entry_ref))
    for n in range(NS):
        for t in range(tiles):
            states[groups, n, :, lanes(t)] = last[n * tiles + t]
    zero = jnp.zeros((SUB, HD), F32)

    def span(g, i):
        return pl.ds(g * stride + i, SUB, stride=seg)

    for t in range(tiles):

        def skips(g, total, t=t):
            grad = grad_ref[t, pl.ds(g, SUB, stride=groups), :]
            for i in range(stride - 1):
                back_ref[t, span(g, i), :] = zero
            back_ref[t, span(g, stride - 1), :] = grad * skip[:, lanes(t)]
            return total + grad * hat_ref[t, span(g, stride - 1), :]

        total = lax.fori_loop(0, groups, skips, zero)
        skipg_ref[:, lanes(t)] = jnp.sum(total, 0, keepdims=True) * gain[:, lanes(t)]
    lot = 4
    kinds = stride + 2
    for t in range(tiles):
        for first in range(0, NS, lot):
            names = range(first, first + lot)

            def group(i, carry, t=t, names=names):
                g = groups - 1 - i
                adj, acc = carry
                grad = grad_ref[t, pl.ds(g, SUB, stride=groups), :]
                taps = [hat_ref[t, span(g, i), :] for i in range(stride)]
                backs = [back_ref[t, span(g, i), :] for i in range(stride)]
                new_adj, new_acc = [], []
                for k, n in enumerate(names):
                    now = adj[k] * jump_tab[n, :, lanes(t)] + grad
                    new_adj.append(now)
                    for i in range(stride):
                        backs[i] = backs[i] + tap_tab[i, n, :, lanes(t)] * now
                        new_acc.append(acc[k * kinds + i] + now * taps[i])
                    new_acc.append(acc[k * kinds + stride] + now * states[g, n, :, lanes(t)])
                    new_acc.append(acc[k * kinds + stride + 1] + grad * states[g + 1, n, :, lanes(t)])
                for i in range(stride):
                    back_ref[t, span(g, i), :] = backs[i]
                return tuple(new_adj), tuple(new_acc)

            start = (tuple(entryb[n, :, lanes(t)] for n in names), (zero,) * (lot * kinds))
            _, acc = lax.fori_loop(0, groups, group, start)
            for k, n in enumerate(names):
                for j in range(kinds):
                    sums[j, n : n + 1, lanes(t)] = jnp.sum(acc[k * kinds + j], 0, keepdims=True)
    decay = jnp.exp(-rate)
    powers = [jnp.ones_like(rate)]
    for _ in range(stride):
        powers.append(powers[-1] * decay)
    coeff_grad = sum(powers[stride - 1 - i] * sums[i] for i in range(stride)) * s_out * gain
    decay_grad = float(stride) * powers[stride - 1] * sums[stride]
    for i in range(stride - 1):
        decay_grad = decay_grad + float(stride - 1 - i) * powers[stride - 2 - i] * sums[i]
    decay_grad = decay_grad * coeff * s_out * gain
    soutg_ref[...] = coeff * gain * sums[stride + 1]
    sing_ref[...] = coeff_grad * root
    rateg_ref[...] = coeff_grad * s_in * (decay * decay / root) - decay * decay_grad


def carried(value, hop, axis, forward):
    count = lax.axis_size(axis)
    mine = lax.axis_index(axis)
    whole = value
    enter = jnp.zeros_like(value)
    for bit in low_bits(count):
        other = swap(whole, axis, bit)
        upper = (mine & bit) != 0
        offset = mine & (bit - 1)
        if not forward:
            upper = jnp.logical_not(upper)
            offset = bit - 1 - offset
        enter = jnp.where(upper, enter + hop(offset) * other, enter)
        span = hop(bit)
        whole = jnp.where(upper, whole + span * other, other + span * whole)
    return enter


def qkv_kernel(x_ref, wq_ref, wk_ref, wv_ref, q_ref, k_ref, v_ref):
    x = x_ref[...]
    q_ref[...] = nn(x, wq_ref[...]).astype(BF16)
    k_ref[...] = nn(x, wk_ref[...]).astype(BF16)
    v_ref[...] = nn(x, wv_ref[...]).astype(BF16)


def masks(first, tile, block, stride):
    row = lax.broadcasted_iota(jnp.int32, (tile, CTX), 0) + first
    col = lax.broadcasted_iota(jnp.int32, (tile, CTX), 1)
    side = stride * col + (stride - 1) <= row
    row = lax.broadcasted_iota(jnp.int32, (tile, block), 0) + first
    col = lax.broadcasted_iota(jnp.int32, (tile, block), 1)
    return side, col <= row


def attend_kernel(parts, scale, idx_ref, q_ref, k_ref, v_ref, wk_ref, wv_ref, *rest):
    ctx_refs, (out_ref, kc_ref, vc_ref, lse_ref) = rest[:parts], rest[parts:]
    block, width = q_ref.shape
    stride = block // CTX
    idx = idx_ref[0]
    key_c = jnp.zeros((CTX, width), F32)
    val_c = jnp.zeros((CTX, width), F32)
    for p in range(parts):
        at = pl.ds(pl.multiple_of((idx ^ p) * width, width), width)
        key_c = key_c + nn(ctx_refs[p][...], wk_ref[at, :])
        val_c = val_c + nn(ctx_refs[p][...], wv_ref[at, :])
    kc_ref[...] = key_c.astype(BF16)
    vc_ref[...] = val_c.astype(BF16)
    tile = min(256, block)
    for h in range(width // HD):
        cols = slice(h * HD, (h + 1) * HD)
        for first in range(0, block, tile):
            seen = first + tile
            rows = slice(first, seen)
            q = q_ref[rows, cols]
            side_ok, own_ok = masks(first, tile, seen, stride)
            side = jnp.where(side_ok, nt(q, kc_ref[:, cols]), -1e30)
            own = jnp.where(own_ok, nt(q, k_ref[:seen, cols]), -1e30)
            top = jnp.maximum(jnp.max(side, -1, keepdims=True), jnp.max(own, -1, keepdims=True))
            side = jnp.exp((side - top) * scale)
            own = jnp.exp((own - top) * scale)
            total = jnp.sum(side, -1, keepdims=True) + jnp.sum(own, -1, keepdims=True)
            share = 1.0 / total
            got = nn((side * share).astype(BF16), vc_ref[:, cols]) + nn((own * share).astype(BF16), v_ref[:seen, cols])
            out_ref[rows, cols] = got.astype(BF16)
            lse_ref[rows, h : h + 1] = top * scale + jnp.log(total)


def attend_back_kernel(
    seq, scale, info_ref, mid_ref, near_ref, far_ref, grad_ref, gain_ref, wo_ref, q_ref, k_ref, v_ref, kc_ref, vc_ref, lse_ref,
    wq_ref, wk_ref, wv_ref,
    low_ref, slice_ref, gaing_ref, dq_ref, dk_ref, dv_ref, dkc_ref, dvc_ref, ckeep_ref, csend_ref, nkeep_ref, nsend_ref,
    n2_ref, full_ref, key_acc, val_acc, skey_acc, sval_acc,
):
    block, width = q_ref.shape
    model = mid_ref.shape[1]
    half = model // 2
    stride = block // CTX
    idx, mine, limit = info_ref[0], info_ref[1], info_ref[2 + seq]
    n2_ref[:, pl.ds(pl.multiple_of(mine * half, half), half)] = near_ref[...]
    n2_ref[:, pl.ds(pl.multiple_of((1 - mine) * half, half), half)] = far_ref[...]
    gain = gain_ref[...]
    step = 64

    def norm(i, total):
        at = pl.ds(pl.multiple_of(i * step, step), step)
        mid = mid_ref[at, :]
        inv = lax.rsqrt(jnp.sum(mid * mid, -1, keepdims=True) * (1.0 / model) + EPS)
        hat = mid * inv
        n2 = n2_ref[at, :].astype(F32)
        prod = n2 * hat
        h2 = n2 * gain
        mean = jnp.sum(h2 * hat, -1, keepdims=True) * (1.0 / model)
        place = lax.broadcasted_iota(jnp.int32, (step, 1), 0) + i * step
        cot = jnp.where(place < limit, grad_ref[at, :].astype(F32), 0.0)
        grad = cot + inv * (h2 - hat * mean)
        full_ref[at, :] = grad
        low_ref[at, :] = grad.astype(BF16)
        return total + jnp.sum(prod, 0, keepdims=True)

    gaing_ref[...] = lax.fori_loop(0, block // step, norm, jnp.zeros((1, model), F32))
    slice_ref[...] = full_ref[:, pl.ds(pl.multiple_of(idx * width, width), width)]
    att_grad = nt(low_ref[...], wo_ref[...]).astype(BF16)
    tile = min(256, block)
    for h in range(width // HD):
        cols = slice(h * HD, (h + 1) * HD)
        for first in range(0, block, tile):
            seen = first + tile
            rows = slice(first, seen)
            q = q_ref[rows, cols]
            grad = att_grad[rows, cols]
            lse = lse_ref[rows, h : h + 1]
            side_ok, own_ok = masks(first, tile, seen, stride)
            kc, k = kc_ref[:, cols], k_ref[:seen, cols]
            side = jnp.exp(jnp.where(side_ok, nt(q, kc) * scale - lse, -1e30))
            own = jnp.exp(jnp.where(own_ok, nt(q, k) * scale - lse, -1e30))
            dside = nt(grad, vc_ref[:, cols])
            down = nt(grad, v_ref[:seen, cols])
            term = jnp.sum(side * dside, -1, keepdims=True) + jnp.sum(own * down, -1, keepdims=True)
            dside = (side * (dside - term)).astype(BF16)
            down = (own * (down - term)).astype(BF16)
            dq_ref[rows, cols] = ((nn(dside, kc) + nn(down, k)) * scale).astype(BF16)
            side = side.astype(BF16)
            own = own.astype(BF16)
            last = first + tile >= block
            fresh = first == 0
            for acc, score, right in (
                (skey_acc, dside, q),
                (sval_acc, side, grad),
            ):
                got = tn(score, right)
                acc[...] = got if fresh else acc[...] + got
            for acc, score, right in (
                (key_acc, down, q),
                (val_acc, own, grad),
            ):
                got = tn(score, right)
                if fresh:
                    acc[:seen, :] = got
                else:
                    acc[:first, :] = acc[:first, :] + got[:first]
                    acc[first:seen, :] = got[first:]
            if last:
                dk_ref[:, cols] = (key_acc[...] * scale).astype(BF16)
                dv_ref[:, cols] = val_acc[...].astype(BF16)
                dkc_ref[:, cols] = (skey_acc[...] * scale).astype(BF16)
                dvc_ref[:, cols] = sval_acc[...].astype(BF16)
    count = model // width
    for p in range(count):
        at = pl.ds(pl.multiple_of((idx ^ p) * width, width), width)
        wk, wv = wk_ref[at, :], wv_ref[at, :]
        ctx = nt(dkc_ref[...], wk) + nt(dvc_ref[...], wv)
        (csend_ref if p % 2 else ckeep_ref)[p // 2] = ctx.astype(BF16)
    for p in range(count):
        at = pl.ds(pl.multiple_of((idx ^ p) * width, width), width)
        own = nt(dq_ref[...], wq_ref[at, :]) + nt(dk_ref[...], wk_ref[at, :]) + nt(dv_ref[...], wv_ref[at, :])
        (nsend_ref if p % 2 else nkeep_ref)[p // 2] = own.astype(BF16)


def feed_kernel(parts, tile, seq, info_ref, x_ref, grad_ref, gain_ref, up_ref, down_ref, *rest):
    att_refs, wo_refs = rest[:parts], rest[parts : 2 * parts]
    mid_ref, n2_ref, act_ref, pre_ref, cot_ref, keep_ref, send_ref, okeep_ref, osend_ref = rest[2 * parts :]
    model = x_ref.shape[1]
    half = model // 2
    mine, limit = info_ref[1], info_ref[2 + seq]
    mid = x_ref[...].astype(F32)
    got = nn(att_refs[0][...], wo_refs[0][...])
    for p in range(1, parts):
        got = got + nn(att_refs[p][...], wo_refs[p][...])
    mid = mid + got
    mid_ref[...] = mid
    inv = lax.rsqrt(jnp.sum(mid * mid, -1, keepdims=True) * (1.0 / model) + EPS)
    n2_ref[...] = (mid * inv * gain_ref[...]).astype(BF16)
    place = lax.broadcasted_iota(jnp.int32, (tile, 1), 0) + pl.program_id(0) * tile
    cot = jnp.where(place < limit, grad_ref[...].astype(F32), 0.0).astype(BF16)
    cot_ref[...] = cot
    pre = nn(n2_ref[...], up_ref[...])
    cdf = 0.5 * (1.0 + lax.erf(pre * 0.7071067811865476))
    pdf = jnp.exp(pre * pre * -0.5) * 0.3989422804014327
    act_ref[...] = (pre * cdf).astype(BF16)
    pull = nt(cot, down_ref[...])
    pre_ref[...] = (pull * (cdf + pre * pdf)).astype(BF16)
    near = pl.ds(pl.multiple_of(mine * half, half), half)
    far = pl.ds(pl.multiple_of((1 - mine) * half, half), half)
    send_ref[...] = nt(pre_ref[...], up_ref[far, :]).astype(BF16)
    keep_ref[...] = nt(pre_ref[...], up_ref[near, :]).astype(BF16)
    osend_ref[...] = nn(act_ref[...], down_ref[:, far]).astype(BF16)
    okeep_ref[...] = nn(act_ref[...], down_ref[:, near]).astype(BF16)


def outer_kernel(pairs, *refs):
    out_ref = refs[-1]
    total = tn(refs[0][...], refs[1][...])
    for p in range(1, pairs):
        total = total + tn(refs[2 * p][...], refs[2 * p + 1][...])
    out_ref[...] = total.astype(BF16)


def outer(lefts, rights, tile):
    rows = lefts[0].shape[1]
    cols = rights[0].shape[1]
    tile = min(tile, rows)
    args, specs = [], []
    flops = 0
    for a, b in zip(lefts, rights):
        args += [a, b]
        specs += [
            pl.BlockSpec((a.shape[0], tile), lambda i: (0, i)),
            pl.BlockSpec(b.shape, lambda i: (0, 0)),
        ]
        flops += 2 * a.shape[0] * rows * cols
    return pl.pallas_call(
        functools.partial(outer_kernel, len(lefts)),
        grid=(rows // tile,),
        in_specs=specs,
        out_specs=pl.BlockSpec((tile, cols), lambda i: (i, 0)),
        out_shape=sds((rows, cols), BF16),
        compiler_params=params(24),
        cost_estimate=cost(flops, 2 * rows * cols + sum(a.size * 2 for a in args)),
    )(*args)


def project_grad_kernel(seqs, info_ref, *refs):
    lows = refs[:seqs]
    dqs, dks, dvs = refs[seqs : 2 * seqs], refs[2 * seqs : 3 * seqs], refs[3 * seqs : 4 * seqs]
    ctx_ref = refs[4 * seqs]
    dkcs, dvcs = refs[4 * seqs + 1 : 5 * seqs + 1], refs[5 * seqs + 1 : 6 * seqs + 1]
    gq_ref, gk_ref, gv_ref = refs[6 * seqs + 1 :]
    for out_ref, grads, sides in ((gq_ref, dqs, None), (gk_ref, dks, dkcs), (gv_ref, dvs, dvcs)):
        total = 0.0
        for s in range(seqs):
            total = total + tn(lows[s][...], grads[s][...])
            if sides is not None:
                total = total + tn(ctx_ref[0, s * CTX : (s + 1) * CTX, :], sides[s][...])
        out_ref[...] = total.astype(BF16)


def gather_parts(value, axis):
    parts = [value]
    for bit in reversed(low_bits(lax.axis_size(axis))):
        parts = parts + [None] * 0 + [swap(p, axis, bit) for p in parts]
    count = len(parts)
    order = [0]
    for bit in reversed(low_bits(count)):
        order = order + [k ^ bit for k in order]
    out = [None] * count
    for k, p in zip(order, parts):
        out[k] = p
    return out


def add_low(a, b):
    return (a.astype(F32) + b.astype(F32)).astype(BF16)


def scatter_parts(keep, send, axis):
    bits = low_bits(lax.axis_size(axis))
    got = swap(send, axis, 1)
    for bit in bits[1:]:
        now = add_low(keep, got)
        keep, send = now[0::2], now[1::2]
        got = swap(send, axis, bit)
    return keep[0], got[0]


def local(
    inputs, out_grad, lengths, norm_gain, query_weight, key_weight, value_weight, out_weight,
    mlp_gain, up_weight, down_weight, decay_rate, state_input, state_output, skip_gain,
):
    seqs, block, model = inputs.shape
    width = query_weight.shape[1]
    units = up_weight.shape[1]
    heads = width // HD
    stride = block // CTX
    scale = HD ** (-0.5)
    tensor_count = lax.axis_size("tensor")
    idx = lax.axis_index("tensor")
    place = lax.axis_index("seq")
    mine = idx & 1
    rows = seqs * block
    seg = rows // SUB
    half = model // 2
    seq_bits = low_bits(lax.axis_size("seq"))
    info = jnp.concatenate([jnp.stack([idx, mine]).astype(jnp.int32), (lengths - place * block).astype(jnp.int32)])

    flat_in = inputs.reshape(rows, model)
    chan_start = idx * width
    in_chan = lax.dynamic_slice_in_dim(flat_in, chan_start, width, 1)
    gain_chan = lax.dynamic_slice_in_dim(norm_gain, chan_start, width, 0)
    root = jnp.sqrt(-jnp.expm1(-2.0 * decay_rate))
    coeff = root * state_input
    skip_row = skip_gain.reshape(1, width)
    gain_row = gain_chan.reshape(1, width)
    tiles = width // HD
    tab = pltpu.VMEM((NS, SUB, width), F32)

    wo_parts = gather_parts(out_weight, "tensor")

    normed_low, hat, inverse, seg_end, final = pl.pallas_call(
        functools.partial(enter_kernel, seqs, stride),
        in_specs=[vmem()] * 4,
        out_specs=[vmem()] * 5,
        out_shape=[
            sds((rows, model), BF16),
            sds((tiles, rows, HD), F32),
            sds((rows, 1), F32),
            sds((NS, SUB, width), F32),
            sds((seqs, NS, width), F32),
        ],
        scratch_shapes=[tab, tab],
        compiler_params=params(16),
        cost_estimate=cost(rows * model * 8, rows * model * 5),
        name="enter",
    )(flat_in, in_chan, norm_gain.reshape(1, model), decay_rate)

    def hop(blocks):
        return jnp.exp(-decay_rate * (jnp.asarray(blocks, F32) * block))[None]

    carry_in = carried(final, hop, "seq", True)

    tile = 256
    query, key_self, value_self = pl.pallas_call(
        qkv_kernel,
        grid=(rows // tile,),
        in_specs=[pl.BlockSpec((tile, model), lambda i: (i, 0))]
        + [pl.BlockSpec((model, width), lambda i: (0, 0))] * 3,
        out_specs=[pl.BlockSpec((tile, width), lambda i: (i, 0))] * 3,
        out_shape=[sds((rows, width), BF16)] * 3,
        compiler_params=params(16),
        cost_estimate=cost(6 * rows * model * width, rows * model * 2 + 3 * model * width * 2),
        name="qkv",
    )(normed_low, query_weight, key_weight, value_weight)

    ctx_low, entry = pl.pallas_call(
        functools.partial(context_kernel, seqs, stride),
        in_specs=[vmem()] * 8,
        out_specs=[vmem()] * 2,
        out_shape=[sds((seqs * CTX, width), BF16), sds((NS, SUB, width), F32)],
        scratch_shapes=[tab, tab, tab, pltpu.VMEM((tiles, seqs * CTX, HD), F32)],
        compiler_params=params(16),
        cost_estimate=cost(rows * width * NS * 4, rows * width * 4),
        name="context",
    )(hat, seg_end, carry_in, decay_rate, coeff, state_output, skip_row, gain_row)
    ctx_parts = gather_parts(ctx_low, "tensor")

    def rows_of(s):
        return pl.BlockSpec((block, width), lambda i, s=s: (s, 0))

    def whole(shape):
        return pl.BlockSpec(shape, lambda i: (0,) * len(shape))

    attended, key_ctx, value_ctx, log_sum = [], [], [], []
    for s in range(seqs):
        a, kc, vc, ls = pl.pallas_call(
            functools.partial(attend_kernel, tensor_count, scale),
            grid=(1,),
            in_specs=[smem()]
            + [rows_of(s)] * 3
            + [whole((model, width))] * 2
            + [pl.BlockSpec((CTX, width), lambda i, s=s: (s, 0))] * tensor_count,
            out_specs=[whole((block, width)), whole((CTX, width)), whole((CTX, width)), whole((block, heads))],
            out_shape=[sds((block, width), BF16), sds((CTX, width), BF16), sds((CTX, width), BF16), sds((block, heads), F32)],
            compiler_params=params(24),
            cost_estimate=cost(4 * block * (block + CTX) * width + 4 * CTX * model * width, 4 * model * width + 8 * block * width, block * (block + CTX) * heads),
            name="attend",
        )(info, query, key_self, value_self, key_weight, value_weight, *ctx_parts)
        attended.append(a)
        key_ctx.append(kc)
        value_ctx.append(vc)
        log_sum.append(ls)

    flat_grad = out_grad.reshape(rows, model)
    gain2 = mlp_gain.reshape(1, model)
    att_parts = [gather_parts(a, "tensor") for a in attended]
    tile = 256
    steps = block // tile
    middle, normed2, act, pre_grad, cot, n2_near, n2_far, out_keep, out_send = ([] for _ in range(9))
    for s in range(seqs):

        def at(cols, s=s):
            return pl.BlockSpec((tile, cols), lambda i, s=s: (s * steps + i, 0))

        def own(cols):
            return pl.BlockSpec((tile, cols), lambda i: (i, 0))

        got = pl.pallas_call(
            functools.partial(feed_kernel, tensor_count, tile, s),
            grid=(steps,),
            in_specs=[smem(), at(model), at(model), whole((1, model)), whole((model, units)), whole((units, model))]
            + [own(width)] * tensor_count
            + [whole((width, model))] * tensor_count,
            out_specs=[own(model), own(model), own(units), own(units), own(model)] + [own(half)] * 4,
            out_shape=[sds((block, model), F32), sds((block, model), BF16), sds((block, units), BF16), sds((block, units), BF16), sds((block, model), BF16)]
            + [sds((block, half), BF16)] * 4,
            compiler_params=params(48),
            cost_estimate=cost(2 * block * model * (model + 4 * units), 3 * 2 * model * units + block * model * 16, block * units * 2),
            name="feed",
        )(info, flat_in, flat_grad, gain2, up_weight, down_weight, *att_parts[s], *wo_parts)
        middle.append(got[0])
        normed2.append(got[1])
        act.append(got[2])
        pre_grad.append(got[3])
        cot.append(got[4])
        near = add_low(got[5], swap(got[6], "tensor", 1))
        for bit in low_bits(tensor_count)[1:]:
            near = add_low(near, swap(near, "tensor", bit))
        n2_near.append(near)
        n2_far.append(swap(near, "tensor", 1))
        out_keep.append(got[7])
        out_send.append(got[8])

    down_grad = outer(act, cot, 256)
    up_grad = outer(normed2, pre_grad, 256)

    outputs = []
    for s in range(seqs):
        near = add_low(out_keep[s], swap(out_send[s], "tensor", 1))
        for bit in low_bits(tensor_count)[1:]:
            near = add_low(near, swap(near, "tensor", bit))
        mid_near = lax.dynamic_slice_in_dim(middle[s], mine * half, half, 1)
        near = (mid_near + near.astype(F32)).astype(BF16)
        far = swap(near, "tensor", 1)
        outputs.append(jnp.where(mine == 0, jnp.concatenate([near, far], 1), jnp.concatenate([far, near], 1)))
    outputs = jnp.stack(outputs)

    pairs = tensor_count // 2
    mid_low, mid_slice, gain2_part, dq, dk, dv, dkc, dvc, c_keep, c_send, n_keep, n_send = ([] for _ in range(12))
    for s in range(seqs):
        got = pl.pallas_call(
            functools.partial(attend_back_kernel, s, scale),
            grid=(1,),
            in_specs=[smem(), whole((block, model)), whole((block, half)), whole((block, half)), pl.BlockSpec((block, model), lambda i, s=s: (s, 0)), whole((1, model)), whole((width, model))]
            + [rows_of(s)] * 3
            + [whole((CTX, width))] * 2
            + [whole((block, heads))]
            + [whole((model, width))] * 3,
            out_specs=[whole((block, model)), whole((block, width)), whole((1, model))]
            + [whole((block, width))] * 3
            + [whole((CTX, width))] * 2
            + [whole((pairs, CTX, width))] * 2
            + [whole((pairs, block, width))] * 2,
            out_shape=[sds((block, model), BF16), sds((block, width), F32), sds((1, model), F32)]
            + [sds((block, width), BF16)] * 3
            + [sds((CTX, width), BF16)] * 2
            + [sds((pairs, CTX, width), BF16)] * 2
            + [sds((pairs, block, width), BF16)] * 2,
            scratch_shapes=[pltpu.VMEM((block, model), BF16), pltpu.VMEM((block, model), F32)]
            + [pltpu.VMEM((block, HD), F32)] * 2
            + [pltpu.VMEM((CTX, HD), F32)] * 2,
            compiler_params=params(32),
            cost_estimate=cost(10 * block * (block + CTX) * width + 8 * block * model * width, block * model * 12 + 8 * model * width, block * (block + CTX) * heads),
            name="attend_back",
        )(info, middle[s], n2_near[s], n2_far[s], flat_grad, gain2, out_weight, query, key_self, value_self, key_ctx[s], value_ctx[s], log_sum[s], query_weight, key_weight, value_weight)
        for slot, value in zip((mid_low, mid_slice, gain2_part, dq, dk, dv, dkc, dvc, c_keep, c_send, n_keep, n_send), got):
            slot.append(value)

    ctx_near, ctx_far = scatter_parts(jnp.concatenate(c_keep, 1), jnp.concatenate(c_send, 1), "tensor")
    n1_share = []
    for s in range(seqs):
        near, far = scatter_parts(n_keep[s], n_send[s], "tensor")
        n1_share.append(near.astype(F32) + far.astype(F32))

    ctx_grad, segb_end, lead = pl.pallas_call(
        functools.partial(lead_kernel, seqs, stride),
        in_specs=[vmem()] * 3,
        out_specs=[vmem()] * 3,
        out_shape=[sds((tiles, seqs * CTX, HD), F32), sds((NS, SUB, width), F32), sds((seqs, NS, width), F32)],
        scratch_shapes=[tab],
        compiler_params=params(16),
        cost_estimate=cost(seqs * CTX * width * NS * 2, seqs * CTX * width * 4),
        name="lead",
    )(ctx_near, ctx_far, decay_rate)
    carry_back = carried(lead, hop, "seq", False)

    out_weight_grad = outer(attended, mid_low, 256)
    ctx_stack = jnp.stack(ctx_parts)
    query_weight_grad, key_weight_grad, value_weight_grad = pl.pallas_call(
        functools.partial(project_grad_kernel, seqs),
        grid_spec=pltpu.PrefetchScalarGridSpec(
            num_scalar_prefetch=1,
            grid=(tensor_count,),
            in_specs=[pl.BlockSpec((block, width), lambda i, info, s=s: (s, i)) for s in range(seqs)]
            + [pl.BlockSpec((block, width), lambda i, info: (0, 0))] * (3 * seqs)
            + [pl.BlockSpec((1, seqs * CTX, width), lambda i, info: (i ^ info[0], 0, 0))]
            + [pl.BlockSpec((CTX, width), lambda i, info: (0, 0))] * (2 * seqs),
            out_specs=[pl.BlockSpec((width, width), lambda i, info: (i, 0))] * 3,
        ),
        out_shape=[sds((model, width), BF16)] * 3,
        compiler_params=params(24),
        cost_estimate=cost(6 * rows * model * width, rows * model * 2 + 6 * rows * width),
        name="project_grad",
    )(info, *([normed_low] * seqs), *dq, *dk, *dv, ctx_stack, *dkc, *dvc)

    chan_grad, rate_grad, sin_grad, sout_grad, skip_grad = pl.pallas_call(
        functools.partial(state_back_kernel, seqs, stride),
        in_specs=[vmem()] * 11,
        out_specs=[vmem()] * 5,
        out_shape=[sds((tiles, rows, HD), F32)] + [sds((NS, width), F32)] * 3 + [sds((1, width), F32)],
        scratch_shapes=[tab, tab, pltpu.VMEM((stride, NS, SUB, width), F32), tab, pltpu.VMEM((seg // stride + 1, NS, SUB, width), F32), pltpu.VMEM((stride + 2, NS, width), F32)],
        compiler_params=params(24),
        cost_estimate=cost(rows * width * NS * 12, rows * width * 12),
        name="state_back",
    )(hat, ctx_grad, entry, segb_end, carry_back, decay_rate, root, state_input, state_output, skip_row, gain_row)

    n1_grad = jnp.concatenate(n1_share, 0) + jnp.concatenate([chan_grad[t] for t in range(tiles)], 1)
    hat_chan = in_chan.astype(F32) * inverse
    norm_gain_grad = jnp.sum(n1_grad * hat_chan, 0)
    h1 = n1_grad * gain_chan
    total = jnp.sum(h1 * hat_chan, -1).reshape(rows // 128, 128)
    for bit in low_bits(tensor_count):
        total = total + swap(total, "tensor", bit)
    mid_chan = jnp.concatenate(mid_slice, 0)
    input_grad = mid_chan + inverse * (h1 - hat_chan * (total.reshape(rows, 1) / model))
    input_grad = input_grad.astype(BF16).reshape(seqs, block, width)

    mlp_gain_grad = sum(gain2_part)
    small = jnp.concatenate([rate_grad, sin_grad, sout_grad, skip_grad, norm_gain_grad.reshape(1, width), mlp_gain_grad.reshape(model // width, width)], 0)
    for bit in seq_bits:
        small = small + swap(small, "seq", bit)

    big = lax.psum((down_grad, up_grad), "seq")
    rest = lax.psum((query_weight_grad, key_weight_grad, value_weight_grad, out_weight_grad), "seq")
    return (
        outputs,
        input_grad,
        small[3 * NS + 1],
        rest[0].astype(F32),
        rest[1].astype(F32),
        rest[2].astype(F32),
        rest[3].astype(F32),
        small[3 * NS + 2 :].reshape(model),
        big[1].astype(F32),
        big[0].astype(F32),
        small[:NS],
        small[NS : 2 * NS],
        small[2 * NS : 3 * NS],
        small[3 * NS],
    )


def solution(mesh):
    in_specs = (
        P(None, "seq", None),
        P(None, "seq", None),
        P(),
        P(),
        P(None, "tensor"),
        P(None, "tensor"),
        P(None, "tensor"),
        P("tensor", None),
        P(),
        P(None, "tensor"),
        P("tensor", None),
        P(None, "tensor"),
        P(None, "tensor"),
        P(None, "tensor"),
        P("tensor"),
    )
    out_specs = (
        P(None, "seq", None),
        P(None, "seq", "tensor"),
        P("tensor"),
        P(None, "tensor"),
        P(None, "tensor"),
        P(None, "tensor"),
        P("tensor", None),
        P(),
        P(None, "tensor"),
        P("tensor", None),
        P(None, "tensor"),
        P(None, "tensor"),
        P(None, "tensor"),
        P("tensor"),
    )
    return jax.shard_map(local, mesh=mesh, in_specs=in_specs, out_specs=out_specs, check_vma=False)
```

```python
import functools

import jax
import jax.numpy as jnp
from jax import lax
from jax.experimental import pallas as pl
from jax.experimental.pallas import tpu as pltpu
from jax.sharding import PartitionSpec as P

HD = 128
NS = 16
CTX = 128
SUB = 8
EPS = 1e-06
F32 = jnp.float32
BF16 = jnp.bfloat16
MIB = 1 << 20


def nn(a, b):
    return lax.dot_general(a, b, (((1,), (0,)), ((), ())), preferred_element_type=F32)


def nt(a, b):
    return lax.dot_general(a, b, (((1,), (1,)), ((), ())), preferred_element_type=F32)


def tn(a, b):
    return lax.dot_general(a, b, (((0,), (0,)), ((), ())), preferred_element_type=F32)


def swap(value, axis, bit):
    count = lax.axis_size(axis)
    return lax.ppermute(value, axis, [(i, i ^ bit) for i in range(count)])


def low_bits(count):
    bit, out = 1, []
    while bit < count:
        out.append(bit)
        bit *= 2
    return out


def sds(shape, dtype):
    return jax.ShapeDtypeStruct(shape, dtype)


def vmem():
    return pl.BlockSpec(memory_space=pltpu.VMEM)


def smem():
    return pl.BlockSpec(memory_space=pltpu.SMEM)


class Line:
    def __init__(self):
        self.last = None
        self.held = []

    def run(self, name, kernel, args, in_specs, outs, grid=None, prefetch=(), scratch=(), limit=24, chain=True, after=None):
        args, in_specs = list(args), list(in_specs)
        extra = [t for t in (self.last if chain else None, after, *self.held) if t is not None]
        self.held = []
        count = len(prefetch) + len(args)
        body = kernel
        if extra:

            def body(*refs):
                return kernel(*refs[:count], *refs[count + len(extra) :])

            args += extra
            in_specs += [pl.BlockSpec(memory_space=pl.ANY)] * len(extra)
        got = pl.pallas_call(
            body,
            grid_spec=pltpu.PrefetchScalarGridSpec(
                num_scalar_prefetch=len(prefetch),
                grid=grid or (1,),
                in_specs=in_specs,
                out_specs=[o[2] for o in outs],
                scratch_shapes=list(scratch),
            ),
            out_shape=[sds(o[0], o[1]) for o in outs],
            compiler_params=pltpu.CompilerParams(vmem_limit_bytes=limit * MIB),
            cost_estimate=pl.CostEstimate(flops=1, bytes_accessed=1, transcendentals=0),
            name=name,
        )(*prefetch, *args)
        if chain:
            self.last = min(got, key=lambda g: g.size)
        return got


def full(shape):
    return pl.BlockSpec(shape, lambda *a: (0,) * len(shape))


def out_full(shape, dtype):
    return (shape, dtype, full(shape))


def lanes(tile):
    return slice(tile * HD, (tile + 1) * HD)


def spread(table, rows, factor=None):
    for n in range(NS):
        row = rows[n : n + 1, :]
        if factor is not None:
            row = jnp.exp(row * factor)
        table[n] = jnp.broadcast_to(row, table.shape[1:])


def scan_step(taps, decay_tab, jump_tab, state):
    tiles = len(taps)
    out = []
    for n in range(NS):
        for t in range(tiles):
            decay = decay_tab[n, :, lanes(t)]
            inner = taps[t][0]
            for tap in taps[t][1:]:
                inner = inner * decay + tap
            out.append(state[n * tiles + t] * jump_tab[n, :, lanes(t)] + inner)
    return tuple(out)


def taps_of(runs_ref, group, stride):
    return [[runs_ref[t, group * stride + i] for i in range(stride)] for t in range(runs_ref.shape[0])]


def segment_ends(state, rate, seg, seqs, seg_ref, end_ref, forward):
    per = SUB // seqs
    tiles = rate.shape[1] // HD
    place = lax.rem(lax.broadcasted_iota(jnp.int32, (SUB, HD), 0), per)
    away = ((per - 1 - place if forward else place) * seg).astype(F32)
    for n in range(NS):
        for t in range(tiles):
            now = state[n * tiles + t]
            seg_ref[n, :, lanes(t)] = now
            part = now * jnp.exp(-rate[n : n + 1, lanes(t)] * away)
            for s in range(seqs):
                end_ref[s, n : n + 1, lanes(t)] = jnp.sum(part[s * per : (s + 1) * per], 0, keepdims=True)


def entry_states(entry_ref, carry_ref, seg_ref, hop, seqs, forward):
    per = SUB // seqs
    for n in range(NS):
        step = hop[n : n + 1, :]
        for s in range(seqs):
            now = carry_ref[s, n : n + 1, :]
            for k in range(per):
                q = s * per + (k if forward else per - 1 - k)
                entry_ref[n, q : q + 1, :] = now
                if k < per - 1:
                    now = now * step + seg_ref[n, q : q + 1, :]


def read_state(ref):
    tiles = ref.shape[2] // HD
    return tuple(ref[n, :, lanes(t)] for n in range(NS) for t in range(tiles))


def enter_kernel(seqs, stride, info_ref, x_ref, xc_ref, gain_ref, rate_ref, low_ref, inv_ref, runs_ref, seg_ref, fin_ref, flat, decay_tab, jump_tab):
    step, width = x_ref.shape
    tiles, seg = runs_ref.shape[:2]
    piece = 64
    gain = gain_ref[...]
    rate = rate_ref[...]

    @pl.when(pl.program_id(0) == 0)
    def _():
        spread(decay_tab, rate, -1.0)
        spread(jump_tab, rate, -float(stride))

    def norm(i, carry):
        at = pl.ds(pl.multiple_of(i * piece, piece), piece)
        x = x_ref[at, :].astype(F32)
        inv = lax.rsqrt(jnp.sum(x * x, -1, keepdims=True) * (1.0 / width) + EPS)
        low_ref[at, :] = (x * inv * gain).astype(BF16)
        inv_ref[at, :] = inv
        to = pl.ds(pl.multiple_of(pl.program_id(0) * step + i * piece, piece), piece)
        for t in range(tiles):
            flat[t, to, :] = xc_ref[at, lanes(t)].astype(F32) * inv
        return carry

    lax.fori_loop(0, step // piece, norm, 0)

    @pl.when(pl.program_id(0) == pl.num_programs(0) - 1)
    def _():
        def group(g, state):
            taps = []
            for t in range(tiles):
                row = [flat[t, pl.ds(g * stride + i, SUB, stride=seg), :] for i in range(stride)]
                for i in range(stride):
                    runs_ref[t, g * stride + i] = row[i]
                taps.append(row)
            return scan_step(taps, decay_tab, jump_tab, state)

        state = lax.fori_loop(0, seg // stride, group, (jnp.zeros((SUB, HD), F32),) * (NS * tiles))
        segment_ends(state, rate, seg, seqs, seg_ref, fin_ref, True)


def context_kernel(seqs, stride, runs_ref, seg_ref, carry_ref, rate_ref, coeff_ref, sout_ref, skip_ref, gain_ref, ctx_ref, entry_ref, decay_tab, jump_tab, out_tab, flat):
    tiles, seg = runs_ref.shape[:2]
    rate = rate_ref[...]
    spread(decay_tab, rate, -1.0)
    spread(jump_tab, rate, -float(stride))
    spread(out_tab, coeff_ref[...] * sout_ref[...] * gain_ref[...])
    entry_states(entry_ref, carry_ref, seg_ref, jnp.exp(rate * (-float(seg))), seqs, True)
    skip = skip_ref[...] * gain_ref[...]
    groups = seg // stride

    def group(g, state):
        taps = taps_of(runs_ref, g, stride)
        state = scan_step(taps, decay_tab, jump_tab, state)
        for t in range(tiles):
            total = skip[:, lanes(t)] * taps[t][-1]
            for n in range(NS):
                total = total + out_tab[n, :, lanes(t)] * state[n * tiles + t]
            flat[t, pl.ds(g, SUB, stride=groups), :] = total
        return state

    lax.fori_loop(0, groups, group, read_state(entry_ref))
    for t in range(tiles):
        ctx_ref[:, lanes(t)] = flat[t].astype(BF16)


def lead_kernel(seqs, stride, near_ref, far_ref, rate_ref, grads_ref, segb_ref, lead_ref, flat, jump_tab):
    tiles, groups = grads_ref.shape[:2]
    for t in range(tiles):
        flat[t] = near_ref[:, lanes(t)].astype(F32) + far_ref[:, lanes(t)].astype(F32)
    rate = rate_ref[...]
    spread(jump_tab, rate, -float(stride))

    def group(i, state):
        g = groups - 1 - i
        grads = [flat[t, pl.ds(g, SUB, stride=groups), :] for t in range(tiles)]
        for t in range(tiles):
            grads_ref[t, g] = grads[t]
        return tuple(state[n * tiles + t] * jump_tab[n, :, lanes(t)] + grads[t] for n in range(NS) for t in range(tiles))

    state = lax.fori_loop(0, groups, group, (jnp.zeros((SUB, HD), F32),) * (NS * tiles))
    segment_ends(state, rate, groups * stride, seqs, segb_ref, lead_ref, False)


def state_back_kernel(
    seqs, stride, runs_ref, grads_ref, entry_ref, segb_ref, carryb_ref, rate_ref, root_ref, sin_ref, sout_ref, skip_ref, gain_ref,
    back_ref, rateg_ref, sing_ref, soutg_ref, skipg_ref,
    decay_tab, jump_tab, tap_tab, entryb, states, backs, sums,
):
    tiles, seg = runs_ref.shape[:2]
    groups = seg // stride
    rate = rate_ref[...]
    root = root_ref[...]
    s_in = sin_ref[...]
    s_out = sout_ref[...]
    gain = gain_ref[...]
    coeff = root * s_in
    spread(decay_tab, rate, -1.0)
    spread(jump_tab, rate, -float(stride))
    both = coeff * s_out
    for i in range(stride):
        spread(tap_tab.at[i], both * jnp.exp(rate * (-float(stride - 1 - i))))
    entry_states(entryb, carryb_ref, segb_ref, jnp.exp(rate * (-float(seg))), seqs, False)
    skip = skip_ref[...]
    zero = jnp.zeros((SUB, HD), F32)

    def forward(g, carry):
        state, totals = carry
        for n in range(NS):
            for t in range(tiles):
                states[g, n, :, lanes(t)] = state[n * tiles + t]
        taps = taps_of(runs_ref, g, stride)
        out = []
        for t in range(tiles):
            grad = grads_ref[t, g]
            out.append(totals[t] + grad * taps[t][-1])
            backs[t, g * stride + stride - 1] = grad * skip[:, lanes(t)]
            for i in range(stride - 1):
                backs[t, g * stride + i] = zero
        return scan_step(taps, decay_tab, jump_tab, state), tuple(out)

    last, totals = lax.fori_loop(0, groups, forward, (read_state(entry_ref), (zero,) * tiles))
    for n in range(NS):
        for t in range(tiles):
            states[groups, n, :, lanes(t)] = last[n * tiles + t]
    for t in range(tiles):
        skipg_ref[:, lanes(t)] = jnp.sum(totals[t], 0, keepdims=True) * gain[:, lanes(t)]
    lot = 4
    kinds = stride + 2
    for t in range(tiles):
        for first in range(0, NS, lot):
            names = range(first, first + lot)

            def group(i, carry, t=t, names=names):
                g = groups - 1 - i
                adj, acc = carry
                grad = grads_ref[t, g]
                taps = [runs_ref[t, g * stride + i] for i in range(stride)]
                sums_b = [backs[t, g * stride + i] for i in range(stride)]
                new_adj, new_acc = [], []
                for k, n in enumerate(names):
                    now = adj[k] * jump_tab[n, :, lanes(t)] + grad
                    new_adj.append(now)
                    for i in range(stride):
                        sums_b[i] = sums_b[i] + tap_tab[i, n, :, lanes(t)] * now
                        new_acc.append(acc[k * kinds + i] + now * taps[i])
                    new_acc.append(acc[k * kinds + stride] + now * states[g, n, :, lanes(t)])
                    new_acc.append(acc[k * kinds + stride + 1] + grad * states[g + 1, n, :, lanes(t)])
                for i in range(stride):
                    backs[t, g * stride + i] = sums_b[i]
                return tuple(new_adj), tuple(new_acc)

            start = (tuple(entryb[n, :, lanes(t)] for n in names), (zero,) * (lot * kinds))
            _, acc = lax.fori_loop(0, groups, group, start)
            for k, n in enumerate(names):
                for j in range(kinds):
                    sums[j, n : n + 1, lanes(t)] = jnp.sum(acc[k * kinds + j], 0, keepdims=True)

    def spill(g, carry):
        for t in range(tiles):
            for i in range(stride):
                back_ref[t, pl.ds(g * stride + i, SUB, stride=seg), :] = backs[t, g * stride + i]
        return carry

    lax.fori_loop(0, groups, spill, 0)
    decay = jnp.exp(-rate)
    powers = [jnp.ones_like(rate)]
    for _ in range(stride):
        powers.append(powers[-1] * decay)
    coeff_grad = sum(powers[stride - 1 - i] * sums[i] for i in range(stride)) * s_out * gain
    decay_grad = float(stride) * powers[stride - 1] * sums[stride]
    for i in range(stride - 1):
        decay_grad = decay_grad + float(stride - 1 - i) * powers[stride - 2 - i] * sums[i]
    decay_grad = decay_grad * coeff * s_out * gain
    soutg_ref[...] = coeff * gain * sums[stride + 1]
    sing_ref[...] = coeff_grad * root
    rateg_ref[...] = coeff_grad * s_in * (decay * decay / root) - decay * decay_grad


def carried(value, hop, axis, forward):
    count = lax.axis_size(axis)
    mine = lax.axis_index(axis)
    whole = value
    enter = jnp.zeros_like(value)
    for bit in low_bits(count):
        other = swap(whole, axis, bit)
        upper = (mine & bit) != 0
        offset = mine & (bit - 1)
        if not forward:
            upper = jnp.logical_not(upper)
            offset = bit - 1 - offset
        enter = jnp.where(upper, enter + hop(offset) * other, enter)
        span = hop(bit)
        whole = jnp.where(upper, whole + span * other, other + span * whole)
    return enter


def qkv_kernel(x_ref, wq_ref, wk_ref, wv_ref, q_ref, k_ref, v_ref):
    x = x_ref[...]
    q_ref[...] = nn(x, wq_ref[...]).astype(BF16)
    k_ref[...] = nn(x, wk_ref[...]).astype(BF16)
    v_ref[...] = nn(x, wv_ref[...]).astype(BF16)


def masks(first, tile, block, stride):
    row = lax.broadcasted_iota(jnp.int32, (tile, CTX), 0) + first
    col = lax.broadcasted_iota(jnp.int32, (tile, CTX), 1)
    side = stride * col + (stride - 1) <= row
    row = lax.broadcasted_iota(jnp.int32, (tile, block), 0) + first
    col = lax.broadcasted_iota(jnp.int32, (tile, block), 1)
    return side, col <= row


def attend_kernel(parts, scale, idx_ref, q_ref, k_ref, v_ref, wk_ref, wv_ref, *rest):
    ctx_refs, (out_ref, kc_ref, vc_ref, lse_ref) = rest[:parts], rest[parts:]
    block, width = q_ref.shape
    stride = block // CTX
    idx = idx_ref[2]
    key_c = jnp.zeros((CTX, width), F32)
    val_c = jnp.zeros((CTX, width), F32)
    for p in range(parts):
        at = pl.ds(pl.multiple_of((idx ^ p) * width, width), width)
        key_c = key_c + nn(ctx_refs[p][...], wk_ref[at, :])
        val_c = val_c + nn(ctx_refs[p][...], wv_ref[at, :])
    kc_ref[...] = key_c.astype(BF16)
    vc_ref[...] = val_c.astype(BF16)
    tile = min(256, block)
    for h in range(width // HD):
        cols = slice(h * HD, (h + 1) * HD)
        for first in range(0, block, tile):
            seen = first + tile
            rows = slice(first, seen)
            q = q_ref[rows, cols]
            side_ok, own_ok = masks(first, tile, seen, stride)
            side = jnp.where(side_ok, nt(q, kc_ref[:, cols]), -1e30)
            own = jnp.where(own_ok, nt(q, k_ref[:seen, cols]), -1e30)
            top = jnp.maximum(jnp.max(side, -1, keepdims=True), jnp.max(own, -1, keepdims=True))
            side = jnp.exp((side - top) * scale)
            own = jnp.exp((own - top) * scale)
            total = jnp.sum(side, -1, keepdims=True) + jnp.sum(own, -1, keepdims=True)
            share = 1.0 / total
            got = nn((side * share).astype(BF16), vc_ref[:, cols]) + nn((own * share).astype(BF16), v_ref[:seen, cols])
            out_ref[rows, cols] = got.astype(BF16)
            lse_ref[rows, h : h + 1] = top * scale + jnp.log(total)


def attend_back_kernel(
    seq, scale, info_ref, mid_ref, near_ref, far_ref, grad_ref, gain_ref, wo_ref, q_ref, k_ref, v_ref, kc_ref, vc_ref, lse_ref,
    wq_ref, wk_ref, wv_ref,
    low_ref, slice_ref, gaing_ref, dq_ref, dk_ref, dv_ref, dkc_ref, dvc_ref, ckeep_ref, csend_ref, nkeep_ref, nsend_ref,
    n2_ref, full_ref, key_acc, val_acc, skey_acc, sval_acc,
):
    block, width = q_ref.shape
    model = mid_ref.shape[1]
    half = model // 2
    stride = block // CTX
    idx, mine, limit = info_ref[2], info_ref[3], info_ref[4 + seq]
    n2_ref[:, pl.ds(pl.multiple_of(mine * half, half), half)] = near_ref[...]
    n2_ref[:, pl.ds(pl.multiple_of((1 - mine) * half, half), half)] = far_ref[...]
    gain = gain_ref[...]
    step = 64

    def norm(i, total):
        at = pl.ds(pl.multiple_of(i * step, step), step)
        mid = mid_ref[at, :]
        inv = lax.rsqrt(jnp.sum(mid * mid, -1, keepdims=True) * (1.0 / model) + EPS)
        hat = mid * inv
        n2 = n2_ref[at, :].astype(F32)
        prod = n2 * hat
        h2 = n2 * gain
        mean = jnp.sum(h2 * hat, -1, keepdims=True) * (1.0 / model)
        place = lax.broadcasted_iota(jnp.int32, (step, 1), 0) + i * step
        cot = jnp.where(place < limit, grad_ref[at, :].astype(F32), 0.0)
        grad = cot + inv * (h2 - hat * mean)
        full_ref[at, :] = grad
        low_ref[at, :] = grad.astype(BF16)
        return total + jnp.sum(prod, 0, keepdims=True)

    gaing_ref[...] = lax.fori_loop(0, block // step, norm, jnp.zeros((1, model), F32))
    slice_ref[...] = full_ref[:, pl.ds(pl.multiple_of(idx * width, width), width)]
    att_grad = nt(low_ref[...], wo_ref[...]).astype(BF16)
    tile = min(256, block)
    for h in range(width // HD):
        cols = slice(h * HD, (h + 1) * HD)
        for first in range(0, block, tile):
            seen = first + tile
            rows = slice(first, seen)
            q = q_ref[rows, cols]
            grad = att_grad[rows, cols]
            lse = lse_ref[rows, h : h + 1]
            side_ok, own_ok = masks(first, tile, seen, stride)
            kc, k = kc_ref[:, cols], k_ref[:seen, cols]
            side = jnp.exp(jnp.where(side_ok, nt(q, kc) * scale - lse, -1e30))
            own = jnp.exp(jnp.where(own_ok, nt(q, k) * scale - lse, -1e30))
            dside = nt(grad, vc_ref[:, cols])
            down = nt(grad, v_ref[:seen, cols])
            term = jnp.sum(side * dside, -1, keepdims=True) + jnp.sum(own * down, -1, keepdims=True)
            dside = (side * (dside - term)).astype(BF16)
            down = (own * (down - term)).astype(BF16)
            dq_ref[rows, cols] = ((nn(dside, kc) + nn(down, k)) * scale).astype(BF16)
            side = side.astype(BF16)
            own = own.astype(BF16)
            last = first + tile >= block
            fresh = first == 0
            for acc, score, right in (
                (skey_acc, dside, q),
                (sval_acc, side, grad),
            ):
                got = tn(score, right)
                acc[...] = got if fresh else acc[...] + got
            for acc, score, right in (
                (key_acc, down, q),
                (val_acc, own, grad),
            ):
                got = tn(score, right)
                if fresh:
                    acc[:seen, :] = got
                else:
                    acc[:first, :] = acc[:first, :] + got[:first]
                    acc[first:seen, :] = got[first:]
            if last:
                dk_ref[:, cols] = (key_acc[...] * scale).astype(BF16)
                dv_ref[:, cols] = val_acc[...].astype(BF16)
                dkc_ref[:, cols] = (skey_acc[...] * scale).astype(BF16)
                dvc_ref[:, cols] = sval_acc[...].astype(BF16)
    count = model // width
    for p in range(count):
        at = pl.ds(pl.multiple_of((idx ^ p) * width, width), width)
        wk, wv = wk_ref[at, :], wv_ref[at, :]
        ctx = nt(dkc_ref[...], wk) + nt(dvc_ref[...], wv)
        (csend_ref if p % 2 else ckeep_ref)[p // 2] = ctx.astype(BF16)
    for p in range(count):
        at = pl.ds(pl.multiple_of((idx ^ p) * width, width), width)
        own = nt(dq_ref[...], wq_ref[at, :]) + nt(dk_ref[...], wk_ref[at, :]) + nt(dv_ref[...], wv_ref[at, :])
        (nsend_ref if p % 2 else nkeep_ref)[p // 2] = own.astype(BF16)


def feed_kernel(parts, tile, seq, info_ref, x_ref, grad_ref, gain_ref, up_ref, *rest):
    att_refs, wo_refs = rest[:parts], rest[parts : 2 * parts]
    mid_ref, n2_ref, act_ref, slope_ref, cot_ref = rest[2 * parts :]
    model = x_ref.shape[1]
    limit = info_ref[4 + seq]
    mid = x_ref[...].astype(F32)
    got = nn(att_refs[0][...], wo_refs[0][...])
    for p in range(1, parts):
        got = got + nn(att_refs[p][...], wo_refs[p][...])
    mid = mid + got
    mid_ref[...] = mid
    inv = lax.rsqrt(jnp.sum(mid * mid, -1, keepdims=True) * (1.0 / model) + EPS)
    n2_ref[...] = (mid * inv * gain_ref[...]).astype(BF16)
    place = lax.broadcasted_iota(jnp.int32, (tile, 1), 0) + pl.program_id(0) * tile
    cot_ref[...] = jnp.where(place < limit, grad_ref[...].astype(F32), 0.0).astype(BF16)
    pre = nn(n2_ref[...], up_ref[...])
    cdf = 0.5 * (1.0 + lax.erf(pre * 0.7071067811865476))
    pdf = jnp.exp(pre * pre * -0.5) * 0.3989422804014327
    act_ref[...] = (pre * cdf).astype(BF16)
    slope_ref[...] = (cdf + pre * pdf).astype(BF16)


def halves(info_ref, half):
    mine = info_ref[3]
    return (
        pl.ds(pl.multiple_of(mine * half, half), half),
        pl.ds(pl.multiple_of((1 - mine) * half, half), half),
    )


def feed_back_kernel(info_ref, cot_ref, slope_ref, up_ref, down_ref, pre_ref, keep_ref, send_ref):
    near, far = halves(info_ref, keep_ref.shape[1])
    pull = nt(cot_ref[...], down_ref[...])
    pre_ref[...] = (pull * slope_ref[...].astype(F32)).astype(BF16)
    send_ref[...] = nt(pre_ref[...], up_ref[far, :]).astype(BF16)
    keep_ref[...] = nt(pre_ref[...], up_ref[near, :]).astype(BF16)


def feed_out_kernel(info_ref, act_ref, down_ref, keep_ref, send_ref):
    near, far = halves(info_ref, keep_ref.shape[1])
    send_ref[...] = nn(act_ref[...], down_ref[:, far]).astype(BF16)
    keep_ref[...] = nn(act_ref[...], down_ref[:, near]).astype(BF16)


def add_kernel(a_ref, b_ref, out_ref):
    out_ref[...] = (a_ref[...].astype(F32) + b_ref[...].astype(F32)).astype(BF16)


def add_pair_kernel(a_ref, b_ref, out0_ref, out1_ref):
    out0_ref[...] = (a_ref[0].astype(F32) + b_ref[0].astype(F32)).astype(BF16)
    out1_ref[...] = (a_ref[1].astype(F32) + b_ref[1].astype(F32)).astype(BF16)


def add_parts_kernel(pairs, count, *refs):
    keeps, gots, outs = refs[:count], refs[count : 2 * count], refs[2 * count :]
    block = keeps[0].shape[1]
    for m in range(pairs):
        for s in range(count):
            outs[m][s * block : (s + 1) * block, :] = (keeps[s][m].astype(F32) + gots[s][m].astype(F32)).astype(BF16)


def add_out_kernel(info_ref, mid_ref, a_ref, b_ref, out_ref):
    near, _ = halves(info_ref, out_ref.shape[1])
    total = a_ref[...].astype(F32) + b_ref[...].astype(F32)
    out_ref[...] = (mid_ref[:, near] + total).astype(BF16)


def join_kernel(seqs, info_ref, *refs):
    out_ref = refs[-1]
    block, half = refs[0].shape
    near, far = halves(info_ref, half)
    for s in range(seqs):
        out_ref[s, :, near] = refs[s][...]
        out_ref[s, :, far] = refs[seqs + s][...]


def add_pair(line, a, b):
    return line.run("add_pair", add_pair_kernel, (a, b), [full(a.shape)] * 2, [out_full(a.shape[1:], BF16)] * 2, limit=8)


def add_parts(line, keeps, gots):
    pairs, block, width = keeps[0].shape
    count = len(keeps)
    return line.run(
        "add_parts",
        functools.partial(add_parts_kernel, pairs, count),
        (*keeps, *gots),
        [full((pairs, block, width))] * (2 * count),
        [out_full((count * block, width), BF16)] * pairs,
        limit=8,
    )


def add(line, a, b):
    return line.run("add", add_kernel, (a, b), [full(a.shape)] * 2, [out_full(a.shape, BF16)], limit=8)[0]


def quarter(info, far, step):
    return (info[0] ^ far) * 2 + (info[1] ^ step)


PIECES = ((0, 0), (0, 1), (1, 0), (1, 1))


def outer_kernel(pairs, info_ref, *refs):
    piece = refs[0].shape[1] // 4
    for far, step in PIECES:
        out_ref = refs[2 * pairs + far].at[step]
        at = pl.ds(pl.multiple_of(quarter(info_ref, far, step) * piece, piece), piece)
        total = tn(refs[0][:, at], refs[pairs][...])
        for p in range(1, pairs):
            total = total + tn(refs[p][:, at], refs[pairs + p][...])
        out_ref[...] = total.astype(BF16)


def outer(line, info, lefts, rights):
    rows, cols = lefts[0].shape[1], rights[0].shape[1]
    return line.run(
        "outer",
        functools.partial(outer_kernel, len(lefts)),
        [*lefts, *rights],
        [full(a.shape) for a in (*lefts, *rights)],
        [out_full((2, rows // 4, cols), BF16)] * 2,
        prefetch=(info,),
    )


def project_grad_kernel(seqs, info_ref, *refs):
    refs = list(refs)

    def take(count):
        got = refs[:count]
        del refs[:count]
        return got

    (low_ref,) = take(1)
    mids = take(seqs)
    (ctx_ref,) = take(1)
    dqs, dks, dvs, dkcs, dvcs, atts = (take(seqs) for _ in range(6))
    block, width = dqs[0].shape
    quart = low_ref.shape[1] // 4 // width
    for far, step in PIECES:
        out_ref = refs[far].at[step]
        for i in range(quart):
            part = quarter(info_ref, far, step) * quart + i
            at = pl.ds(pl.multiple_of(part * width, width), width)
            rows = slice(i * width, (i + 1) * width)
            for k, (grads, more) in enumerate(((dqs, None), (dks, dkcs), (dvs, dvcs))):
                total = 0.0
                for s in range(seqs):
                    total = total + tn(low_ref[s * block : (s + 1) * block, at], grads[s][...])
                    if more is not None:
                        total = total + tn(ctx_ref[part ^ info_ref[2], s * CTX : (s + 1) * CTX, :], more[s][...])
                out_ref[rows, k * width : (k + 1) * width] = total.astype(BF16)
            total = 0.0
            for s in range(seqs):
                total = total + tn(atts[s][...], mids[s][:, at])
            out_ref[rows, 3 * width :] = total.astype(BF16)


def widen_kernel(flags_ref, *refs):
    for p in range(4):

        @pl.when(pl.program_id(0) == p)
        def _(p=p):
            refs[4][...] = refs[p][...].astype(F32)


def order(p, f):
    return quarter(f, p // 2, p % 2)


def widen(line, info, pieces, after=None):
    piece, cols = pieces[0].shape
    return line.run(
        "widen",
        widen_kernel,
        pieces,
        [full((piece, cols))] * 4,
        [((4 * piece, cols), F32, pl.BlockSpec((piece, cols), lambda p, f: (order(p, f), 0)))],
        grid=(4,),
        prefetch=(info,),
        after=after,
    )[0]


def widen_project_kernel(flags_ref, *refs):
    width = refs[0].shape[1] // 4
    for p in range(4):

        @pl.when(pl.program_id(0) == p)
        def _(p=p):
            for k in range(3):
                refs[4 + k][...] = refs[p][:, k * width : (k + 1) * width].astype(F32)
            for j in range(refs[0].shape[0] // width):
                refs[7][:, j * width : (j + 1) * width] = refs[p][j * width : (j + 1) * width, 3 * width :].astype(F32)


def widen_project(line, info, pieces):
    piece, cols = pieces[0].shape
    width = cols // 4
    return line.run(
        "widen_project",
        widen_project_kernel,
        pieces,
        [full((piece, cols))] * 4,
        [((4 * piece, width), F32, pl.BlockSpec((piece, width), lambda p, f: (order(p, f), 0)))] * 3
        + [((width, 4 * piece), F32, pl.BlockSpec((width, piece), lambda p, f: (0, order(p, f))))],
        grid=(4,),
        prefetch=(info,),
    )


def gather_parts(value, axis):
    parts = [value]
    for bit in reversed(low_bits(lax.axis_size(axis))):
        parts = parts + [None] * 0 + [swap(p, axis, bit) for p in parts]
    count = len(parts)
    order = [0]
    for bit in reversed(low_bits(count)):
        order = order + [k ^ bit for k in order]
    out = [None] * count
    for k, p in zip(order, parts):
        out[k] = p
    return out


def add_low(a, b):
    return (a.astype(F32) + b.astype(F32)).astype(BF16)


def scatter_parts(parts, axis):
    bits = low_bits(lax.axis_size(axis))[1:]
    for bit in bits:
        keep, send = parts[0::2], parts[1::2]
        got = [swap(p, axis, bit) for p in send]
        if bit != bits[-1]:
            parts = [add_low(a, b) for a, b in zip(keep, got)]
    return keep[0], got[0]


KINDS = {"D": 0, "U": 0, "Q": 0}
ORDER = (
    ("outD", 0), ("fb", 0), ("fb", 1), ("na", 0), ("outU", 0), ("na", 1), ("ny", 0), ("s2", "D"), ("ny", 1),
    ("ab", 0), ("s3", "D"), ("ab", 1), ("s2", "U"), ("pr", 0), ("np", 0), ("cp", 0), ("fo", 1), ("fo", 0), ("ld", 0),
    ("s4", "D"), ("s3", "U"), ("oc", 1), ("s2", "Q"), ("s4", "U"), ("p1", "D"), ("st", 0), ("p2", "U"), ("oc", 0),
    ("s3", "Q"), ("wd", "D"), ("s4", "Q"), ("oa", 0), ("p2", "Q"), ("oa", 1), ("wd", "U"), ("jn", 0), ("wd", "Q"),
)


def local(
    inputs, out_grad, lengths, norm_gain, query_weight, key_weight, value_weight, out_weight,
    mlp_gain, up_weight, down_weight, decay_rate, state_input, state_output, skip_gain,
):
    seqs, block, model = inputs.shape
    width = query_weight.shape[1]
    units = up_weight.shape[1]
    heads = width // HD
    tiles = width // HD
    stride = block // CTX
    scale = HD ** (-0.5)
    tensor_count = lax.axis_size("tensor")
    tensor_bits = low_bits(tensor_count)
    idx = lax.axis_index("tensor")
    place = lax.axis_index("seq")
    rows = seqs * block
    seg = rows // SUB
    half = model // 2
    pairs = tensor_count // 2
    seq_bits = low_bits(lax.axis_size("seq"))
    first, second = seq_bits[:2]
    line = Line()
    info = jnp.concatenate(
        [
            jnp.stack([(place & first) // first, (place & second) // second, idx, idx & 1]).astype(jnp.int32),
            (lengths - place * block).astype(jnp.int32),
        ]
    )

    flat_in = inputs.reshape(rows, model)
    flat_grad = out_grad.reshape(rows, model)
    gain_all = norm_gain.reshape(1, model)
    gain2 = mlp_gain.reshape(1, model)
    gain_chan = lax.dynamic_slice_in_dim(norm_gain, idx * width, width, 0)
    gain_row = gain_chan.reshape(1, width)
    skip_row = skip_gain.reshape(1, width)
    root = jnp.sqrt(-jnp.expm1(-2.0 * decay_rate))
    coeff = root * state_input
    tab = pltpu.VMEM((NS, SUB, width), F32)
    state_shape = (NS, SUB, width)

    def hop(blocks):
        return jnp.exp(-decay_rate * (jnp.asarray(blocks, F32) * block))[None]

    def rows_of(s):
        return pl.BlockSpec((block, width), lambda *a, s=s: (s, 0))

    wo_parts = gather_parts(out_weight, "tensor")

    tile = 256
    normed_low, inverse, runs, seg_end, final = line.run(
        "enter",
        functools.partial(enter_kernel, seqs, stride),
        (flat_in, flat_in, gain_all, decay_rate),
        [
            pl.BlockSpec((tile, model), lambda i, f: (i, 0)),
            pl.BlockSpec((tile, width), lambda i, f: (i, f[2])),
            full((1, model)),
            full((NS, width)),
        ],
        [
            ((rows, model), BF16, pl.BlockSpec((tile, model), lambda i, f: (i, 0))),
            ((rows, 1), F32, pl.BlockSpec((tile, 1), lambda i, f: (i, 0))),
            out_full((tiles, seg, SUB, HD), F32),
            out_full(state_shape, F32),
            out_full((seqs, NS, width), F32),
        ],
        grid=(rows // tile,),
        prefetch=(info,),
        scratch=[pltpu.VMEM((tiles, rows, HD), F32), tab, tab],
    )
    carry_in = carried(final, hop, "seq", True)

    query, key_self, value_self = line.run(
        "qkv",
        qkv_kernel,
        (normed_low, query_weight, key_weight, value_weight),
        [pl.BlockSpec((tile, model), lambda i: (i, 0))] + [full((model, width))] * 3,
        [((rows, width), BF16, pl.BlockSpec((tile, width), lambda i: (i, 0)))] * 3,
        grid=(rows // tile,),
    )
    ctx_low, entry = line.run(
        "context",
        functools.partial(context_kernel, seqs, stride),
        (runs, seg_end, carry_in, decay_rate, coeff, state_output, skip_row, gain_row),
        [vmem()] * 8,
        [((seqs * CTX, width), BF16, vmem()), (state_shape, F32, vmem())],
        scratch=[tab, tab, tab, pltpu.VMEM((tiles, seqs * CTX, HD), F32)],
        after=wo_parts[2] if tensor_count > 2 else None,
    )
    ctx_parts = gather_parts(ctx_low, "tensor")

    attended, key_ctx, value_ctx, log_sum, att_parts = [], [], [], [], []
    for s in range(seqs):
        a, kc, vc, ls = line.run(
            "attend",
            functools.partial(attend_kernel, tensor_count, scale),
            (query, key_self, value_self, key_weight, value_weight, *ctx_parts),
            [rows_of(s)] * 3
            + [full((model, width))] * 2
            + [pl.BlockSpec((CTX, width), lambda *a, s=s: (s, 0))] * tensor_count,
            [
                out_full((block, width), BF16),
                out_full((CTX, width), BF16),
                out_full((CTX, width), BF16),
                out_full((block, heads), F32),
            ],
            prefetch=(info,),
        )
        attended.append(a)
        key_ctx.append(kc)
        value_ctx.append(vc)
        log_sum.append(ls)
        att_parts.append(gather_parts(a, "tensor"))

    steps = block // tile
    middle, normed2, act, slope, cot = ([] for _ in range(5))
    for s in range(seqs):

        def at(cols, s=s):
            return pl.BlockSpec((tile, cols), lambda i, f, s=s: (s * steps + i, 0))

        def own(cols):
            return pl.BlockSpec((tile, cols), lambda i, f: (i, 0))

        got = line.run(
            "feed",
            functools.partial(feed_kernel, tensor_count, tile, s),
            (flat_in, flat_grad, gain2, up_weight, *att_parts[s], *wo_parts),
            [at(model), at(model), full((1, model)), full((model, units))]
            + [own(width)] * tensor_count
            + [full((width, model))] * tensor_count,
            [((block, c), t, own(c)) for c, t in ((model, F32), (model, BF16), (units, BF16), (units, BF16), (model, BF16))],
            grid=(steps,),
            prefetch=(info,),
            limit=40,
        )
        for slot, value in zip((middle, normed2, act, slope, cot), got):
            slot.append(value)

    box = {}

    def feed_back(s):
        got = line.run(
            "feed_back",
            feed_back_kernel,
            (cot[s], slope[s], up_weight, down_weight),
            [pl.BlockSpec((tile, model), lambda i, f: (i, 0)), pl.BlockSpec((tile, units), lambda i, f: (i, 0)), full((model, units)), full((units, model))],
            [((block, c), BF16, pl.BlockSpec((tile, c), lambda i, f: (i, 0))) for c in (units, half, half)],
            grid=(steps,),
            prefetch=(info,),
            limit=32,
        )
        box["pre", s], box["n2_keep", s] = got[:2]
        box["n2_send", s] = swap(got[2], "tensor", 1)

    def near_core(s):
        box["n2_core", s] = add(line, box["n2_keep", s], box["n2_send", s])
        box["n2_y", s] = swap(box["n2_core", s], "tensor", tensor_bits[1])

    def near_y(s):
        total = add(line, box["n2_core", s], box["n2_y", s])
        for bit in tensor_bits[2:]:
            total = add(line, total, swap(total, "tensor", bit))
        box["n2_near", s] = total
        box["n2_far", s] = swap(total, "tensor", 1)

    def attend_back(s):
        outs = [
            ((block, model), BF16), ((block, width), F32), ((1, model), F32),
            ((block, width), BF16), ((block, width), BF16), ((block, width), BF16),
            ((CTX, width), BF16), ((CTX, width), BF16),
            ((pairs, CTX, width), BF16), ((pairs, CTX, width), BF16),
            ((pairs, block, width), BF16), ((pairs, block, width), BF16),
        ]
        got = line.run(
            "attend_back",
            functools.partial(attend_back_kernel, s, scale),
            (middle[s], box["n2_near", s], box["n2_far", s], flat_grad, gain2, out_weight, query, key_self, value_self, key_ctx[s], value_ctx[s], log_sum[s], query_weight, key_weight, value_weight),
            [full((block, model)), full((block, half)), full((block, half)), pl.BlockSpec((block, model), lambda *a, s=s: (s, 0)), full((1, model)), full((width, model))]
            + [rows_of(s)] * 3
            + [full((CTX, width))] * 2
            + [full((block, heads))]
            + [full((model, width))] * 3,
            [out_full(*o) for o in outs],
            prefetch=(info,),
            scratch=[pltpu.VMEM((block, model), BF16), pltpu.VMEM((block, model), F32)]
            + [pltpu.VMEM((block, HD), F32)] * 2
            + [pltpu.VMEM((CTX, HD), F32)] * 2,
            limit=32,
        )

        box["back", s] = got
        box["ctx_got", s] = swap(got[9], "tensor", 1)
        box["n1_got", s] = swap(got[11], "tensor", 1)

    def backs(k):
        return [box["back", s][k] for s in range(seqs)]

    def both(key):
        return [box[key, s] for s in range(seqs)]

    def sum_start(key, pieces):
        box[key] = pieces[0], swap(pieces[1], "seq", bits_of[key][0])

    def sum_second(key):
        near, far = add_pair(line, *box[key])
        box[key, "near"], box[key, "z"] = near, swap(far, "seq", bits_of[key][1])

    def sum_third(key):
        total = add(line, box[key, "near"], box[key, "z"])
        for bit in bits_of[key][2:-1]:
            total = add(line, total, swap(total, "seq", bit))
        box[key, "total"] = total
        if len(seq_bits) > 2:
            box[key, "hop"] = swap(total, "seq", bits_of[key][-1])

    def sum_last(key):
        total = box[key, "total"]
        if len(seq_bits) > 2:
            total = add(line, total, box[key, "hop"])
        other = swap(total, "seq", bits_of[key][1])
        back0, back1 = swap(total, "seq", bits_of[key][0]), swap(other, "seq", bits_of[key][0])
        box[key, "pieces"] = [total, other, back0, back1]

    def pin(key, k):
        line.held.append(box[key, "pieces"][k])

    def project(_):
        mid_low, mid_slice, gain2_part, dq, dk, dv, dkc, dvc = (backs(k) for k in range(8))
        ctx_stack = jnp.stack(ctx_parts)
        ins = (normed_low, *mid_low, ctx_stack, *dq, *dk, *dv, *dkc, *dvc, *attended)
        got = (
            line.run(
                "project_grad",
                functools.partial(project_grad_kernel, seqs),
                ins,
                [full(a.shape) for a in ins],
                [out_full((2, model // 4, 4 * width), BF16)] * 2,
                prefetch=(info,),
                limit=32,
            )
        )
        sum_start("Q", got)

    def ctx_parts_sum(_):
        box["ctx"] = scatter_parts(add_parts(line, backs(8), both("ctx_got")), "tensor")

    def n1_parts_sum(_):
        box["n1"] = scatter_parts(add_parts(line, backs(10), both("n1_got")), "tensor")

    def lead_step(_):
        ctx_near, ctx_far = box["ctx"]
        ctx_grads, segb_end, lead = line.run(
            "lead",
            functools.partial(lead_kernel, seqs, stride),
            (ctx_near, ctx_far, decay_rate),
            [vmem()] * 3,
            [((tiles, seqs * CTX // SUB, SUB, HD), F32, vmem()), (state_shape, F32, vmem()), ((seqs, NS, width), F32, vmem())],
            scratch=[pltpu.VMEM((tiles, seqs * CTX, HD), F32), tab],
        )
        box["lead"] = ctx_grads, segb_end
        box["carry"] = carried(lead, hop, "seq", False)

    def state_step(_):
        ctx_grads, segb_end = box["lead"]
        carry_back = box["carry"]
        chan_grad, rate_grad, sin_grad, sout_grad, skip_grad = line.run(
            "state_back",
            functools.partial(state_back_kernel, seqs, stride),
            (runs, ctx_grads, entry, segb_end, carry_back, decay_rate, root, state_input, state_output, skip_row, gain_row),
            [vmem()] * 11,
            [((tiles, rows, HD), F32, vmem())] + [((NS, width), F32, vmem())] * 3 + [((1, width), F32, vmem())],
            scratch=[
                tab,
                tab,
                pltpu.VMEM((stride, NS, SUB, width), F32),
                tab,
                pltpu.VMEM((seg // stride + 1, NS, SUB, width), F32),
                pltpu.VMEM((tiles, seg, SUB, HD), F32),
                pltpu.VMEM((stride + 2, NS, width), F32),
            ],
        )
        box["state"] = chan_grad, rate_grad, sin_grad, sout_grad, skip_grad

    def feed_out(s):
        got = line.run(
            "feed_out",
            feed_out_kernel,
            (act[s], down_weight),
            [pl.BlockSpec((tile, units), lambda i, f: (i, 0)), full((units, model))],
            [((block, half), BF16, pl.BlockSpec((tile, half), lambda i, f: (i, 0)))] * 2,
            grid=(steps,),
            prefetch=(info,),
        )
        box["out_keep", s], box["out_send", s] = got[0], swap(got[1], "tensor", 1)

    def out_core(s):
        total = add(line, box["out_keep", s], box["out_send", s])
        for bit in tensor_bits[1:-1]:
            total = add(line, total, swap(total, "tensor", bit))
        box["out_core", s], box["out_y", s] = total, swap(total, "tensor", tensor_bits[-1])

    def out_add(s):
        box["out_near", s] = line.run(
            "add_out",
            add_out_kernel,
            (middle[s], box["out_core", s], box["out_y", s]),
            [full((block, model)), full((block, half)), full((block, half))],
            [out_full((block, half), BF16)],
            prefetch=(info,),
        )[0]
        box["out_far", s] = swap(box["out_near", s], "tensor", 1)

    def join(_):
        box["outputs"] = line.run(
            "join",
            functools.partial(join_kernel, seqs),
            (*both("out_near"), *both("out_far")),
            [full((block, half))] * (2 * seqs),
            [out_full((seqs, block, model), BF16)],
            prefetch=(info,),
        )[0]

    def flags_of(key):
        return swapped if KINDS[key] else info

    def widen_step(key):
        box[key, "wide"] = (widen_project if key == "Q" else widen)(line, flags_of(key), box[key, "pieces"])

    swapped = jnp.concatenate([info[1::-1], info[2:]])
    bits_of = {key: [second, first, *seq_bits[2:]] if kind else seq_bits for key, kind in KINDS.items()}
    steps_of = {
        "outD": lambda k: sum_start("D", outer(line, flags_of("D"), act, cot)),
        "outU": lambda k: sum_start("U", outer(line, flags_of("U"), normed2, both("pre"))),
        "fb": feed_back, "na": near_core, "ny": near_y, "ab": attend_back, "cp": ctx_parts_sum, "np": n1_parts_sum,
        "pr": project, "ld": lead_step, "st": state_step, "fo": feed_out, "oc": out_core, "oa": out_add, "jn": join,
        "s2": sum_second, "s3": sum_third, "s4": sum_last, "wd": widen_step,
        "p1": lambda k: pin(k, 1), "p2": lambda k: pin(k, 2), "p3": lambda k: pin(k, 3),
    }
    for step, which in ORDER:
        steps_of[step](which)
    mid_slice, gain2_part = backs(1), backs(2)
    chan_grad, rate_grad, sin_grad, sout_grad, skip_grad = box["state"]
    outputs, down_grad, up_grad = box["outputs"], box["D", "wide"], box["U", "wide"]
    query_grad, key_grad, value_grad, out_grad_w = box["Q", "wide"]
    n1_near, n1_far = box["n1"]
    n1_share = n1_near.astype(F32) + n1_far.astype(F32)

    in_chan = lax.dynamic_slice_in_dim(flat_in, idx * width, width, 1)
    n1_grad = n1_share + jnp.concatenate([chan_grad[t] for t in range(tiles)], 1)
    hat_chan = in_chan.astype(F32) * inverse
    norm_gain_grad = jnp.sum(n1_grad * hat_chan, 0)
    h1 = n1_grad * gain_chan
    total = jnp.sum(h1 * hat_chan, -1).reshape(rows // 128, 128)
    for bit in tensor_bits:
        total = total + swap(total, "tensor", bit)
    mid_chan = jnp.concatenate(mid_slice, 0)
    input_grad = mid_chan + inverse * (h1 - hat_chan * (total.reshape(rows, 1) / model))
    input_grad = input_grad.astype(BF16).reshape(seqs, block, width)

    mlp_gain_grad = sum(gain2_part)
    small = jnp.concatenate([rate_grad, sin_grad, sout_grad, skip_grad, norm_gain_grad.reshape(1, width), mlp_gain_grad.reshape(model // width, width)], 0)
    for bit in seq_bits:
        small = small + swap(small, "seq", bit)

    return (
        outputs,
        input_grad,
        small[3 * NS + 1],
        query_grad,
        key_grad,
        value_grad,
        out_grad_w,
        small[3 * NS + 2 :].reshape(model),
        up_grad,
        down_grad,
        small[:NS],
        small[NS : 2 * NS],
        small[2 * NS : 3 * NS],
        small[3 * NS],
    )


def solution(mesh):
    in_specs = (
        P(None, "seq", None),
        P(None, "seq", None),
        P(),
        P(),
        P(None, "tensor"),
        P(None, "tensor"),
        P(None, "tensor"),
        P("tensor", None),
        P(),
        P(None, "tensor"),
        P("tensor", None),
        P(None, "tensor"),
        P(None, "tensor"),
        P(None, "tensor"),
        P("tensor"),
    )
    out_specs = (
        P(None, "seq", None),
        P(None, "seq", "tensor"),
        P("tensor"),
        P(None, "tensor"),
        P(None, "tensor"),
        P(None, "tensor"),
        P("tensor", None),
        P(),
        P(None, "tensor"),
        P("tensor", None),
        P(None, "tensor"),
        P(None, "tensor"),
        P(None, "tensor"),
        P("tensor"),
    )
    return jax.shard_map(local, mesh=mesh, in_specs=in_specs, out_specs=out_specs, check_vma=False)
```

```python
import functools

import jax
import jax.numpy as jnp
from jax import lax
from jax.experimental import pallas as pl
from jax.experimental.pallas import tpu as pltpu
from jax.sharding import PartitionSpec as P

HD = 128
NS = 16
CTX = 128
SUB = 8
EPS = 1e-06
F32 = jnp.float32
BF16 = jnp.bfloat16
MIB = 1 << 20


def nn(a, b):
    return lax.dot_general(a, b, (((1,), (0,)), ((), ())), preferred_element_type=F32)


def nt(a, b):
    return lax.dot_general(a, b, (((1,), (1,)), ((), ())), preferred_element_type=F32)


def tn(a, b):
    return lax.dot_general(a, b, (((0,), (0,)), ((), ())), preferred_element_type=F32)


def swap(value, axis, bit):
    count = lax.axis_size(axis)
    return lax.ppermute(value, axis, [(i, i ^ bit) for i in range(count)])


def low_bits(count):
    bit, out = 1, []
    while bit < count:
        out.append(bit)
        bit *= 2
    return out


def sds(shape, dtype):
    return jax.ShapeDtypeStruct(shape, dtype)


def vmem():
    return pl.BlockSpec(memory_space=pltpu.VMEM)


def smem():
    return pl.BlockSpec(memory_space=pltpu.SMEM)


LIMITS = {
    "enter": 10, "qkv": 10, "context": 6, "attend": 12, "feed": 30, "outer": 20, "feed_back": 18, "feed_out": 14,
    "attend_back": 28, "project_grad": 28, "lead": 4, "state_back": 10, "widen": 10, "widen_project": 10,
    "join": 6, "add_out": 12, "norm_back": 12, "input_grad": 12,
}


class Line:
    def __init__(self):
        self.mark = None
        self.held = []

    def run(self, name, kernel, args, in_specs, outs, grid=None, prefetch=(), scratch=(), limit=None, after=None, hbm=()):
        args = [pltpu.with_memory_space_constraint(a, pltpu.HBM) if k in hbm else a for k, a in enumerate(args)]
        in_specs = list(in_specs)
        marks = [] if self.mark is None else [pltpu.with_memory_space_constraint(self.mark, pltpu.HBM)]
        others = [t for t in (after, *self.held) if t is not None]
        self.held = []
        count, extra = len(prefetch) + len(args), len(marks) + len(others)

        def body(*refs):
            return kernel(*refs[:count], *refs[count + extra : count + extra + len(outs)], *refs[count + extra + len(outs) + 1 :])

        in_specs += [pl.BlockSpec(memory_space=pltpu.HBM)] * len(marks) + [pl.BlockSpec(memory_space=pl.ANY)] * len(others)
        *got, self.mark = pl.pallas_call(
            body,
            grid_spec=pltpu.PrefetchScalarGridSpec(
                num_scalar_prefetch=len(prefetch),
                grid=grid or (1,),
                in_specs=in_specs,
                out_specs=[o[2] for o in outs] + [pl.BlockSpec(memory_space=pltpu.HBM)],
                scratch_shapes=list(scratch),
            ),
            out_shape=[pltpu.HBM(o[0], o[1]) if len(o) > 3 else sds(o[0], o[1]) for o in outs] + [pltpu.HBM((SUB, HD), F32)],
            compiler_params=pltpu.CompilerParams(vmem_limit_bytes=(limit or LIMITS[name]) * MIB),
            cost_estimate=pl.CostEstimate(flops=1, bytes_accessed=1, transcendentals=0),
            name=name,
        )(*prefetch, *args, *marks, *others)
        return got


def full(shape):
    return pl.BlockSpec(shape, lambda *a: (0,) * len(shape))


def out_full(shape, dtype):
    return (shape, dtype, full(shape))


def lanes(tile):
    return slice(tile * HD, (tile + 1) * HD)


def spread(table, rows, factor=None):
    for n in range(NS):
        row = rows[n : n + 1, :]
        if factor is not None:
            row = jnp.exp(row * factor)
        table[n] = jnp.broadcast_to(row, table.shape[1:])


def scan_step(taps, decay_tab, jump_tab, state):
    tiles = len(taps)
    out = []
    for n in range(NS):
        for t in range(tiles):
            decay = decay_tab[n, :, lanes(t)]
            inner = taps[t][0]
            for tap in taps[t][1:]:
                inner = inner * decay + tap
            out.append(state[n * tiles + t] * jump_tab[n, :, lanes(t)] + inner)
    return tuple(out)


def taps_of(runs_ref, group, stride):
    return [[runs_ref[t, group * stride + i] for i in range(stride)] for t in range(runs_ref.shape[0])]


def segment_ends(state, rate, seg, seqs, seg_ref, end_ref, forward):
    per = SUB // seqs
    tiles = rate.shape[1] // HD
    place = lax.rem(lax.broadcasted_iota(jnp.int32, (SUB, HD), 0), per)
    away = ((per - 1 - place if forward else place) * seg).astype(F32)
    for n in range(NS):
        for t in range(tiles):
            now = state[n * tiles + t]
            seg_ref[n, :, lanes(t)] = now
            part = now * jnp.exp(-rate[n : n + 1, lanes(t)] * away)
            for s in range(seqs):
                end_ref[s, n : n + 1, lanes(t)] = jnp.sum(part[s * per : (s + 1) * per], 0, keepdims=True)


def entry_states(entry_ref, carry_ref, seg_ref, hop, seqs, forward):
    per = SUB // seqs
    for n in range(NS):
        step = hop[n : n + 1, :]
        for s in range(seqs):
            now = carry_ref[s, n : n + 1, :]
            for k in range(per):
                q = s * per + (k if forward else per - 1 - k)
                entry_ref[n, q : q + 1, :] = now
                if k < per - 1:
                    now = now * step + seg_ref[n, q : q + 1, :]


def read_state(ref):
    tiles = ref.shape[2] // HD
    return tuple(ref[n, :, lanes(t)] for n in range(NS) for t in range(tiles))


PACKED = 72
CHUNK = 128


def unpack(pack_ref):
    return (*(pack_ref[k * NS : (k + 1) * NS, :] for k in range(4)), pack_ref[4 * NS : 4 * NS + 1, :], pack_ref[4 * NS + 1 : 4 * NS + 2, :])


def enter_kernel(seqs, stride, info_ref, x_ref, xc_ref, gain_ref, rate_ref, low_ref, inv_ref, runs_ref, seg_ref, fin_ref, flat, decay_tab, jump_tab):
    step, width = x_ref.shape
    tiles, seg = runs_ref.shape[:2]
    piece = CHUNK
    gain = gain_ref[...]
    rate = rate_ref[...]

    @pl.when(pl.program_id(0) == 0)
    def _():
        spread(decay_tab, rate, -1.0)
        spread(jump_tab, rate, -float(stride))

    def norm(i, carry):
        at = pl.ds(pl.multiple_of(i * piece, piece), piece)
        x = x_ref[at, :].astype(F32)
        inv = lax.rsqrt(jnp.sum(x * x, -1, keepdims=True) * (1.0 / width) + EPS)
        low_ref[at, :] = (x * inv * gain).astype(BF16)
        inv_ref[at, :] = inv
        to = pl.ds(pl.multiple_of(pl.program_id(0) * step + i * piece, piece), piece)
        for t in range(tiles):
            flat[t, to, :] = xc_ref[at, lanes(t)].astype(F32) * inv
        return carry

    lax.fori_loop(0, step // piece, norm, 0)

    @pl.when(pl.program_id(0) == pl.num_programs(0) - 1)
    def _():
        def group(g, state):
            taps = []
            for t in range(tiles):
                row = [flat[t, pl.ds(g * stride + i, SUB, stride=seg), :] for i in range(stride)]
                for i in range(stride):
                    runs_ref[t, g * stride + i] = row[i]
                taps.append(row)
            return scan_step(taps, decay_tab, jump_tab, state)

        state = lax.fori_loop(0, seg // stride, group, (jnp.zeros((SUB, HD), F32),) * (NS * tiles))
        segment_ends(state, rate, seg, seqs, seg_ref, fin_ref, True)


def context_kernel(seqs, stride, runs_ref, seg_ref, carry_ref, pack_ref, ctx_ref, entry_ref, decay_tab, jump_tab, out_tab, flat):
    tiles, seg = runs_ref.shape[:2]
    rate, root, s_in, s_out, skip, gain = unpack(pack_ref)
    spread(decay_tab, rate, -1.0)
    spread(jump_tab, rate, -float(stride))
    spread(out_tab, root * s_in * s_out * gain)
    entry_states(entry_ref, carry_ref, seg_ref, jnp.exp(rate * (-float(seg))), seqs, True)
    skip = skip * gain
    groups = seg // stride

    def group(g, state):
        taps = taps_of(runs_ref, g, stride)
        state = scan_step(taps, decay_tab, jump_tab, state)
        for t in range(tiles):
            total = skip[:, lanes(t)] * taps[t][-1]
            for n in range(NS):
                total = total + out_tab[n, :, lanes(t)] * state[n * tiles + t]
            flat[t, pl.ds(g, SUB, stride=groups), :] = total
        return state

    lax.fori_loop(0, groups, group, read_state(entry_ref))
    for t in range(tiles):
        ctx_ref[:, lanes(t)] = flat[t].astype(BF16)


def lead_kernel(seqs, stride, near_ref, far_ref, pack_ref, grads_ref, segb_ref, lead_ref, flat, jump_tab):
    tiles, groups = grads_ref.shape[:2]
    for t in range(tiles):
        flat[t] = near_ref[:, lanes(t)].astype(F32) + far_ref[:, lanes(t)].astype(F32)
    rate = unpack(pack_ref)[0]
    spread(jump_tab, rate, -float(stride))

    def group(i, state):
        g = groups - 1 - i
        grads = [flat[t, pl.ds(g, SUB, stride=groups), :] for t in range(tiles)]
        for t in range(tiles):
            grads_ref[t, g] = grads[t]
        return tuple(state[n * tiles + t] * jump_tab[n, :, lanes(t)] + grads[t] for n in range(NS) for t in range(tiles))

    state = lax.fori_loop(0, groups, group, (jnp.zeros((SUB, HD), F32),) * (NS * tiles))
    segment_ends(state, rate, groups * stride, seqs, segb_ref, lead_ref, False)


def state_back_kernel(
    seqs, stride, runs_ref, grads_ref, entry_ref, segb_ref, carryb_ref, pack_ref, back_ref, packg_ref,
    decay_tab, jump_tab, tap_tab, entryb, states, backs, sums,
):
    tiles, seg = runs_ref.shape[:2]
    groups = seg // stride
    rate, root, s_in, s_out, skip, gain = unpack(pack_ref)
    coeff = root * s_in
    spread(decay_tab, rate, -1.0)
    spread(jump_tab, rate, -float(stride))
    both = coeff * s_out
    for i in range(stride):
        spread(tap_tab.at[i], both * jnp.exp(rate * (-float(stride - 1 - i))))
    entry_states(entryb, carryb_ref, segb_ref, jnp.exp(rate * (-float(seg))), seqs, False)
    zero = jnp.zeros((SUB, HD), F32)

    def forward(g, carry):
        state, totals = carry
        for n in range(NS):
            for t in range(tiles):
                states[g, n, :, lanes(t)] = state[n * tiles + t]
        taps = taps_of(runs_ref, g, stride)
        out = []
        for t in range(tiles):
            grad = grads_ref[t, g]
            out.append(totals[t] + grad * taps[t][-1])
            backs[t, g * stride + stride - 1] = grad * skip[:, lanes(t)]
            for i in range(stride - 1):
                backs[t, g * stride + i] = zero
        return scan_step(taps, decay_tab, jump_tab, state), tuple(out)

    last, totals = lax.fori_loop(0, groups, forward, (read_state(entry_ref), (zero,) * tiles))
    for n in range(NS):
        for t in range(tiles):
            states[groups, n, :, lanes(t)] = last[n * tiles + t]
    for t in range(tiles):
        packg_ref[3 * NS : 3 * NS + 1, lanes(t)] = jnp.sum(totals[t], 0, keepdims=True) * gain[:, lanes(t)]
    lot = 2
    kinds = stride + 2
    for t in range(tiles):
        for first in range(0, NS, lot):
            names = range(first, first + lot)

            def group(i, carry, t=t, names=names):
                g = groups - 1 - i
                adj, acc = carry
                grad = grads_ref[t, g]
                taps = [runs_ref[t, g * stride + i] for i in range(stride)]
                sums_b = [backs[t, g * stride + i] for i in range(stride)]
                new_adj, new_acc = [], []
                for k, n in enumerate(names):
                    now = adj[k] * jump_tab[n, :, lanes(t)] + grad
                    new_adj.append(now)
                    for i in range(stride):
                        sums_b[i] = sums_b[i] + tap_tab[i, n, :, lanes(t)] * now
                        new_acc.append(acc[k * kinds + i] + now * taps[i])
                    new_acc.append(acc[k * kinds + stride] + now * states[g, n, :, lanes(t)])
                    new_acc.append(acc[k * kinds + stride + 1] + grad * states[g + 1, n, :, lanes(t)])
                for i in range(stride):
                    backs[t, g * stride + i] = sums_b[i]
                return tuple(new_adj), tuple(new_acc)

            start = (tuple(entryb[n, :, lanes(t)] for n in names), (zero,) * (lot * kinds))
            _, acc = lax.fori_loop(0, groups, group, start, unroll=2)
            for k, n in enumerate(names):
                for j in range(kinds):
                    sums[j, n : n + 1, lanes(t)] = jnp.sum(acc[k * kinds + j], 0, keepdims=True)

    def spill(g, carry):
        for t in range(tiles):
            for i in range(stride):
                back_ref[t, pl.ds(g * stride + i, SUB, stride=seg), :] = backs[t, g * stride + i]
        return carry

    lax.fori_loop(0, groups, spill, 0)
    decay = jnp.exp(-rate)
    powers = [jnp.ones_like(rate)]
    for _ in range(stride):
        powers.append(powers[-1] * decay)
    coeff_grad = sum(powers[stride - 1 - i] * sums[i] for i in range(stride)) * s_out * gain
    decay_grad = float(stride) * powers[stride - 1] * sums[stride]
    for i in range(stride - 1):
        decay_grad = decay_grad + float(stride - 1 - i) * powers[stride - 2 - i] * sums[i]
    decay_grad = decay_grad * coeff * s_out * gain
    packg_ref[:NS, :] = coeff_grad * s_in * (decay * decay / root) - decay * decay_grad
    packg_ref[NS : 2 * NS, :] = coeff_grad * root
    packg_ref[2 * NS : 3 * NS, :] = coeff * gain * sums[stride + 1]


def carried(value, hop, axis, forward, seen=None):
    count = lax.axis_size(axis)
    mine = lax.axis_index(axis)
    whole = value
    enter = jnp.zeros_like(value)
    for bit in low_bits(count):
        other = swap(whole, axis, bit)
        if seen is not None:
            seen.append(other)
        upper = (mine & bit) != 0
        offset = mine & (bit - 1)
        if not forward:
            upper = jnp.logical_not(upper)
            offset = bit - 1 - offset
        enter = jnp.where(upper, enter + hop(offset) * other, enter)
        span = hop(bit)
        whole = jnp.where(upper, whole + span * other, other + span * whole)
    return enter


def qkv_kernel(x_ref, wq_ref, wk_ref, wv_ref, q_ref, k_ref, v_ref):
    x = x_ref[...]
    q_ref[...] = nn(x, wq_ref[...]).astype(BF16)
    k_ref[...] = nn(x, wk_ref[...]).astype(BF16)
    v_ref[...] = nn(x, wv_ref[...]).astype(BF16)


def masks(first, tile, block, stride):
    row = lax.broadcasted_iota(jnp.int32, (tile, CTX), 0) + first
    col = lax.broadcasted_iota(jnp.int32, (tile, CTX), 1)
    side = stride * col + (stride - 1) <= row
    row = lax.broadcasted_iota(jnp.int32, (tile, block), 0) + first
    col = lax.broadcasted_iota(jnp.int32, (tile, block), 1)
    return side, col <= row


def attend_kernel(parts, scale, idx_ref, q_ref, k_ref, v_ref, wk_ref, wv_ref, *rest):
    ctx_refs, (out_ref, kc_ref, vc_ref, lse_ref) = rest[:parts], rest[parts:]
    block, width = q_ref.shape
    stride = block // CTX
    idx = idx_ref[2]
    key_c = jnp.zeros((CTX, width), F32)
    val_c = jnp.zeros((CTX, width), F32)
    for p in range(parts):
        at = pl.ds(pl.multiple_of((idx ^ p) * width, width), width)
        key_c = key_c + nn(ctx_refs[p][...], wk_ref[at, :])
        val_c = val_c + nn(ctx_refs[p][...], wv_ref[at, :])
    kc_ref[...] = key_c.astype(BF16)
    vc_ref[...] = val_c.astype(BF16)
    tile = min(256, block)
    for h in range(width // HD):
        cols = slice(h * HD, (h + 1) * HD)
        for first in range(0, block, tile):
            seen = first + tile
            rows = slice(first, seen)
            q = q_ref[rows, cols]
            side_ok, own_ok = masks(first, tile, seen, stride)
            side = jnp.where(side_ok, nt(q, kc_ref[:, cols]), -1e30)
            own = jnp.where(own_ok, nt(q, k_ref[:seen, cols]), -1e30)
            top = jnp.maximum(jnp.max(side, -1, keepdims=True), jnp.max(own, -1, keepdims=True))
            side = jnp.exp((side - top) * scale)
            own = jnp.exp((own - top) * scale)
            total = jnp.sum(side, -1, keepdims=True) + jnp.sum(own, -1, keepdims=True)
            share = 1.0 / total
            got = nn((side * share).astype(BF16), vc_ref[:, cols]) + nn((own * share).astype(BF16), v_ref[:seen, cols])
            out_ref[rows, cols] = got.astype(BF16)
            lse_ref[rows, h : h + 1] = top * scale + jnp.log(total)


def attend_back_kernel(
    seq, scale, info_ref, mid_ref, near_ref, far_ref, grad_ref, gain_ref, wo_ref, q_ref, k_ref, v_ref, kc_ref, vc_ref, lse_ref,
    wq_ref, wk_ref, wv_ref,
    low_ref, slice_ref, gaing_ref, dq_ref, dk_ref, dv_ref, dkc_ref, dvc_ref, keep_ref, send_ref,
    n2_ref, full_ref, key_acc, val_acc, skey_acc, sval_acc,
):
    block, width = q_ref.shape
    model = mid_ref.shape[1]
    half = model // 2
    stride = block // CTX
    idx, mine, limit = info_ref[2], info_ref[3], info_ref[4 + seq]
    n2_ref[:, pl.ds(pl.multiple_of(mine * half, half), half)] = near_ref[...]
    n2_ref[:, pl.ds(pl.multiple_of((1 - mine) * half, half), half)] = far_ref[...]
    gain = gain_ref[...]
    step = CHUNK

    def norm(i, total):
        at = pl.ds(pl.multiple_of(i * step, step), step)
        mid = mid_ref[at, :]
        inv = lax.rsqrt(jnp.sum(mid * mid, -1, keepdims=True) * (1.0 / model) + EPS)
        hat = mid * inv
        n2 = n2_ref[at, :].astype(F32)
        prod = n2 * hat
        h2 = n2 * gain
        mean = jnp.sum(h2 * hat, -1, keepdims=True) * (1.0 / model)
        place = lax.broadcasted_iota(jnp.int32, (step, 1), 0) + i * step
        cot = jnp.where(place < limit, grad_ref[at, :].astype(F32), 0.0)
        grad = cot + inv * (h2 - hat * mean)
        full_ref[at, :] = grad
        low_ref[at, :] = grad.astype(BF16)
        return total + jnp.sum(prod, 0, keepdims=True)

    gaing_ref[...] = lax.fori_loop(0, block // step, norm, jnp.zeros((1, model), F32))
    slice_ref[...] = full_ref[:, pl.ds(pl.multiple_of(idx * width, width), width)]
    att_grad = nt(low_ref[...], wo_ref[...]).astype(BF16)
    tile = min(256, block)
    for h in range(width // HD):
        cols = slice(h * HD, (h + 1) * HD)
        for first in range(0, block, tile):
            seen = first + tile
            rows = slice(first, seen)
            q = q_ref[rows, cols]
            grad = att_grad[rows, cols]
            lse = lse_ref[rows, h : h + 1]
            side_ok, own_ok = masks(first, tile, seen, stride)
            kc, k = kc_ref[:, cols], k_ref[:seen, cols]
            side = jnp.exp(jnp.where(side_ok, nt(q, kc) * scale - lse, -1e30))
            own = jnp.exp(jnp.where(own_ok, nt(q, k) * scale - lse, -1e30))
            dside = nt(grad, vc_ref[:, cols])
            down = nt(grad, v_ref[:seen, cols])
            term = jnp.sum(side * dside, -1, keepdims=True) + jnp.sum(own * down, -1, keepdims=True)
            dside = (side * (dside - term)).astype(BF16)
            down = (own * (down - term)).astype(BF16)
            dq_ref[rows, cols] = ((nn(dside, kc) + nn(down, k)) * scale).astype(BF16)
            side = side.astype(BF16)
            own = own.astype(BF16)
            last = first + tile >= block
            fresh = first == 0
            for acc, score, right in (
                (skey_acc, dside, q),
                (sval_acc, side, grad),
            ):
                got = tn(score, right)
                acc[...] = got if fresh else acc[...] + got
            for acc, score, right in (
                (key_acc, down, q),
                (val_acc, own, grad),
            ):
                got = tn(score, right)
                if fresh:
                    acc[:seen, :] = got
                else:
                    acc[:first, :] = acc[:first, :] + got[:first]
                    acc[first:seen, :] = got[first:]
            if last:
                dk_ref[:, cols] = (key_acc[...] * scale).astype(BF16)
                dv_ref[:, cols] = val_acc[...].astype(BF16)
                dkc_ref[:, cols] = (skey_acc[...] * scale).astype(BF16)
                dvc_ref[:, cols] = sval_acc[...].astype(BF16)
    count = model // width
    for p in range(count):
        at = pl.ds(pl.multiple_of((idx ^ p) * width, width), width)
        wk, wv = wk_ref[at, :], wv_ref[at, :]
        ctx = nt(dkc_ref[...], wk) + nt(dvc_ref[...], wv)
        (send_ref if p % 2 else keep_ref)[p // 2, :CTX, :] = ctx.astype(BF16)
    for p in range(count):
        at = pl.ds(pl.multiple_of((idx ^ p) * width, width), width)
        own = nt(dq_ref[...], wq_ref[at, :]) + nt(dk_ref[...], wk_ref[at, :]) + nt(dv_ref[...], wv_ref[at, :])
        (send_ref if p % 2 else keep_ref)[p // 2, CTX:, :] = own.astype(BF16)


def feed_kernel(parts, tile, seq, info_ref, x_ref, grad_ref, gain_ref, up_ref, *rest):
    att_refs, wo_refs = rest[:parts], rest[parts : 2 * parts]
    mid_ref, n2_ref, act_ref, slope_ref, cot_ref = rest[2 * parts :]
    model = x_ref.shape[1]
    limit = info_ref[4 + seq]
    mid = x_ref[...].astype(F32)
    got = nn(att_refs[0][...], wo_refs[0][...])
    for p in range(1, parts):
        got = got + nn(att_refs[p][...], wo_refs[p][...])
    mid = mid + got
    mid_ref[...] = mid
    inv = lax.rsqrt(jnp.sum(mid * mid, -1, keepdims=True) * (1.0 / model) + EPS)
    n2_ref[...] = (mid * inv * gain_ref[...]).astype(BF16)
    place = lax.broadcasted_iota(jnp.int32, (tile, 1), 0) + pl.program_id(0) * tile
    cot_ref[...] = jnp.where(place < limit, grad_ref[...].astype(F32), 0.0).astype(BF16)
    pre = nn(n2_ref[...], up_ref[...])
    cdf = 0.5 * (1.0 + lax.erf(pre * 0.7071067811865476))
    pdf = jnp.exp(pre * pre * -0.5) * 0.3989422804014327
    act_ref[...] = (pre * cdf).astype(BF16)
    slope_ref[...] = (cdf + pre * pdf).astype(BF16)


def halves(info_ref, half):
    mine = info_ref[3]
    return (
        pl.ds(pl.multiple_of(mine * half, half), half),
        pl.ds(pl.multiple_of((1 - mine) * half, half), half),
    )


def feed_back_kernel(info_ref, cot_ref, slope_ref, up_ref, down_ref, pre_ref, keep_ref, send_ref):
    near, far = halves(info_ref, keep_ref.shape[1])
    pull = nt(cot_ref[...], down_ref[...])
    pre_ref[...] = (pull * slope_ref[...].astype(F32)).astype(BF16)
    send_ref[...] = nt(pre_ref[...], up_ref[far, :]).astype(BF16)
    keep_ref[...] = nt(pre_ref[...], up_ref[near, :]).astype(BF16)


def feed_out_kernel(seqs, steps, info_ref, *refs):
    down_ref, keep_ref, send_ref = refs[seqs:]
    near, far = halves(info_ref, keep_ref.shape[1])
    for s in range(seqs):

        @pl.when(pl.program_id(0) // steps == s)
        def _(s=s):
            send_ref[...] = nn(refs[s][...], down_ref[:, far]).astype(BF16)
            keep_ref[...] = nn(refs[s][...], down_ref[:, near]).astype(BF16)


def add_kernel(a_ref, b_ref, out_ref):
    out_ref[...] = (a_ref[...].astype(F32) + b_ref[...].astype(F32)).astype(BF16)


def add_pair_kernel(a_ref, b_ref, out0_ref, out1_ref):
    out0_ref[...] = (a_ref[0].astype(F32) + b_ref[0].astype(F32)).astype(BF16)
    out1_ref[...] = (a_ref[1].astype(F32) + b_ref[1].astype(F32)).astype(BF16)


def add_parts_kernel(pairs, count, start, size, *refs):
    keeps, gots, outs = refs[:count], refs[count : 2 * count], refs[2 * count :]
    at = slice(start, start + size)
    for m in range(pairs):
        for s in range(count):
            outs[m][s * size : (s + 1) * size, :] = (keeps[s][m, at].astype(F32) + gots[s][m, at].astype(F32)).astype(BF16)


def add_out_kernel(seqs, info_ref, *refs):
    mids, (a_ref, b_ref, out_ref) = refs[:seqs], refs[seqs:]
    near, _ = halves(info_ref, out_ref.shape[1])
    block = mids[0].shape[0]
    for s in range(seqs):
        at = slice(s * block, (s + 1) * block)
        total = a_ref[at, :].astype(F32) + b_ref[at, :].astype(F32)
        out_ref[at, :] = (mids[s][:, near] + total).astype(BF16)


def join_kernel(info_ref, near_ref, far_ref, out_ref):
    near, far = halves(info_ref, near_ref.shape[1])
    out_ref[:, near] = near_ref[...]
    out_ref[:, far] = far_ref[...]


def high(a, b, dims):
    return lax.dot_general(a, b, (dims, ((), ())), precision=lax.Precision.HIGHEST, preferred_element_type=F32)


def norm_back_kernel(seqs, near_ref, far_ref, back_ref, x_ref, inv_ref, pack_ref, packg_ref, *refs):
    gains, (h1_ref, small_ref, sums_ref) = refs[:seqs], refs[seqs:]
    tiles, rows = back_ref.shape[:2]
    width = tiles * HD
    gain = unpack(pack_ref)[5]
    step = 128
    ones = jnp.ones((SUB, HD), F32)

    def part(i, total):
        at = pl.ds(pl.multiple_of(i * step, step), step)
        inv = inv_ref[at, :]
        sums, out = 0.0, []
        for t in range(tiles):
            n1 = near_ref[at, lanes(t)].astype(F32) + far_ref[at, lanes(t)].astype(F32) + back_ref[t, at, :]
            hat = x_ref[at, lanes(t)].astype(F32) * inv
            prod = n1 * hat
            h1 = n1 * gain[:, lanes(t)]
            h1_ref[at, lanes(t)] = h1
            out.append(total[t] + jnp.sum(prod, 0, keepdims=True))
            sums = sums + h1 * hat
        sums_ref[:, at] = high(ones, sums, ((1,), (1,)))
        return tuple(out)

    total = lax.fori_loop(0, rows // step, part, (jnp.zeros((1, HD), F32),) * tiles)
    small_ref[...] = jnp.zeros(small_ref.shape, F32)
    small_ref[: 3 * NS + 1, :] = packg_ref[: 3 * NS + 1, :]
    for t in range(tiles):
        small_ref[3 * NS + 1 : 3 * NS + 2, lanes(t)] = total[t]
    gain2 = gains[0][...]
    for s in range(1, seqs):
        gain2 = gain2 + gains[s][...]
    for k in range(gain2.shape[1] // width):
        small_ref[3 * NS + 2 + k : 3 * NS + 3 + k, :] = gain2[:, k * width : (k + 1) * width]


def add_wide_kernel(a_ref, b_ref, out_ref):
    out_ref[...] = a_ref[...] + b_ref[...]


def add_wide(line, a, b):
    return line.run("add", add_wide_kernel, (a, b), [full(a.shape)] * 2, [out_full(a.shape, F32)], limit=4)[0]


def input_grad_kernel(seqs, model, h1_ref, sums_ref, more_ref, x_ref, inv_ref, *refs):
    mids, out_ref = refs[:seqs], refs[seqs]
    block, width = mids[0].shape
    step = 128
    ones = jnp.full((SUB, HD), 1.0 / (SUB * model), F32)
    for s in range(seqs):

        def part(i, carry, s=s):
            at = pl.ds(pl.multiple_of(s * block + i * step, step), step)
            here = pl.ds(pl.multiple_of(i * step, step), step)
            inv = inv_ref[at, :]
            mean = high(sums_ref[:, at] + more_ref[:, at], ones, ((0,), (0,)))
            for t in range(width // HD):
                hat = x_ref[at, lanes(t)].astype(F32) * inv
                grad = mids[s][here, lanes(t)] + inv * (h1_ref[at, lanes(t)] - hat * mean)
                out_ref[at, lanes(t)] = grad.astype(BF16)
            return carry

        lax.fori_loop(0, block // step, part, 0)


def add_pair(line, a, b):
    return line.run("add_pair", add_pair_kernel, (a, b), [full(a.shape)] * 2, [out_full(a.shape[1:], BF16)] * 2, limit=8)


def add_parts(line, keeps, gots, start, size):
    pairs, _, width = keeps[0].shape
    count = len(keeps)
    return line.run(
        "add_parts",
        functools.partial(add_parts_kernel, pairs, count, start, size),
        (*keeps, *gots),
        [full(keeps[0].shape)] * (2 * count),
        [out_full((count * size, width), BF16)] * pairs,
        limit=12,
    )


def add(line, a, b):
    return line.run("add", add_kernel, (a, b), [full(a.shape)] * 2, [out_full(a.shape, BF16)], limit=8)[0]


def quarter(info, far, step):
    return (info[0] ^ far) * 2 + (info[1] ^ step)


PIECES = ((0, 0), (0, 1), (1, 0), (1, 1))


def outer_kernel(pairs, info_ref, *refs):
    piece = refs[0].shape[1] // 4
    for far, step in PIECES:
        out_ref = refs[2 * pairs + far].at[step]
        at = pl.ds(pl.multiple_of(quarter(info_ref, far, step) * piece, piece), piece)
        total = tn(refs[0][:, at], refs[pairs][...])
        for p in range(1, pairs):
            total = total + tn(refs[p][:, at], refs[pairs + p][...])
        out_ref[...] = total.astype(BF16)


def outer(line, info, lefts, rights):
    rows, cols = lefts[0].shape[1], rights[0].shape[1]
    return line.run(
        "outer",
        functools.partial(outer_kernel, len(lefts)),
        [*lefts, *rights],
        [full(a.shape) for a in (*lefts, *rights)],
        [out_full((2, rows // 4, cols), BF16)] * 2,
        prefetch=(info,),
    )


def project_grad_kernel(seqs, info_ref, *refs):
    refs = list(refs)

    def take(count):
        got = refs[:count]
        del refs[:count]
        return got

    (low_ref,) = take(1)
    mids = take(seqs)
    (ctx_ref,) = take(1)
    dqs, dks, dvs, dkcs, dvcs, atts = (take(seqs) for _ in range(6))
    block, width = dqs[0].shape
    quart = low_ref.shape[1] // 4 // width
    for far, step in PIECES:
        out_ref = refs[far].at[step]
        for i in range(quart):
            part = quarter(info_ref, far, step) * quart + i
            at = pl.ds(pl.multiple_of(part * width, width), width)
            rows = slice(i * width, (i + 1) * width)
            for k, (grads, more) in enumerate(((dqs, None), (dks, dkcs), (dvs, dvcs))):
                total = 0.0
                for s in range(seqs):
                    total = total + tn(low_ref[s * block : (s + 1) * block, at], grads[s][...])
                    if more is not None:
                        total = total + tn(ctx_ref[part ^ info_ref[2], s * CTX : (s + 1) * CTX, :], more[s][...])
                out_ref[rows, k * width : (k + 1) * width] = total.astype(BF16)
            total = 0.0
            for s in range(seqs):
                total = total + tn(atts[s][...], mids[s][:, at])
            out_ref[rows, 3 * width :] = total.astype(BF16)


def widen_kernel(flags_ref, *refs):
    for p in range(4):

        @pl.when(pl.program_id(0) == p)
        def _(p=p):
            refs[4][...] = refs[p][...].astype(F32)


def order(p, f):
    return quarter(f, p // 2, p % 2)


def only_at(q, last):
    return lambda p, r, f: (jnp.where(p == q, r, jnp.where(p < q, 0, last)), 0)


def widen(line, info, pieces, after=None):
    piece, cols = pieces[0].shape
    parts = 1
    return line.run(
        "widen",
        widen_kernel,
        pieces,
        [pl.BlockSpec((piece // parts, cols), only_at(q, parts - 1)) for q in range(4)],
        [((4 * piece, cols), F32, pl.BlockSpec((piece // parts, cols), lambda p, r, f: (order(p, f) * parts + r, 0)))],
        grid=(4, parts),
        prefetch=(info,),
        after=after,
    )[0]


def widen_project_kernel(flags_ref, *refs):
    width = refs[0].shape[1] // 4
    for p in range(4):

        @pl.when(pl.program_id(0) == p)
        def _(p=p):
            for k in range(3):
                refs[4 + k][...] = refs[p][:, k * width : (k + 1) * width].astype(F32)
            for j in range(refs[0].shape[0] // width):
                refs[7][:, j * width : (j + 1) * width] = refs[p][j * width : (j + 1) * width, 3 * width :].astype(F32)


def widen_project(line, info, pieces):
    piece, cols = pieces[0].shape
    width = cols // 4
    return line.run(
        "widen_project",
        widen_project_kernel,
        pieces,
        [full((piece, cols))] * 4,
        [((4 * piece, width), F32, pl.BlockSpec((piece, width), lambda p, f: (order(p, f), 0)))] * 3
        + [((width, 4 * piece), F32, pl.BlockSpec((width, piece), lambda p, f: (0, order(p, f))))],
        grid=(4,),
        prefetch=(info,),
    )


def gather_parts(value, axis):
    parts = [value]
    for bit in reversed(low_bits(lax.axis_size(axis))):
        parts = parts + [None] * 0 + [swap(p, axis, bit) for p in parts]
    count = len(parts)
    order = [0]
    for bit in reversed(low_bits(count)):
        order = order + [k ^ bit for k in order]
    out = [None] * count
    for k, p in zip(order, parts):
        out[k] = p
    return out


def add_low(a, b):
    return (a.astype(F32) + b.astype(F32)).astype(BF16)


def scatter_parts(parts, axis):
    bits = low_bits(lax.axis_size(axis))[1:]
    for bit in bits:
        keep, send = parts[0::2], parts[1::2]
        got = [swap(p, axis, bit) for p in send]
        if bit != bits[-1]:
            parts = [add_low(a, b) for a, b in zip(keep, got)]
    return keep[0], got[0]


KINDS = {"D": 0, "U": 0, "Q": 0}
ORDER = (
    ("outD", 0), ("fb", 0), ("fb", 1), ("na", 0), ("outU", 0), ("na", 1), ("ny", 0), ("s2", "D"), ("ny", 1),
    ("ab", 0), ("s3", "D"), ("ab", 1), ("s2", "U"), ("fo", 0), ("pr", 0), ("np", 0), ("cp", 0), ("ld", 0),
    ("s4", "D"), ("s3", "U"), ("s2", "Q"), ("s4", "U"), ("p1", "D"), ("st", 0), ("p2", "U"), ("oc", 0), ("s3", "Q"),
    ("p1", "U"), ("nb", 0), ("rs", 0), ("p2", "D"), ("e", 0), ("wd", "D"), ("e", 1), ("s4", "Q"), ("ig", 0),
    ("wd", "U"), ("c", 0), ("p3", "U"), ("c", 1), ("p2", "Q"), ("e", 2), ("oa", 0), ("jn", 0), ("wd", "Q"),
)


def local(
    inputs, out_grad, lengths, norm_gain, query_weight, key_weight, value_weight, out_weight,
    mlp_gain, up_weight, down_weight, decay_rate, state_input, state_output, skip_gain,
):
    seqs, block, model = inputs.shape
    width = query_weight.shape[1]
    units = up_weight.shape[1]
    heads = width // HD
    tiles = width // HD
    stride = block // CTX
    scale = HD ** (-0.5)
    tensor_count = lax.axis_size("tensor")
    tensor_bits = low_bits(tensor_count)
    idx = lax.axis_index("tensor")
    place = lax.axis_index("seq")
    rows = seqs * block
    seg = rows // SUB
    half = model // 2
    pairs = tensor_count // 2
    small_rows = (3 * NS + 2 + tensor_count + 7) // 8 * 8
    seq_bits = low_bits(lax.axis_size("seq"))
    first, second = seq_bits[:2]
    line = Line()
    info = jnp.concatenate(
        [
            jnp.stack([(place & first) // first, (place & second) // second, idx, idx & 1]).astype(jnp.int32),
            (lengths - place * block).astype(jnp.int32),
        ]
    )

    flat_in = inputs.reshape(rows, model)
    flat_grad = out_grad.reshape(rows, model)
    gain_all = norm_gain.reshape(1, model)
    gain2 = mlp_gain.reshape(1, model)
    gain_chan = lax.dynamic_slice_in_dim(norm_gain, idx * width, width, 0)
    gain_row = gain_chan.reshape(1, width)
    pack = jnp.concatenate(
        [
            decay_rate,
            jnp.sqrt(-jnp.expm1(-2.0 * decay_rate)),
            state_input,
            state_output,
            skip_gain.reshape(1, width),
            gain_row,
            jnp.zeros((PACKED - 4 * NS - 2, width), F32),
        ]
    )
    tab = pltpu.VMEM((NS, SUB, width), F32)
    state_shape = (NS, SUB, width)

    def hop(blocks):
        return jnp.exp(-decay_rate * (jnp.asarray(blocks, F32) * block))[None]

    def rows_of(s):
        return pl.BlockSpec((block, width), lambda *a, s=s: (s, 0))

    wo_parts = gather_parts(out_weight, "tensor")

    tile = 256
    normed_low, inverse, runs, seg_end, final = line.run(
        "enter",
        functools.partial(enter_kernel, seqs, stride),
        (flat_in, flat_in, gain_all, decay_rate),
        [
            pl.BlockSpec((tile, model), lambda i, f: (i, 0)),
            pl.BlockSpec((tile, width), lambda i, f: (i, f[2])),
            full((1, model)),
            full((NS, width)),
        ],
        [
            ((rows, model), BF16, pl.BlockSpec((tile, model), lambda i, f: (i, 0))),
            ((rows, 1), F32, pl.BlockSpec((tile, 1), lambda i, f: (i, 0)), True),
            (*out_full((tiles, seg, SUB, HD), F32), True),
            (*out_full(state_shape, F32), True),
            out_full((seqs, NS, width), F32),
        ],
        grid=(rows // tile,),
        prefetch=(info,),
        scratch=[pltpu.VMEM((tiles, rows, HD), F32), tab, tab],
        hbm=(2, 3),
    )
    carry_in = carried(final, hop, "seq", True)

    ctx_low, entry = line.run(
        "context",
        functools.partial(context_kernel, seqs, stride),
        (runs, seg_end, carry_in, pack),
        [full((tiles, seg, SUB, HD)), full(state_shape), full((seqs, NS, width)), full((PACKED, width))],
        [out_full((seqs * CTX, width), BF16), (*out_full(state_shape, F32), True)],
        scratch=[tab, tab, tab, pltpu.VMEM((tiles, seqs * CTX, HD), F32)],
        after=wo_parts[2] if tensor_count > 2 else None,
        hbm=(0, 1),
    )
    ctx_parts = gather_parts(ctx_low, "tensor")

    query, key_self, value_self = line.run(
        "qkv",
        qkv_kernel,
        (normed_low, query_weight, key_weight, value_weight),
        [pl.BlockSpec((tile, model), lambda i: (i, 0))] + [full((model, width))] * 3,
        [((rows, width), BF16, pl.BlockSpec((tile, width), lambda i: (i, 0)))] * 3,
        grid=(rows // tile,),
    )

    attended, key_ctx, value_ctx, log_sum, att_parts = [], [], [], [], []
    for s in range(seqs):
        a, kc, vc, ls = line.run(
            "attend",
            functools.partial(attend_kernel, tensor_count, scale),
            (query, key_self, value_self, key_weight, value_weight, *ctx_parts),
            [rows_of(s)] * 3
            + [full((model, width))] * 2
            + [pl.BlockSpec((CTX, width), lambda *a, s=s: (s, 0))] * tensor_count,
            [
                out_full((block, width), BF16),
                out_full((CTX, width), BF16),
                out_full((CTX, width), BF16),
                out_full((block, heads), F32),
            ],
            prefetch=(info,),
        )
        attended.append(a)
        key_ctx.append(kc)
        value_ctx.append(vc)
        log_sum.append(ls)
        att_parts.append(gather_parts(a, "tensor"))

    steps = block // tile
    middle, normed2, act, slope, cot = ([] for _ in range(5))
    for s in range(seqs):

        def at(cols, s=s):
            return pl.BlockSpec((tile, cols), lambda i, f, s=s: (s * steps + i, 0))

        def own(cols):
            return pl.BlockSpec((tile, cols), lambda i, f: (i, 0))

        got = line.run(
            "feed",
            functools.partial(feed_kernel, tensor_count, tile, s),
            (flat_in, flat_grad, gain2, up_weight, *att_parts[s], *wo_parts),
            [at(model), at(model), full((1, model)), full((model, units))]
            + [own(width)] * tensor_count
            + [full((width, model))] * tensor_count,
            [((block, c), t, own(c)) for c, t in ((model, F32), (model, BF16), (units, BF16), (units, BF16), (model, BF16))],
            grid=(steps,),
            prefetch=(info,),
        )
        for slot, value in zip((middle, normed2, act, slope, cot), got):
            slot.append(value)

    box = {}

    def feed_back(s):
        got = line.run(
            "feed_back",
            feed_back_kernel,
            (cot[s], slope[s], up_weight, down_weight),
            [pl.BlockSpec((tile, model), lambda i, f: (i, 0)), pl.BlockSpec((tile, units), lambda i, f: (i, 0)), full((model, units)), full((units, model))],
            [((block, c), BF16, pl.BlockSpec((tile, c), lambda i, f: (i, 0))) for c in (units, half, half)],
            grid=(steps,),
            prefetch=(info,),
        )
        box["pre", s], box["n2_keep", s] = got[:2]
        box["n2_send", s] = swap(got[2], "tensor", 1)

    def near_core(s):
        box["n2_core", s] = add(line, box["n2_keep", s], box["n2_send", s])
        box["n2_y", s] = swap(box["n2_core", s], "tensor", tensor_bits[1])

    def near_y(s):
        total = add(line, box["n2_core", s], box["n2_y", s])
        for bit in tensor_bits[2:]:
            total = add(line, total, swap(total, "tensor", bit))
        box["n2_near", s] = total
        box["n2_far", s] = swap(total, "tensor", 1)

    def attend_back(s):
        outs = [
            ((block, model), BF16), ((block, width), F32), ((1, model), F32),
            ((block, width), BF16), ((block, width), BF16), ((block, width), BF16),
            ((CTX, width), BF16), ((CTX, width), BF16),
            ((pairs, CTX + block, width), BF16), ((pairs, CTX + block, width), BF16),
        ]
        got = line.run(
            "attend_back",
            functools.partial(attend_back_kernel, s, scale),
            (middle[s], box["n2_near", s], box["n2_far", s], flat_grad, gain2, out_weight, query, key_self, value_self, key_ctx[s], value_ctx[s], log_sum[s], query_weight, key_weight, value_weight),
            [full((block, model)), full((block, half)), full((block, half)), pl.BlockSpec((block, model), lambda *a, s=s: (s, 0)), full((1, model)), full((width, model))]
            + [rows_of(s)] * 3
            + [full((CTX, width))] * 2
            + [full((block, heads))]
            + [full((model, width))] * 3,
            [out_full(*o) for o in outs],
            prefetch=(info,),
            scratch=[pltpu.VMEM((block, model), BF16), pltpu.VMEM((block, model), F32)]
            + [pltpu.VMEM((block, HD), F32)] * 2
            + [pltpu.VMEM((CTX, HD), F32)] * 2,
        )

        box["back", s] = got
        box["got", s] = swap(got[9], "tensor", 1)

    def backs(k):
        return [box["back", s][k] for s in range(seqs)]

    def both(key):
        return [box[key, s] for s in range(seqs)]

    def sum_start(key, pieces):
        box[key] = pieces[0], swap(pieces[1], "seq", bits_of[key][0])

    def sum_second(key):
        near, far = add_pair(line, *box[key])
        box[key, "near"], box[key, "z"] = near, swap(far, "seq", bits_of[key][1])

    def sum_third(key):
        total = add(line, box[key, "near"], box[key, "z"])
        for bit in bits_of[key][2:-1]:
            total = add(line, total, swap(total, "seq", bit))
        box[key, "total"] = total
        if len(seq_bits) > 2:
            box[key, "hop"] = swap(total, "seq", bits_of[key][-1])

    def sum_last(key):
        total = box[key, "total"]
        if len(seq_bits) > 2:
            total = add(line, total, box[key, "hop"])
        other = swap(total, "seq", bits_of[key][1])
        back0, back1 = swap(total, "seq", bits_of[key][0]), swap(other, "seq", bits_of[key][0])
        box[key, "pieces"] = [total, other, back0, back1]

    def pin(key, k):
        line.held.append(box[key, "pieces"][k])

    def project(_):
        mid_low, mid_slice, gain2_part, dq, dk, dv, dkc, dvc = (backs(k) for k in range(8))
        ctx_stack = jnp.stack(ctx_parts)
        ins = (normed_low, *mid_low, ctx_stack, *dq, *dk, *dv, *dkc, *dvc, *attended)
        got = (
            line.run(
                "project_grad",
                functools.partial(project_grad_kernel, seqs),
                ins,
                [full(a.shape) for a in ins],
                [out_full((2, model // 4, 4 * width), BF16)] * 2,
                prefetch=(info,),
                )
        )
        sum_start("Q", got)

    def ctx_parts_sum(_):
        box["ctx"] = scatter_parts(add_parts(line, backs(8), both("got"), 0, CTX), "tensor")

    def n1_parts_sum(_):
        box["n1"] = scatter_parts(add_parts(line, backs(8), both("got"), CTX, block), "tensor")

    def lead_step(_):
        ctx_near, ctx_far = box["ctx"]
        ctx_grads, segb_end, lead = line.run(
            "lead",
            functools.partial(lead_kernel, seqs, stride),
            (ctx_near, ctx_far, pack),
            [vmem()] * 3,
            [(*out_full((tiles, seqs * CTX // SUB, SUB, HD), F32), True), (state_shape, F32, vmem()), ((seqs, NS, width), F32, vmem())],
            scratch=[pltpu.VMEM((tiles, seqs * CTX, HD), F32), tab],
        )
        box["lead"] = ctx_grads, segb_end
        box["seen"] = []
        box["carry"] = carried(lead, hop, "seq", False, box["seen"])

    def state_step(_):
        ctx_grads, segb_end = box["lead"]
        carry_back = box["carry"]
        box["state"] = line.run(
            "state_back",
            functools.partial(state_back_kernel, seqs, stride),
            (runs, ctx_grads, entry, segb_end, carry_back, pack),
            [
                full((tiles, seg, SUB, HD)),
                full((tiles, seqs * CTX // SUB, SUB, HD)),
                full(state_shape),
                full(state_shape),
                full((seqs, NS, width)),
                full((PACKED, width)),
            ],
            [out_full((tiles, rows, HD), F32), out_full((small_rows, width), F32)],
            scratch=[
                tab,
                tab,
                pltpu.VMEM((stride, NS, SUB, width), F32),
                tab,
                pltpu.VMEM((seg // stride + 1, NS, SUB, width), F32),
                pltpu.VMEM((tiles, seg, SUB, HD), F32),
                pltpu.VMEM((stride + 2, NS, width), F32),
            ],
            hbm=(0, 1, 2),
        )

    def feed_out(_):
        got = line.run(
            "feed_out",
            functools.partial(feed_out_kernel, seqs, steps),
            (*act, down_weight),
            [pl.BlockSpec((tile, units), lambda i, f, s=s: (jnp.clip(i - s * steps, 0, steps - 1), 0)) for s in range(seqs)]
            + [full((units, model))],
            [((rows, half), BF16, pl.BlockSpec((tile, half), lambda i, f: (i, 0)))] * 2,
            grid=(seqs * steps,),
            prefetch=(info,),
        )
        box["out_keep"], box["out_send"] = got[0], swap(got[1], "tensor", 1)

    def out_core(_):
        total = add(line, box["out_keep"], box["out_send"])
        for bit in tensor_bits[1:-1]:
            total = add(line, total, swap(total, "tensor", bit))
        box["out_core"], box["out_y"] = total, swap(total, "tensor", tensor_bits[-1])

    def out_add(_):
        box["out_near"] = line.run(
            "add_out",
            functools.partial(add_out_kernel, seqs),
            (*middle, box["out_core"], box["out_y"]),
            [full((block, model))] * seqs + [full((rows, half))] * 2,
            [out_full((rows, half), BF16)],
            prefetch=(info,),
        )[0]
        box["out_far"] = swap(box["out_near"], "tensor", 1)

    def join(_):
        box["outputs"] = line.run(
            "join",
            join_kernel,
            (box["out_near"], box["out_far"]),
            [pl.BlockSpec((tile, half), lambda i, f: (i, 0))] * 2,
            [((rows, model), BF16, pl.BlockSpec((tile, model), lambda i, f: (i, 0)))],
            grid=(rows // tile,),
            prefetch=(info,),
        )[0].reshape(seqs, block, model)

    def norm_back(_):
        chan_grad, pack_grad = box["state"]
        h1, small, sums = line.run(
            "norm_back",
            functools.partial(norm_back_kernel, seqs),
            (*box["n1"], chan_grad, in_chan, inverse, pack, pack_grad, *backs(2)),
            [full((rows, width))] * 2
            + [full((tiles, rows, HD)), full((rows, width)), full((rows, 1)), full((PACKED, width)), full((small_rows, width))]
            + [full((1, model))] * seqs,
            [out_full((rows, width), F32), out_full((small_rows, width), F32), out_full((SUB, rows), F32)],
        )
        box["h1"], box["small"] = h1, small
        box["sums"], box["more"] = sums, swap(sums, "tensor", 1)
        box["small_got"] = swap(small, "seq", seq_bits[0])

    def row_sums(_):
        total = add_wide(line, box["sums"], box["more"])
        for bit in tensor_bits[1:-1]:
            total = add_wide(line, total, swap(total, "tensor", bit))
        box["sums"], box["more"] = total, swap(total, "tensor", tensor_bits[-1])

    def input_step(_):
        box["input_grad"] = line.run(
            "input_grad",
            functools.partial(input_grad_kernel, seqs, model),
            (box["h1"], box["sums"], box["more"], in_chan, inverse, *backs(1)),
            [full((rows, width)), full((SUB, rows)), full((SUB, rows)), full((rows, width)), full((rows, 1))]
            + [full((block, width))] * seqs,
            [out_full((rows, width), BF16)],
        )[0]

    def small_step(k):
        total = add_wide(line, box["small"], box["small_got"])
        box["small"] = total
        later = seq_bits[k + 1 :]
        if k == 2:
            for bit in later:
                box["small"] = add_wide(line, box["small"], swap(box["small"], "seq", bit))
        elif later:
            box["small_got"] = swap(total, "seq", later[0])

    def flags_of(key):
        return swapped if KINDS[key] else info

    def widen_step(key):
        box[key, "wide"] = (widen_project if key == "Q" else widen)(line, flags_of(key), box[key, "pieces"])

    in_chan = lax.dynamic_slice_in_dim(flat_in, idx * width, width, 1)
    swapped = jnp.concatenate([info[1::-1], info[2:]])
    bits_of = {key: [second, first, *seq_bits[2:]] if kind else seq_bits for key, kind in KINDS.items()}
    steps_of = {
        "outD": lambda k: sum_start("D", outer(line, flags_of("D"), act, cot)),
        "outU": lambda k: sum_start("U", outer(line, flags_of("U"), normed2, both("pre"))),
        "fb": feed_back, "na": near_core, "ny": near_y, "ab": attend_back, "cp": ctx_parts_sum, "np": n1_parts_sum,
        "pr": project, "ld": lead_step, "st": state_step, "fo": feed_out, "oc": out_core, "oa": out_add, "jn": join,
        "nb": norm_back, "rs": row_sums, "ig": input_step, "e": small_step,
        "s2": sum_second, "s3": sum_third, "s4": sum_last, "wd": widen_step,
        "c": lambda k: line.held.append(box["seen"][k]),
        "p1": lambda k: pin(k, 1), "p2": lambda k: pin(k, 2), "p3": lambda k: pin(k, 3),
    }
    for step, which in ORDER:
        steps_of[step](which)
    outputs, down_grad, up_grad = box["outputs"], box["D", "wide"], box["U", "wide"]
    query_grad, key_grad, value_grad, out_grad_w = box["Q", "wide"]
    input_grad = box["input_grad"].reshape(seqs, block, width)
    small = box["small"]
    return (
        outputs,
        input_grad,
        small[3 * NS + 1],
        query_grad,
        key_grad,
        value_grad,
        out_grad_w,
        small[3 * NS + 2 : 3 * NS + 2 + model // width].reshape(model),
        up_grad,
        down_grad,
        small[:NS],
        small[NS : 2 * NS],
        small[2 * NS : 3 * NS],
        small[3 * NS],
    )


def solution(mesh):
    in_specs = (
        P(None, "seq", None),
        P(None, "seq", None),
        P(),
        P(),
        P(None, "tensor"),
        P(None, "tensor"),
        P(None, "tensor"),
        P("tensor", None),
        P(),
        P(None, "tensor"),
        P("tensor", None),
        P(None, "tensor"),
        P(None, "tensor"),
        P(None, "tensor"),
        P("tensor"),
    )
    out_specs = (
        P(None, "seq", None),
        P(None, "seq", "tensor"),
        P("tensor"),
        P(None, "tensor"),
        P(None, "tensor"),
        P(None, "tensor"),
        P("tensor", None),
        P(),
        P(None, "tensor"),
        P("tensor", None),
        P(None, "tensor"),
        P(None, "tensor"),
        P(None, "tensor"),
        P("tensor"),
    )
    return jax.shard_map(local, mesh=mesh, in_specs=in_specs, out_specs=out_specs, check_vma=False)
```

```python
import functools

import jax
import jax.numpy as jnp
from jax import lax
from jax.experimental import pallas as pl
from jax.experimental.pallas import tpu as pltpu
from jax.sharding import PartitionSpec as P

SEQ, TENSOR = "seq", "tensor"
HD = 128
NS = 16
CTX = 128
SUB = 8
EPS = 1e-06
F32 = jnp.float32
BF16 = jnp.bfloat16
MIB = 1 << 20


def nn(a, b):
    return lax.dot_general(a, b, (((1,), (0,)), ((), ())), preferred_element_type=F32)


def nt(a, b):
    return lax.dot_general(a, b, (((1,), (1,)), ((), ())), preferred_element_type=F32)


def tn(a, b):
    return lax.dot_general(a, b, (((0,), (0,)), ((), ())), preferred_element_type=F32)


def swap(value, axis, bit):
    count = lax.axis_size(axis)
    return lax.ppermute(value, axis, [(i, i ^ bit) for i in range(count)])


def low_bits(count):
    bit, out = 1, []
    while bit < count:
        out.append(bit)
        bit *= 2
    return out


def sds(shape, dtype):
    return jax.ShapeDtypeStruct(shape, dtype)


def vmem():
    return pl.BlockSpec(memory_space=pltpu.VMEM)


def smem():
    return pl.BlockSpec(memory_space=pltpu.SMEM)


class Line:
    def __init__(self):
        self.mark = None
        self.held = []

    def run(self, name, limit, kernel, args, in_specs, outs, grid=None, prefetch=(), scratch=(), after=None, hbm=(), aliases=None):
        args = [pltpu.with_memory_space_constraint(a, pltpu.HBM) if k in hbm else a for k, a in enumerate(args)]
        in_specs = list(in_specs)
        marks = [] if self.mark is None else [pltpu.with_memory_space_constraint(self.mark, pltpu.HBM)]
        others = [t for t in (after, *self.held) if t is not None]
        self.held = []
        count, extra = len(prefetch) + len(args), len(marks) + len(others)

        def body(*refs):
            return kernel(*refs[:count], *refs[count + extra : count + extra + len(outs)], *refs[count + extra + len(outs) + 1 :])

        in_specs += [pl.BlockSpec(memory_space=pltpu.HBM)] * len(marks) + [pl.BlockSpec(memory_space=pl.ANY)] * len(others)
        *got, self.mark = pl.pallas_call(
            body,
            grid_spec=pltpu.PrefetchScalarGridSpec(
                num_scalar_prefetch=len(prefetch),
                grid=grid or (1,),
                in_specs=in_specs,
                out_specs=[o[2] for o in outs] + [pl.BlockSpec(memory_space=pltpu.HBM)],
                scratch_shapes=list(scratch),
            ),
            out_shape=[pltpu.HBM(o[0], o[1]) if len(o) > 3 else sds(o[0], o[1]) for o in outs] + [pltpu.HBM((SUB, HD), F32)],
            compiler_params=pltpu.CompilerParams(vmem_limit_bytes=limit * MIB),
            cost_estimate=pl.CostEstimate(flops=1, bytes_accessed=1, transcendentals=0),
            input_output_aliases=aliases or {},
            name=name,
        )(*prefetch, *args, *marks, *others)
        return got


def full(shape):
    return pl.BlockSpec(shape, lambda *a: (0,) * len(shape))


def out_full(shape, dtype):
    return (shape, dtype, full(shape))


def lanes(tile):
    return slice(tile * HD, (tile + 1) * HD)


def spread(table, rows, factor=None):
    for n in range(NS):
        row = rows[n : n + 1, :]
        if factor is not None:
            row = jnp.exp(row * factor)
        table[n] = jnp.broadcast_to(row, table.shape[1:])


def scan_step(taps, decay_tab, jump_tab, state):
    tiles = len(taps)
    out = []
    for n in range(NS):
        for t in range(tiles):
            decay = decay_tab[n, :, lanes(t)]
            inner = taps[t][0]
            for tap in taps[t][1:]:
                inner = inner * decay + tap
            out.append(state[n * tiles + t] * jump_tab[n, :, lanes(t)] + inner)
    return tuple(out)


def taps_of(runs_ref, group, stride):
    return [[runs_ref[t, group * stride + i] for i in range(stride)] for t in range(runs_ref.shape[0])]


def segment_ends(state, rate, seg, seqs, seg_ref, end_ref, forward):
    per = SUB // seqs
    tiles = rate.shape[1] // HD
    place = lax.rem(lax.broadcasted_iota(jnp.int32, (SUB, HD), 0), per)
    away = ((per - 1 - place if forward else place) * seg).astype(F32)
    for n in range(NS):
        for t in range(tiles):
            now = state[n * tiles + t]
            seg_ref[n, :, lanes(t)] = now
            part = now * jnp.exp(-rate[n : n + 1, lanes(t)] * away)
            for s in range(seqs):
                end_ref[s, n : n + 1, lanes(t)] = jnp.sum(part[s * per : (s + 1) * per], 0, keepdims=True)


def entry_states(entry_ref, carry_ref, seg_ref, hop, seqs, forward):
    per = SUB // seqs
    for n in range(NS):
        step = hop[n : n + 1, :]
        for s in range(seqs):
            now = carry_ref[s, n : n + 1, :]
            for k in range(per):
                q = s * per + (k if forward else per - 1 - k)
                entry_ref[n, q : q + 1, :] = now
                if k < per - 1:
                    now = now * step + seg_ref[n, q : q + 1, :]


def read_state(ref):
    tiles = ref.shape[2] // HD
    return tuple(ref[n, :, lanes(t)] for n in range(NS) for t in range(tiles))


PACKED = 72
CHUNK = 256


def unpack(pack_ref):
    return (*(pack_ref[k * NS : (k + 1) * NS, :] for k in range(4)), pack_ref[4 * NS : 4 * NS + 1, :], pack_ref[4 * NS + 1 : 4 * NS + 2, :])


def enter_kernel(seqs, stride, info_ref, x_ref, xc_ref, gain_ref, rate_ref, low_ref, inv_ref, runs_ref, seg_ref, fin_ref, flat, decay_tab, jump_tab):
    step, width = x_ref.shape
    tiles, seg = runs_ref.shape[:2]
    piece = CHUNK
    gain = gain_ref[...]
    rate = rate_ref[...]

    @pl.when(pl.program_id(0) == 0)
    def _():
        spread(decay_tab, rate, -1.0)
        spread(jump_tab, rate, -float(stride))

    def norm(i, carry):
        at = pl.ds(pl.multiple_of(i * piece, piece), piece)
        x = x_ref[at, :].astype(F32)
        inv = lax.rsqrt(jnp.sum(x * x, -1, keepdims=True) * (1.0 / width) + EPS)
        low_ref[at, :] = (x * inv * gain).astype(BF16)
        inv_ref[at, :] = inv
        to = pl.ds(pl.multiple_of(pl.program_id(0) * step + i * piece, piece), piece)
        for t in range(tiles):
            flat[t, to, :] = xc_ref[at, lanes(t)].astype(F32) * inv
        return carry

    lax.fori_loop(0, step // piece, norm, 0)

    @pl.when(pl.program_id(0) == pl.num_programs(0) - 1)
    def _():
        def group(g, state):
            taps = []
            for t in range(tiles):
                row = [flat[t, pl.ds(g * stride + i, SUB, stride=seg), :] for i in range(stride)]
                for i in range(stride):
                    runs_ref[t, g * stride + i] = row[i]
                taps.append(row)
            return scan_step(taps, decay_tab, jump_tab, state)

        state = lax.fori_loop(0, seg // stride, group, (jnp.zeros((SUB, HD), F32),) * (NS * tiles))
        segment_ends(state, rate, seg, seqs, seg_ref, fin_ref, True)


def context_kernel(seqs, stride, runs_ref, seg_ref, carry_ref, pack_ref, ctx_ref, entry_ref, decay_tab, jump_tab, out_tab, flat):
    tiles, seg = runs_ref.shape[:2]
    rate, root, s_in, s_out, skip, gain = unpack(pack_ref)
    spread(decay_tab, rate, -1.0)
    spread(jump_tab, rate, -float(stride))
    spread(out_tab, root * s_in * s_out * gain)
    entry_states(entry_ref, carry_ref, seg_ref, jnp.exp(rate * (-float(seg))), seqs, True)
    skip = skip * gain
    groups = seg // stride

    def group(g, state):
        taps = taps_of(runs_ref, g, stride)
        state = scan_step(taps, decay_tab, jump_tab, state)
        for t in range(tiles):
            total = skip[:, lanes(t)] * taps[t][-1]
            for n in range(NS):
                total = total + out_tab[n, :, lanes(t)] * state[n * tiles + t]
            flat[t, pl.ds(g, SUB, stride=groups), :] = total
        return state

    lax.fori_loop(0, groups, group, read_state(entry_ref))
    for t in range(tiles):
        ctx_ref[:, lanes(t)] = flat[t].astype(BF16)


def lead_kernel(seqs, stride, near_ref, far_ref, pack_ref, grads_ref, segb_ref, lead_ref, flat, jump_tab):
    tiles, groups = grads_ref.shape[:2]
    for t in range(tiles):
        flat[t] = near_ref[:, lanes(t)].astype(F32) + far_ref[:, lanes(t)].astype(F32)
    rate = unpack(pack_ref)[0]
    spread(jump_tab, rate, -float(stride))

    def group(i, state):
        g = groups - 1 - i
        grads = [flat[t, pl.ds(g, SUB, stride=groups), :] for t in range(tiles)]
        for t in range(tiles):
            grads_ref[t, g] = grads[t]
        return tuple(state[n * tiles + t] * jump_tab[n, :, lanes(t)] + grads[t] for n in range(NS) for t in range(tiles))

    state = lax.fori_loop(0, groups, group, (jnp.zeros((SUB, HD), F32),) * (NS * tiles))
    segment_ends(state, rate, groups * stride, seqs, segb_ref, lead_ref, False)


def state_back_kernel(
    seqs, stride, runs_ref, grads_ref, entry_ref, segb_ref, carryb_ref, pack_ref, back_ref, packg_ref,
    decay_tab, jump_tab, tap_tab, entryb, states, backs, sums,
):
    tiles, seg = runs_ref.shape[:2]
    groups = seg // stride
    rate, root, s_in, s_out, skip, gain = unpack(pack_ref)
    coeff = root * s_in
    spread(decay_tab, rate, -1.0)
    spread(jump_tab, rate, -float(stride))
    both = coeff * s_out
    for i in range(stride):
        spread(tap_tab.at[i], both * jnp.exp(rate * (-float(stride - 1 - i))))
    entry_states(entryb, carryb_ref, segb_ref, jnp.exp(rate * (-float(seg))), seqs, False)
    zero = jnp.zeros((SUB, HD), F32)

    def forward(g, carry):
        state, totals = carry
        for n in range(NS):
            for t in range(tiles):
                states[g, n, :, lanes(t)] = state[n * tiles + t]
        taps = taps_of(runs_ref, g, stride)
        out = []
        for t in range(tiles):
            grad = grads_ref[t, g]
            out.append(totals[t] + grad * taps[t][-1])
            backs[t, g * stride + stride - 1] = grad * skip[:, lanes(t)]
            for i in range(stride - 1):
                backs[t, g * stride + i] = zero
        return scan_step(taps, decay_tab, jump_tab, state), tuple(out)

    last, totals = lax.fori_loop(0, groups, forward, (read_state(entry_ref), (zero,) * tiles))
    for n in range(NS):
        for t in range(tiles):
            states[groups, n, :, lanes(t)] = last[n * tiles + t]
    for t in range(tiles):
        packg_ref[3 * NS : 3 * NS + 1, lanes(t)] = jnp.sum(totals[t], 0, keepdims=True) * gain[:, lanes(t)]
    lot = 2
    kinds = stride + 2
    for t in range(tiles):
        for first in range(0, NS, lot):
            names = range(first, first + lot)

            def group(i, carry, t=t, names=names):
                g = groups - 1 - i
                adj, acc = carry
                grad = grads_ref[t, g]
                taps = [runs_ref[t, g * stride + i] for i in range(stride)]
                sums_b = [backs[t, g * stride + i] for i in range(stride)]
                new_adj, new_acc = [], []
                for k, n in enumerate(names):
                    now = adj[k] * jump_tab[n, :, lanes(t)] + grad
                    new_adj.append(now)
                    for i in range(stride):
                        sums_b[i] = sums_b[i] + tap_tab[i, n, :, lanes(t)] * now
                        new_acc.append(acc[k * kinds + i] + now * taps[i])
                    new_acc.append(acc[k * kinds + stride] + now * states[g, n, :, lanes(t)])
                    new_acc.append(acc[k * kinds + stride + 1] + grad * states[g + 1, n, :, lanes(t)])
                for i in range(stride):
                    backs[t, g * stride + i] = sums_b[i]
                return tuple(new_adj), tuple(new_acc)

            start = (tuple(entryb[n, :, lanes(t)] for n in names), (zero,) * (lot * kinds))
            _, acc = lax.fori_loop(0, groups, group, start, unroll=4)
            for k, n in enumerate(names):
                for j in range(kinds):
                    sums[j, n : n + 1, lanes(t)] = jnp.sum(acc[k * kinds + j], 0, keepdims=True)

    def spill(g, carry):
        for t in range(tiles):
            for i in range(stride):
                back_ref[t, pl.ds(g * stride + i, SUB, stride=seg), :] = backs[t, g * stride + i]
        return carry

    lax.fori_loop(0, groups, spill, 0)
    decay = jnp.exp(-rate)
    powers = [jnp.ones_like(rate)]
    for _ in range(stride):
        powers.append(powers[-1] * decay)
    coeff_grad = sum(powers[stride - 1 - i] * sums[i] for i in range(stride)) * s_out * gain
    decay_grad = float(stride) * powers[stride - 1] * sums[stride]
    for i in range(stride - 1):
        decay_grad = decay_grad + float(stride - 1 - i) * powers[stride - 2 - i] * sums[i]
    decay_grad = decay_grad * coeff * s_out * gain
    packg_ref[:NS, :] = coeff_grad * s_in * (decay * decay / root) - decay * decay_grad
    packg_ref[NS : 2 * NS, :] = coeff_grad * root
    packg_ref[2 * NS : 3 * NS, :] = coeff * gain * sums[stride + 1]


def carried(value, hop, axis, forward, seen=None):
    count = lax.axis_size(axis)
    mine = lax.axis_index(axis)
    whole = value
    enter = jnp.zeros_like(value)
    for bit in low_bits(count):
        other = swap(whole, axis, bit)
        if seen is not None:
            seen.append(other)
        upper = (mine & bit) != 0
        offset = mine & (bit - 1)
        if not forward:
            upper = jnp.logical_not(upper)
            offset = bit - 1 - offset
        enter = jnp.where(upper, enter + hop(offset) * other, enter)
        span = hop(bit)
        whole = jnp.where(upper, whole + span * other, other + span * whole)
    return enter


def qkv_kernel(x_ref, wq_ref, wk_ref, wv_ref, q_ref, k_ref, v_ref):
    x = x_ref[...]
    q_ref[...] = nn(x, wq_ref[...]).astype(BF16)
    k_ref[...] = nn(x, wk_ref[...]).astype(BF16)
    v_ref[...] = nn(x, wv_ref[...]).astype(BF16)


def masks(first, tile, block, stride):
    row = lax.broadcasted_iota(jnp.int32, (tile, CTX), 0) + first
    col = lax.broadcasted_iota(jnp.int32, (tile, CTX), 1)
    side = stride * col + (stride - 1) <= row
    row = lax.broadcasted_iota(jnp.int32, (tile, block), 0) + first
    col = lax.broadcasted_iota(jnp.int32, (tile, block), 1)
    return side, col <= row


def attend_kernel(parts, scale, idx_ref, q_ref, k_ref, v_ref, wk_ref, wv_ref, *rest):
    ctx_refs, (out_ref, kc_ref, vc_ref, lse_ref) = rest[:parts], rest[parts:]
    block, width = q_ref.shape
    stride = block // CTX
    idx = idx_ref[2]
    key_c = jnp.zeros((CTX, width), F32)
    val_c = jnp.zeros((CTX, width), F32)
    for p in range(parts):
        at = pl.ds(pl.multiple_of((idx ^ p) * width, width), width)
        key_c = key_c + nn(ctx_refs[p][...], wk_ref[at, :])
        val_c = val_c + nn(ctx_refs[p][...], wv_ref[at, :])
    kc_ref[...] = key_c.astype(BF16)
    vc_ref[...] = val_c.astype(BF16)
    tile = min(256, block)
    for h in range(width // HD):
        cols = slice(h * HD, (h + 1) * HD)
        for first in range(0, block, tile):
            seen = first + tile
            rows = slice(first, seen)
            q = q_ref[rows, cols]
            side_ok, own_ok = masks(first, tile, seen, stride)
            side = jnp.where(side_ok, nt(q, kc_ref[:, cols]), -1e30)
            own = jnp.where(own_ok, nt(q, k_ref[:seen, cols]), -1e30)
            top = jnp.maximum(jnp.max(side, -1, keepdims=True), jnp.max(own, -1, keepdims=True))
            side = jnp.exp((side - top) * scale)
            own = jnp.exp((own - top) * scale)
            total = jnp.sum(side, -1, keepdims=True) + jnp.sum(own, -1, keepdims=True)
            share = 1.0 / total
            got = nn((side * share).astype(BF16), vc_ref[:, cols]) + nn((own * share).astype(BF16), v_ref[:seen, cols])
            out_ref[rows, cols] = got.astype(BF16)
            lse_ref[rows, h : h + 1] = top * scale + jnp.log(total)


def attend_back_kernel(
    seq, scale, info_ref, mid_ref, near_ref, far_ref, grad_ref, gain_ref, wo_ref, q_ref, k_ref, v_ref, kc_ref, vc_ref, lse_ref,
    wq_ref, wk_ref, wv_ref,
    low_ref, slice_ref, gaing_ref, dq_ref, dk_ref, dv_ref, dkc_ref, dvc_ref, keep_ref, send_ref,
    n2_ref, full_ref, key_acc, val_acc, skey_acc, sval_acc,
):
    block, width = q_ref.shape
    model = mid_ref.shape[1]
    half = model // 2
    stride = block // CTX
    idx, mine, limit = info_ref[2], info_ref[3], info_ref[4 + seq]
    n2_ref[:, pl.ds(pl.multiple_of(mine * half, half), half)] = near_ref[...]
    n2_ref[:, pl.ds(pl.multiple_of((1 - mine) * half, half), half)] = far_ref[...]
    gain = gain_ref[...]
    step = CHUNK

    def norm(i, total):
        at = pl.ds(pl.multiple_of(i * step, step), step)
        mid = mid_ref[at, :]
        inv = lax.rsqrt(jnp.sum(mid * mid, -1, keepdims=True) * (1.0 / model) + EPS)
        hat = mid * inv
        n2 = n2_ref[at, :].astype(F32)
        prod = n2 * hat
        h2 = n2 * gain
        mean = jnp.sum(h2 * hat, -1, keepdims=True) * (1.0 / model)
        place = lax.broadcasted_iota(jnp.int32, (step, 1), 0) + i * step
        cot = jnp.where(place < limit, grad_ref[at, :].astype(F32), 0.0)
        grad = cot + inv * (h2 - hat * mean)
        full_ref[at, :] = grad
        low_ref[at, :] = grad.astype(BF16)
        return total + jnp.sum(prod, 0, keepdims=True)

    gaing_ref[...] = lax.fori_loop(0, block // step, norm, jnp.zeros((1, model), F32))
    slice_ref[...] = full_ref[:, pl.ds(pl.multiple_of(idx * width, width), width)]
    att_grad = nt(low_ref[...], wo_ref[...]).astype(BF16)
    tile = min(512, block)
    for h in range(width // HD):
        cols = slice(h * HD, (h + 1) * HD)
        for first in range(0, block, tile):
            seen = first + tile
            rows = slice(first, seen)
            q = q_ref[rows, cols]
            grad = att_grad[rows, cols]
            lse = lse_ref[rows, h : h + 1]
            side_ok, own_ok = masks(first, tile, seen, stride)
            kc, k = kc_ref[:, cols], k_ref[:seen, cols]
            side = jnp.exp(jnp.where(side_ok, nt(q, kc) * scale - lse, -1e30))
            own = jnp.exp(jnp.where(own_ok, nt(q, k) * scale - lse, -1e30))
            dside = nt(grad, vc_ref[:, cols])
            down = nt(grad, v_ref[:seen, cols])
            term = jnp.sum(side * dside, -1, keepdims=True) + jnp.sum(own * down, -1, keepdims=True)
            dside = (side * (dside - term)).astype(BF16)
            down = (own * (down - term)).astype(BF16)
            dq_ref[rows, cols] = ((nn(dside, kc) + nn(down, k)) * scale).astype(BF16)
            side = side.astype(BF16)
            own = own.astype(BF16)
            last = first + tile >= block
            fresh = first == 0
            for acc, score, right in (
                (skey_acc, dside, q),
                (sval_acc, side, grad),
            ):
                got = tn(score, right)
                acc[...] = got if fresh else acc[...] + got
            for acc, score, right in (
                (key_acc, down, q),
                (val_acc, own, grad),
            ):
                got = tn(score, right)
                if fresh:
                    acc[:seen, :] = got
                else:
                    acc[:first, :] = acc[:first, :] + got[:first]
                    acc[first:seen, :] = got[first:]
            if last:
                dk_ref[:, cols] = (key_acc[...] * scale).astype(BF16)
                dv_ref[:, cols] = val_acc[...].astype(BF16)
                dkc_ref[:, cols] = (skey_acc[...] * scale).astype(BF16)
                dvc_ref[:, cols] = sval_acc[...].astype(BF16)
    count = model // width
    for p in range(count):
        at = pl.ds(pl.multiple_of((idx ^ p) * width, width), width)
        wk, wv = wk_ref[at, :], wv_ref[at, :]
        ctx = nt(dkc_ref[...], wk) + nt(dvc_ref[...], wv)
        (send_ref if p % 2 else keep_ref)[p // 2, :CTX, :] = ctx.astype(BF16)
    for p in range(count):
        at = pl.ds(pl.multiple_of((idx ^ p) * width, width), width)
        own = nt(dq_ref[...], wq_ref[at, :]) + nt(dk_ref[...], wk_ref[at, :]) + nt(dv_ref[...], wv_ref[at, :])
        (send_ref if p % 2 else keep_ref)[p // 2, CTX:, :] = own.astype(BF16)


def feed_kernel(parts, tile, seq, info_ref, x_ref, grad_ref, gain_ref, up_ref, *rest):
    att_refs, wo_refs = rest[:parts], rest[parts : 2 * parts]
    mid_ref, n2_ref, act_ref, slope_ref, cot_ref = rest[2 * parts :]
    model = x_ref.shape[1]
    limit = info_ref[4 + seq]
    mid = x_ref[...].astype(F32)
    got = nn(att_refs[0][...], wo_refs[0][...])
    for p in range(1, parts):
        got = got + nn(att_refs[p][...], wo_refs[p][...])
    mid = mid + got
    mid_ref[...] = mid
    inv = lax.rsqrt(jnp.sum(mid * mid, -1, keepdims=True) * (1.0 / model) + EPS)
    n2_ref[...] = (mid * inv * gain_ref[...]).astype(BF16)
    place = lax.broadcasted_iota(jnp.int32, (tile, 1), 0) + pl.program_id(0) * tile
    cot_ref[...] = jnp.where(place < limit, grad_ref[...].astype(F32), 0.0).astype(BF16)
    pre = nn(n2_ref[...], up_ref[...])
    cdf = 0.5 * (1.0 + lax.erf(pre * 0.7071067811865476))
    pdf = jnp.exp(pre * pre * -0.5) * 0.3989422804014327
    act_ref[...] = (pre * cdf).astype(BF16)
    slope_ref[...] = (cdf + pre * pdf).astype(BF16)


def halves(info_ref, half):
    mine = info_ref[3]
    return (
        pl.ds(pl.multiple_of(mine * half, half), half),
        pl.ds(pl.multiple_of((1 - mine) * half, half), half),
    )


def feed_back_kernel(info_ref, cot_ref, slope_ref, up_ref, down_ref, pre_ref, keep_ref, send_ref):
    near, far = halves(info_ref, keep_ref.shape[1])
    pull = nt(cot_ref[...], down_ref[...])
    pre_ref[...] = (pull * slope_ref[...].astype(F32)).astype(BF16)
    send_ref[...] = nt(pre_ref[...], up_ref[far, :]).astype(BF16)
    keep_ref[...] = nt(pre_ref[...], up_ref[near, :]).astype(BF16)


def feed_out_kernel(seqs, steps, info_ref, *refs):
    down_ref, keep_ref, send_ref = refs[seqs:]
    near, far = halves(info_ref, keep_ref.shape[1])
    for s in range(seqs):

        @pl.when(pl.program_id(0) // steps == s)
        def _(s=s):
            send_ref[...] = nn(refs[s][...], down_ref[:, far]).astype(BF16)
            keep_ref[...] = nn(refs[s][...], down_ref[:, near]).astype(BF16)


def add_kernel(a_ref, b_ref, out_ref):
    out_ref[...] = (a_ref[...].astype(F32) + b_ref[...].astype(F32)).astype(BF16)


def add_pair_kernel(a_ref, b_ref, out0_ref, out1_ref):
    out0_ref[...] = (a_ref[0].astype(F32) + b_ref[0].astype(F32)).astype(BF16)
    out1_ref[...] = (a_ref[1].astype(F32) + b_ref[1].astype(F32)).astype(BF16)


def add_parts_kernel(pairs, count, start, size, *refs):
    keeps, gots, outs = refs[:count], refs[count : 2 * count], refs[2 * count :]
    at = slice(start, start + size)
    for m in range(pairs):
        for s in range(count):
            outs[m][s * size : (s + 1) * size, :] = (keeps[s][m, at].astype(F32) + gots[s][m, at].astype(F32)).astype(BF16)


def add_out_kernel(seqs, info_ref, *refs):
    mids, (a_ref, b_ref, out_ref) = refs[:seqs], refs[seqs:]
    near, _ = halves(info_ref, out_ref.shape[1])
    block = mids[0].shape[0]
    for s in range(seqs):
        at = slice(s * block, (s + 1) * block)
        total = a_ref[at, :].astype(F32) + b_ref[at, :].astype(F32)
        out_ref[at, :] = (mids[s][:, near] + total).astype(BF16)


def join_kernel(info_ref, near_ref, far_ref, out_ref):
    near, far = halves(info_ref, near_ref.shape[1])
    out_ref[:, near] = near_ref[...]
    out_ref[:, far] = far_ref[...]


def high(a, b, dims):
    return lax.dot_general(a, b, (dims, ((), ())), precision=lax.Precision.HIGHEST, preferred_element_type=F32)


def norm_back_kernel(seqs, near_ref, far_ref, back_ref, x_ref, inv_ref, pack_ref, packg_ref, *refs):
    gains, (h1_ref, small_ref, sums_ref) = refs[:seqs], refs[seqs:]
    tiles, rows = back_ref.shape[:2]
    width = tiles * HD
    gain = unpack(pack_ref)[5]
    step = 128
    ones = jnp.ones((SUB, HD), F32)

    def part(i, total):
        at = pl.ds(pl.multiple_of(i * step, step), step)
        inv = inv_ref[at, :]
        sums, out = 0.0, []
        for t in range(tiles):
            n1 = near_ref[at, lanes(t)].astype(F32) + far_ref[at, lanes(t)].astype(F32) + back_ref[t, at, :]
            hat = x_ref[at, lanes(t)].astype(F32) * inv
            prod = n1 * hat
            h1 = n1 * gain[:, lanes(t)]
            h1_ref[at, lanes(t)] = h1
            out.append(total[t] + jnp.sum(prod, 0, keepdims=True))
            sums = sums + h1 * hat
        sums_ref[:, at] = high(ones, sums, ((1,), (1,)))
        return tuple(out)

    total = lax.fori_loop(0, rows // step, part, (jnp.zeros((1, HD), F32),) * tiles)
    small_ref[...] = jnp.zeros(small_ref.shape, F32)
    small_ref[: 3 * NS + 1, :] = packg_ref[: 3 * NS + 1, :]
    for t in range(tiles):
        small_ref[3 * NS + 1 : 3 * NS + 2, lanes(t)] = total[t]
    gain2 = gains[0][...]
    for s in range(1, seqs):
        gain2 = gain2 + gains[s][...]
    for k in range(gain2.shape[1] // width):
        small_ref[3 * NS + 2 + k : 3 * NS + 3 + k, :] = gain2[:, k * width : (k + 1) * width]


def add_wide_kernel(a_ref, b_ref, out_ref):
    out_ref[...] = a_ref[...] + b_ref[...]


def add_wide(line, a, b):
    return line.run("add", 4, add_wide_kernel, (a, b), [full(a.shape)] * 2, [out_full(a.shape, F32)])[0]


def input_grad_kernel(seqs, model, h1_ref, sums_ref, more_ref, x_ref, inv_ref, *refs):
    mids, out_ref = refs[:seqs], refs[seqs]
    block, width = mids[0].shape
    step = 128
    ones = jnp.full((SUB, HD), 1.0 / (SUB * model), F32)
    for s in range(seqs):

        def part(i, carry, s=s):
            at = pl.ds(pl.multiple_of(s * block + i * step, step), step)
            here = pl.ds(pl.multiple_of(i * step, step), step)
            inv = inv_ref[at, :]
            mean = high(sums_ref[:, at] + more_ref[:, at], ones, ((0,), (0,)))
            for t in range(width // HD):
                hat = x_ref[at, lanes(t)].astype(F32) * inv
                grad = mids[s][here, lanes(t)] + inv * (h1_ref[at, lanes(t)] - hat * mean)
                out_ref[at, lanes(t)] = grad.astype(BF16)
            return carry

        lax.fori_loop(0, block // step, part, 0)


def add_pair(line, a, b):
    return line.run("add_pair", 8, add_pair_kernel, (a, b), [full(a.shape)] * 2, [out_full(a.shape[1:], BF16)] * 2)


def add_parts(line, keeps, gots, start, size):
    pairs, _, width = keeps[0].shape
    count = len(keeps)
    return line.run(
        "add_parts", 12,
        functools.partial(add_parts_kernel, pairs, count, start, size),
        (*keeps, *gots),
        [full(keeps[0].shape)] * (2 * count),
        [out_full((count * size, width), BF16)] * pairs,
    )


def add(line, a, b):
    return line.run("add", 8, add_kernel, (a, b), [full(a.shape)] * 2, [out_full(a.shape, BF16)])[0]


def quarter(info, far, step):
    return (info[0] ^ far) * 2 + (info[1] ^ step)


PIECES = ((0, 0), (0, 1), (1, 0), (1, 1))


def outer_kernel(pairs, info_ref, *refs):
    piece = refs[0].shape[1] // 4
    for far, step in PIECES:
        out_ref = refs[2 * pairs + far].at[step]
        at = pl.ds(pl.multiple_of(quarter(info_ref, far, step) * piece, piece), piece)
        total = tn(refs[0][:, at], refs[pairs][...])
        for p in range(1, pairs):
            total = total + tn(refs[p][:, at], refs[pairs + p][...])
        out_ref[...] = total.astype(BF16)


def outer(line, info, lefts, rights):
    rows, cols = lefts[0].shape[1], rights[0].shape[1]
    return line.run(
        "outer", 20,
        functools.partial(outer_kernel, len(lefts)),
        [*lefts, *rights],
        [full(a.shape) for a in (*lefts, *rights)],
        [out_full((2, rows // 4, cols), BF16)] * 2,
        prefetch=(info,),
    )


def project_grad_kernel(seqs, info_ref, *refs):
    refs = list(refs)

    def take(count):
        got = refs[:count]
        del refs[:count]
        return got

    (low_ref,) = take(1)
    mids = take(seqs)
    (ctx_ref,) = take(1)
    dqs, dks, dvs, dkcs, dvcs, atts = (take(seqs) for _ in range(6))
    block, width = dqs[0].shape
    quart = low_ref.shape[1] // 4 // width
    for far, step in PIECES:
        out_ref = refs[far].at[step]
        for i in range(quart):
            part = quarter(info_ref, far, step) * quart + i
            at = pl.ds(pl.multiple_of(part * width, width), width)
            rows = slice(i * width, (i + 1) * width)
            for k, (grads, more) in enumerate(((dqs, None), (dks, dkcs), (dvs, dvcs))):
                total = 0.0
                for s in range(seqs):
                    total = total + tn(low_ref[s * block : (s + 1) * block, at], grads[s][...])
                    if more is not None:
                        total = total + tn(ctx_ref[part ^ info_ref[2], s * CTX : (s + 1) * CTX, :], more[s][...])
                out_ref[rows, k * width : (k + 1) * width] = total.astype(BF16)
            total = 0.0
            for s in range(seqs):
                total = total + tn(atts[s][...], mids[s][:, at])
            out_ref[rows, 3 * width :] = total.astype(BF16)


def order(p, f):
    return quarter(f, p // 2, p % 2)


def widen_kernel(flags_ref, *refs):
    out_ref = refs[-1]
    for p in range(4):

        @pl.when(pl.program_id(0) == p)
        def _(p=p):
            start = 0
            for ref in refs[p : p + 1] if p < 3 else refs[3:-1]:
                size = ref.shape[0]
                out_ref[start : start + size, :] = ref[...].astype(F32)
                start += size


def widen(line, info, pieces):
    piece, cols = pieces[0].shape
    return line.run(
        "widen", 10,
        widen_kernel,
        pieces,
        [full(p.shape) for p in pieces],
        [((4 * piece, cols), F32, pl.BlockSpec((piece, cols), lambda p, f: (order(p, f), 0)))],
        grid=(4,),
        prefetch=(info,),
    )[0]


def widen_project_kernel(first, count, parts, flags_ref, *refs):
    pieces, outs = refs[:parts], refs[-4:]
    width = pieces[0].shape[1] // 4
    for p in range(count):

        @pl.when(pl.program_id(0) == p)
        def _(p=p):
            start = 0
            for ref in pieces[p : p + 1] if first + p < 3 else pieces[p:]:
                size = ref.shape[0]
                for k in range(3):
                    outs[k][start : start + size, :] = ref[:, k * width : (k + 1) * width].astype(F32)
                step = min(size, width)
                for j in range(0, size, step):
                    row = (start + j) % width
                    to = (start + j) // width * width
                    outs[3][row : row + step, to : to + width] = ref[j : j + step, 3 * width :].astype(F32)
                start += size


def widen_project(line, info, pieces, first, count, before=None):
    rows = pieces[0].shape[0] if first == 0 else sum(p.shape[0] for p in pieces)
    cols = pieces[0].shape[1]
    width = cols // 4
    given = pieces[first : first + count] if first == 0 else pieces
    before = before or []
    return line.run(
        "widen_project", 10,
        functools.partial(widen_project_kernel, first, count, len(given)),
        [*given, *before],
        [full(p.shape) for p in given] + [pl.BlockSpec(memory_space=pl.ANY)] * len(before),
        [((4 * rows, width), F32, pl.BlockSpec((rows, width), lambda p, f: (order(p + first, f), 0)))] * 3
        + [((width, 4 * rows), F32, pl.BlockSpec((width, rows), lambda p, f: (0, order(p + first, f))))],
        grid=(count,),
        prefetch=(info,),
        aliases={1 + len(given) + k: k for k in range(len(before))},
    )


def gather_parts(value, axis):
    parts = [value]
    for bit in reversed(low_bits(lax.axis_size(axis))):
        parts = parts + [None] * 0 + [swap(p, axis, bit) for p in parts]
    count = len(parts)
    order = [0]
    for bit in reversed(low_bits(count)):
        order = order + [k ^ bit for k in order]
    out = [None] * count
    for k, p in zip(order, parts):
        out[k] = p
    return out


def add_low(a, b):
    return (a.astype(F32) + b.astype(F32)).astype(BF16)


def scatter_parts(parts, axis):
    bits = low_bits(lax.axis_size(axis))[1:]
    for bit in bits:
        keep, send = parts[0::2], parts[1::2]
        got = [swap(p, axis, bit) for p in send]
        if bit != bits[-1]:
            parts = [add_low(a, b) for a, b in zip(keep, got)]
    return keep[0], got[0]


(
    AT_PRE, AT_N2_KEEP, AT_N2_SEND, AT_N2_CORE, AT_N2_Y, AT_N2_NEAR, AT_N2_FAR, AT_BACK, AT_GOT, AT_NEAR, AT_Z,
    AT_TOTAL, AT_HOP, AT_QUARTERS, AT_CTX, AT_N1, AT_LEAD, AT_SEEN, AT_CARRY, AT_STATE, AT_OUT_KEEP, AT_OUT_SEND,
    AT_OUT_CORE, AT_OUT_Y, AT_OUT_NEAR, AT_OUT_FAR, AT_OUTPUTS, AT_H1, AT_SMALL, AT_SUMS, AT_MORE, AT_SMALL_GOT,
    AT_INPUT_GRAD, AT_WIDE, DOWN, UP, QUERY, AT_CTX_STACK, VALUE,
) = range(39)
KINDS = {DOWN: 2, UP: 0, QUERY: 4}


def local(
    inputs, out_grad, lengths, norm_gain, query_weight, key_weight, value_weight, out_weight,
    mlp_gain, up_weight, down_weight, decay_rate, state_input, state_output, skip_gain,
):
    seqs, block, model = inputs.shape
    width = query_weight.shape[1]
    units = up_weight.shape[1]
    heads = width // HD
    tiles = width // HD
    stride = block // CTX
    scale = HD ** (-0.5)
    tensor_count = lax.axis_size(TENSOR)
    tensor_bits = low_bits(tensor_count)
    idx = lax.axis_index(TENSOR)
    place = lax.axis_index(SEQ)
    rows = seqs * block
    seg = rows // SUB
    half = model // 2
    pairs = tensor_count // 2
    small_rows = (3 * NS + 2 + tensor_count + 7) // 8 * 8
    seq_bits = low_bits(lax.axis_size(SEQ))
    first, second = seq_bits[:2]
    line = Line()
    info = jnp.concatenate(
        [
            jnp.stack([(place & first) // first, (place & second) // second, idx, idx & 1]).astype(jnp.int32),
            (lengths - place * block).astype(jnp.int32),
        ]
    )

    flat_in = inputs.reshape(rows, model)
    flat_grad = out_grad.reshape(rows, model)
    gain_all = norm_gain.reshape(1, model)
    gain2 = mlp_gain.reshape(1, model)
    gain_chan = lax.dynamic_slice_in_dim(norm_gain, idx * width, width, 0)
    gain_row = gain_chan.reshape(1, width)
    pack = jnp.concatenate(
        [
            decay_rate,
            jnp.sqrt(-jnp.expm1(-2.0 * decay_rate)),
            state_input,
            state_output,
            skip_gain.reshape(1, width),
            gain_row,
            jnp.zeros((PACKED - 4 * NS - 2, width), F32),
        ]
    )
    tab = pltpu.VMEM((NS, SUB, width), F32)
    state_shape = (NS, SUB, width)

    def hop(blocks):
        return jnp.exp(-decay_rate * (jnp.asarray(blocks, F32) * block))[None]

    def rows_of(s):
        return pl.BlockSpec((block, width), lambda *a, s=s: (s, 0))

    wo_parts = gather_parts(out_weight, TENSOR)

    tile = 256
    normed_low, inverse, runs, seg_end, final = line.run(
        "enter", 10,
        functools.partial(enter_kernel, seqs, stride),
        (flat_in, flat_in, gain_all, decay_rate),
        [
            pl.BlockSpec((tile, model), lambda i, f: (i, 0)),
            pl.BlockSpec((tile, width), lambda i, f: (i, f[2])),
            full((1, model)),
            full((NS, width)),
        ],
        [
            ((rows, model), BF16, pl.BlockSpec((tile, model), lambda i, f: (i, 0))),
            ((rows, 1), F32, pl.BlockSpec((tile, 1), lambda i, f: (i, 0)), True),
            (*out_full((tiles, seg, SUB, HD), F32), True),
            (*out_full(state_shape, F32), True),
            out_full((seqs, NS, width), F32),
        ],
        grid=(rows // tile,),
        prefetch=(info,),
        scratch=[pltpu.VMEM((tiles, rows, HD), F32), tab, tab],
        hbm=(2, 3),
    )
    carry_in = carried(final, hop, SEQ, True)

    ctx_low, entry = line.run(
        "context", 6,
        functools.partial(context_kernel, seqs, stride),
        (runs, seg_end, carry_in, pack),
        [full((tiles, seg, SUB, HD)), full(state_shape), full((seqs, NS, width)), full((PACKED, width))],
        [out_full((seqs * CTX, width), BF16), (*out_full(state_shape, F32), True)],
        scratch=[tab, tab, tab, pltpu.VMEM((tiles, seqs * CTX, HD), F32)],
        hbm=(0, 1),
    )
    ctx_parts = gather_parts(ctx_low, TENSOR)

    query, key_self, value_self = line.run(
        "qkv", 10,
        qkv_kernel,
        (normed_low, query_weight, key_weight, value_weight),
        [pl.BlockSpec((tile, model), lambda i: (i, 0))] + [full((model, width))] * 3,
        [((rows, width), BF16, pl.BlockSpec((tile, width), lambda i: (i, 0)))] * 3,
        grid=(rows // tile,),
        after=wo_parts[2] if tensor_count > 2 else None,
    )

    attended, key_ctx, value_ctx, log_sum, att_parts = [], [], [], [], []
    for s in range(seqs):
        a, kc, vc, ls = line.run(
            "attend", 12,
            functools.partial(attend_kernel, tensor_count, scale),
            (query, key_self, value_self, key_weight, value_weight, *ctx_parts),
            [rows_of(s)] * 3
            + [full((model, width))] * 2
            + [pl.BlockSpec((CTX, width), lambda *a, s=s: (s, 0))] * tensor_count,
            [
                out_full((block, width), BF16),
                out_full((CTX, width), BF16),
                out_full((CTX, width), BF16),
                out_full((block, heads), F32),
            ],
            prefetch=(info,),
        )
        attended.append(a)
        key_ctx.append(kc)
        value_ctx.append(vc)
        log_sum.append(ls)
        att_parts.append(gather_parts(a, TENSOR))

    steps = block // tile
    middle, normed2, act, slope, cot = ([] for _ in range(5))
    for s in range(seqs):

        def at(cols, s=s):
            return pl.BlockSpec((tile, cols), lambda i, f, s=s: (s * steps + i, 0))

        def own(cols):
            return pl.BlockSpec((tile, cols), lambda i, f: (i, 0))

        got = line.run(
            "feed", 30,
            functools.partial(feed_kernel, tensor_count, tile, s),
            (flat_in, flat_grad, gain2, up_weight, *att_parts[s], *wo_parts),
            [at(model), at(model), full((1, model)), full((model, units))]
            + [own(width)] * tensor_count
            + [full((width, model))] * tensor_count,
            [((block, c), t, own(c)) for c, t in ((model, F32), (model, BF16), (units, BF16), (units, BF16), (model, BF16))],
            grid=(steps,),
            prefetch=(info,),
        )
        for slot, value in zip((middle, normed2, act, slope, cot), got):
            slot.append(value)

    box = {}

    def feed_back(s):
        got = line.run(
            "feed_back", 18,
            feed_back_kernel,
            (cot[s], slope[s], up_weight, down_weight),
            [pl.BlockSpec((tile, model), lambda i, f: (i, 0)), pl.BlockSpec((tile, units), lambda i, f: (i, 0)), full((model, units)), full((units, model))],
            [((block, c), BF16, pl.BlockSpec((tile, c), lambda i, f: (i, 0))) for c in (units, half, half)],
            grid=(steps,),
            prefetch=(info,),
        )
        box[AT_PRE, s], box[AT_N2_KEEP, s] = got[:2]
        box[AT_N2_SEND, s] = swap(got[2], TENSOR, 1)

    def near_core(s):
        box[AT_N2_CORE, s] = add(line, box[AT_N2_KEEP, s], box[AT_N2_SEND, s])
        box[AT_N2_Y, s] = swap(box[AT_N2_CORE, s], TENSOR, tensor_bits[1])

    def near_y(s):
        total = add(line, box[AT_N2_CORE, s], box[AT_N2_Y, s])
        for bit in tensor_bits[2:]:
            total = add(line, total, swap(total, TENSOR, bit))
        box[AT_N2_NEAR, s] = total
        box[AT_N2_FAR, s] = swap(total, TENSOR, 1)

    def attend_back(s):
        outs = [
            ((block, model), BF16), ((block, width), F32), ((1, model), F32),
            ((block, width), BF16), ((block, width), BF16), ((block, width), BF16),
            ((CTX, width), BF16), ((CTX, width), BF16),
            ((pairs, CTX + block, width), BF16), ((pairs, CTX + block, width), BF16),
        ]
        got = line.run(
            "attend_back", 28,
            functools.partial(attend_back_kernel, s, scale),
            (middle[s], box[AT_N2_NEAR, s], box[AT_N2_FAR, s], flat_grad, gain2, out_weight, query, key_self, value_self, key_ctx[s], value_ctx[s], log_sum[s], query_weight, key_weight, value_weight),
            [full((block, model)), full((block, half)), full((block, half)), pl.BlockSpec((block, model), lambda *a, s=s: (s, 0)), full((1, model)), full((width, model))]
            + [rows_of(s)] * 3
            + [full((CTX, width))] * 2
            + [full((block, heads))]
            + [full((model, width))] * 3,
            [out_full(*o) for o in outs],
            prefetch=(info,),
            scratch=[pltpu.VMEM((block, model), BF16), pltpu.VMEM((block, model), F32)]
            + [pltpu.VMEM((block, HD), F32)] * 2
            + [pltpu.VMEM((CTX, HD), F32)] * 2,
        )

        box[AT_BACK, s] = got
        box[AT_GOT, s] = swap(got[9], TENSOR, 1)

    def backs(k):
        return [box[AT_BACK, s][k] for s in range(seqs)]

    def both(key):
        return [box[key, s] for s in range(seqs)]

    def sum_start(key, pieces):
        box[key] = pieces[0], swap(pieces[1], SEQ, bits_of[key][0])

    def sum_second(key):
        near, far = add_pair(line, *box[key])
        box[key, AT_NEAR], box[key, AT_Z] = near, swap(far, SEQ, bits_of[key][1])

    def sum_third(key):
        total = add(line, box[key, AT_NEAR], box[key, AT_Z])
        for bit in bits_of[key][2:-1]:
            total = add(line, total, swap(total, SEQ, bit))
        box[key, AT_TOTAL] = total
        if len(seq_bits) > 2:
            box[key, AT_HOP] = swap(total, SEQ, bits_of[key][-1])

    def sum_last(key):
        total = box[key, AT_TOTAL]
        if len(seq_bits) > 2:
            total = add(line, total, box[key, AT_HOP])
        one, two = bits_of[key][:2]
        across, along = swap(total, SEQ, two), swap(total, SEQ, one)
        last = KINDS[key] >> 1
        if last == 0:
            far = [swap(across, SEQ, one)]
        elif last == 1:
            far = [swap(along, SEQ, two)]
        else:
            size = total.shape[0] // 2
            far = [swap(across[:size], SEQ, one), swap(along[size:], SEQ, two)]
        box[key, AT_QUARTERS] = [total, across, along, *far]

    def pin(key, k):
        line.held.append(box[key, AT_QUARTERS][k])

    def project():
        mid_low, mid_slice, gain2_part, dq, dk, dv, dkc, dvc = (backs(k) for k in range(8))
        ctx_stack = jnp.stack(ctx_parts)
        ins = (normed_low, *mid_low, ctx_stack, *dq, *dk, *dv, *dkc, *dvc, *attended)
        got = (
            line.run(
                "project_grad", 28,
                functools.partial(project_grad_kernel, seqs),
                ins,
                [full(a.shape) for a in ins],
                [out_full((2, model // 4, 4 * width), BF16)] * 2,
                prefetch=(info,),
                )
        )
        sum_start(QUERY, got)

    def ctx_parts_sum():
        box[AT_CTX] = scatter_parts(add_parts(line, backs(8), both(AT_GOT), 0, CTX), TENSOR)

    def n1_parts_sum():
        box[AT_N1] = scatter_parts(add_parts(line, backs(8), both(AT_GOT), CTX, block), TENSOR)

    def lead_step():
        ctx_near, ctx_far = box[AT_CTX]
        ctx_grads, segb_end, lead = line.run(
            "lead", 4,
            functools.partial(lead_kernel, seqs, stride),
            (ctx_near, ctx_far, pack),
            [vmem()] * 3,
            [(*out_full((tiles, seqs * CTX // SUB, SUB, HD), F32), True), (state_shape, F32, vmem()), ((seqs, NS, width), F32, vmem())],
            scratch=[pltpu.VMEM((tiles, seqs * CTX, HD), F32), tab],
        )
        box[AT_LEAD] = ctx_grads, segb_end
        box[AT_SEEN] = []
        box[AT_CARRY] = carried(lead, hop, SEQ, False, box[AT_SEEN])

    def state_step():
        ctx_grads, segb_end = box[AT_LEAD]
        carry_back = box[AT_CARRY]
        box[AT_STATE] = line.run(
            "state_back", 10,
            functools.partial(state_back_kernel, seqs, stride),
            (runs, ctx_grads, entry, segb_end, carry_back, pack),
            [
                full((tiles, seg, SUB, HD)),
                full((tiles, seqs * CTX // SUB, SUB, HD)),
                full(state_shape),
                full(state_shape),
                full((seqs, NS, width)),
                full((PACKED, width)),
            ],
            [out_full((tiles, rows, HD), F32), out_full((small_rows, width), F32)],
            scratch=[
                tab,
                tab,
                pltpu.VMEM((stride, NS, SUB, width), F32),
                tab,
                pltpu.VMEM((seg // stride + 1, NS, SUB, width), F32),
                pltpu.VMEM((tiles, seg, SUB, HD), F32),
                pltpu.VMEM((stride + 2, NS, width), F32),
            ],
            hbm=(0, 1, 2),
        )

    def feed_out():
        got = line.run(
            "feed_out", 14,
            functools.partial(feed_out_kernel, seqs, steps),
            (*act, down_weight),
            [pl.BlockSpec((tile, units), lambda i, f, s=s: (jnp.clip(i - s * steps, 0, steps - 1), 0)) for s in range(seqs)]
            + [full((units, model))],
            [((rows, half), BF16, pl.BlockSpec((tile, half), lambda i, f: (i, 0)))] * 2,
            grid=(seqs * steps,),
            prefetch=(info,),
        )
        box[AT_OUT_KEEP], box[AT_OUT_SEND] = got[0], swap(got[1], TENSOR, 1)

    def out_core():
        total = add(line, box[AT_OUT_KEEP], box[AT_OUT_SEND])
        for bit in tensor_bits[1:-1]:
            total = add(line, total, swap(total, TENSOR, bit))
        box[AT_OUT_CORE], box[AT_OUT_Y] = total, swap(total, TENSOR, tensor_bits[-1])

    def out_add():
        box[AT_OUT_NEAR] = line.run(
            "add_out", 12,
            functools.partial(add_out_kernel, seqs),
            (*middle, box[AT_OUT_CORE], box[AT_OUT_Y]),
            [full((block, model))] * seqs + [full((rows, half))] * 2,
            [out_full((rows, half), BF16)],
            prefetch=(info,),
        )[0]
        box[AT_OUT_FAR] = swap(box[AT_OUT_NEAR], TENSOR, 1)

    def join():
        box[AT_OUTPUTS] = line.run(
            "join", 6,
            join_kernel,
            (box[AT_OUT_NEAR], box[AT_OUT_FAR]),
            [pl.BlockSpec((tile, half), lambda i, f: (i, 0))] * 2,
            [((rows, model), BF16, pl.BlockSpec((tile, model), lambda i, f: (i, 0)))],
            grid=(rows // tile,),
            prefetch=(info,),
        )[0].reshape(seqs, block, model)

    def norm_back():
        chan_grad, pack_grad = box[AT_STATE]
        h1, small, sums = line.run(
            "norm_back", 12,
            functools.partial(norm_back_kernel, seqs),
            (*box[AT_N1], chan_grad, in_chan, inverse, pack, pack_grad, *backs(2)),
            [full((rows, width))] * 2
            + [full((tiles, rows, HD)), full((rows, width)), full((rows, 1)), full((PACKED, width)), full((small_rows, width))]
            + [full((1, model))] * seqs,
            [out_full((rows, width), F32), out_full((small_rows, width), F32), out_full((SUB, rows), F32)],
        )
        box[AT_H1], box[AT_SMALL] = h1, small
        box[AT_SUMS], box[AT_MORE] = sums, swap(sums, TENSOR, 1)
        box[AT_SMALL_GOT] = swap(small, SEQ, seq_bits[0])

    def row_sums():
        total = add_wide(line, box[AT_SUMS], box[AT_MORE])
        for bit in tensor_bits[1:-1]:
            total = add_wide(line, total, swap(total, TENSOR, bit))
        box[AT_SUMS], box[AT_MORE] = total, swap(total, TENSOR, tensor_bits[-1])

    def input_step():
        box[AT_INPUT_GRAD] = line.run(
            "input_grad", 12,
            functools.partial(input_grad_kernel, seqs, model),
            (box[AT_H1], box[AT_SUMS], box[AT_MORE], in_chan, inverse, *backs(1)),
            [full((rows, width)), full((SUB, rows)), full((SUB, rows)), full((rows, width)), full((rows, 1))]
            + [full((block, width))] * seqs,
            [out_full((rows, width), BF16)],
        )[0]

    def small_step(k):
        total = add_wide(line, box[AT_SMALL], box[AT_SMALL_GOT])
        box[AT_SMALL] = total
        later = seq_bits[k + 1 :]
        if k == 2:
            for bit in later:
                box[AT_SMALL] = add_wide(line, box[AT_SMALL], swap(box[AT_SMALL], SEQ, bit))
        elif later:
            box[AT_SMALL_GOT] = swap(total, SEQ, later[0])

    def flags_of(key):
        return swapped if KINDS[key] & 1 else info

    def widen_step(key):
        pieces = box[key, AT_QUARTERS]
        if key == QUERY:
            early = widen_project(line, flags_of(key), pieces[:3], 0, 3)
            box[key, AT_WIDE] = widen_project(line, flags_of(key), pieces[3:], 3, 1, early)
        else:
            box[key, AT_WIDE] = widen(line, flags_of(key), pieces)

    in_chan = lax.dynamic_slice_in_dim(flat_in, idx * width, width, 1)
    swapped = jnp.concatenate([info[1::-1], info[2:]])
    bits_of = {key: [second, first, *seq_bits[2:]] if kind & 1 else seq_bits for key, kind in KINDS.items()}
    feed_back(0)
    sum_start(DOWN, outer(line, flags_of(DOWN), act, cot))
    near_core(0)
    feed_back(1)
    sum_start(UP, outer(line, flags_of(UP), normed2, both(AT_PRE)))
    near_core(1)
    feed_out()
    near_y(0)
    sum_second(DOWN)
    near_y(1)
    attend_back(0)
    sum_third(DOWN)
    attend_back(1)
    sum_second(UP)
    project()
    n1_parts_sum()
    ctx_parts_sum()
    lead_step()
    sum_last(DOWN)
    sum_third(UP)
    sum_second(QUERY)
    sum_last(UP)
    pin(DOWN, 1)
    state_step()
    pin(UP, 2)
    pin(DOWN, 2)
    out_core()
    sum_third(QUERY)
    norm_back()
    row_sums()
    small_step(0)
    widen_step(DOWN)
    small_step(1)
    sum_last(QUERY)
    line.held.append(box[AT_SEEN][0])
    pin(UP, 3)
    input_step()
    widen_step(UP)
    line.held.append(box[AT_SEEN][1])
    pin(QUERY, 2)
    small_step(2)
    out_add()
    join()
    widen_step(QUERY)
    outputs, down_grad, up_grad = box[AT_OUTPUTS], box[DOWN, AT_WIDE], box[UP, AT_WIDE]
    query_grad, key_grad, value_grad, out_grad_w = box[QUERY, AT_WIDE]
    input_grad = box[AT_INPUT_GRAD].reshape(seqs, block, width)
    small = box[AT_SMALL]
    return (
        outputs,
        input_grad,
        small[3 * NS + 1],
        query_grad,
        key_grad,
        value_grad,
        out_grad_w,
        small[3 * NS + 2 : 3 * NS + 2 + model // width].reshape(model),
        up_grad,
        down_grad,
        small[:NS],
        small[NS : 2 * NS],
        small[2 * NS : 3 * NS],
        small[3 * NS],
    )


def solution(mesh):
    in_specs = (
        P(None, SEQ, None),
        P(None, SEQ, None),
        P(),
        P(),
        P(None, TENSOR),
        P(None, TENSOR),
        P(None, TENSOR),
        P(TENSOR, None),
        P(),
        P(None, TENSOR),
        P(TENSOR, None),
        P(None, TENSOR),
        P(None, TENSOR),
        P(None, TENSOR),
        P(TENSOR),
    )
    out_specs = (
        P(None, SEQ, None),
        P(None, SEQ, TENSOR),
        P(TENSOR),
        P(None, TENSOR),
        P(None, TENSOR),
        P(None, TENSOR),
        P(TENSOR, None),
        P(),
        P(None, TENSOR),
        P(TENSOR, None),
        P(None, TENSOR),
        P(None, TENSOR),
        P(None, TENSOR),
        P(TENSOR),
    )
    return jax.shard_map(local, mesh=mesh, in_specs=in_specs, out_specs=out_specs, check_vma=False)
```

```python
import functools

import jax
import jax.numpy as jnp
from jax import lax
from jax.experimental import pallas as pl
from jax.experimental.pallas import tpu as pltpu
from jax.sharding import PartitionSpec as P

SEQ, TENSOR = "seq", "tensor"
HD = 128
NS = 16
CTX = 128
SUB = 8
EPS = 1e-06
F32 = jnp.float32
BF16 = jnp.bfloat16
MIB = 1 << 20


def nn(a, b):
    return lax.dot_general(a, b, (((1,), (0,)), ((), ())), preferred_element_type=F32)


def nt(a, b):
    return lax.dot_general(a, b, (((1,), (1,)), ((), ())), preferred_element_type=F32)


def tn(a, b):
    return lax.dot_general(a, b, (((0,), (0,)), ((), ())), preferred_element_type=F32)


def swap(value, axis, bit):
    count = lax.axis_size(axis)
    return lax.ppermute(value, axis, [(i, i ^ bit) for i in range(count)])


def low_bits(count):
    bit, out = 1, []
    while bit < count:
        out.append(bit)
        bit *= 2
    return out


def sds(shape, dtype):
    return jax.ShapeDtypeStruct(shape, dtype)


def vmem():
    return pl.BlockSpec(memory_space=pltpu.VMEM)


def smem():
    return pl.BlockSpec(memory_space=pltpu.SMEM)


class Line:
    def __init__(self):
        self.mark = None
        self.held = []

    def run(self, name, limit, kernel, args, in_specs, outs, grid=None, prefetch=(), scratch=(), after=None, hbm=(), aliases=None):
        args = [pltpu.with_memory_space_constraint(a, pltpu.HBM) if k in hbm else a for k, a in enumerate(args)]
        in_specs = list(in_specs)
        marks = [] if self.mark is None else [pltpu.with_memory_space_constraint(self.mark, pltpu.HBM)]
        others = [t for t in (after, *self.held) if t is not None]
        self.held = []
        count, extra = len(prefetch) + len(args), len(marks) + len(others)

        def body(*refs):
            return kernel(*refs[:count], *refs[count + extra : count + extra + len(outs)], *refs[count + extra + len(outs) + 1 :])

        in_specs += [pl.BlockSpec(memory_space=pltpu.HBM)] * len(marks) + [pl.BlockSpec(memory_space=pl.ANY)] * len(others)
        *got, self.mark = pl.pallas_call(
            body,
            grid_spec=pltpu.PrefetchScalarGridSpec(
                num_scalar_prefetch=len(prefetch),
                grid=grid or (1,),
                in_specs=in_specs,
                out_specs=[o[2] for o in outs] + [pl.BlockSpec(memory_space=pltpu.HBM)],
                scratch_shapes=list(scratch),
            ),
            out_shape=[pltpu.HBM(o[0], o[1]) if len(o) > 3 else sds(o[0], o[1]) for o in outs] + [pltpu.HBM((SUB, HD), F32)],
            compiler_params=pltpu.CompilerParams(vmem_limit_bytes=limit * MIB),
            cost_estimate=pl.CostEstimate(flops=1, bytes_accessed=1, transcendentals=0),
            input_output_aliases=aliases or {},
            name=name,
        )(*prefetch, *args, *marks, *others)
        return got


def full(shape):
    return pl.BlockSpec(shape, lambda *a: (0,) * len(shape))


def out_full(shape, dtype):
    return (shape, dtype, full(shape))


def lanes(tile):
    return slice(tile * HD, (tile + 1) * HD)


def spread(table, rows, factor=None):
    for n in range(NS):
        row = rows[n : n + 1, :]
        if factor is not None:
            row = jnp.exp(row * factor)
        table[n] = jnp.broadcast_to(row, table.shape[1:])


def scan_step(taps, decay_tab, jump_tab, state):
    tiles = len(taps)
    out = []
    for n in range(NS):
        for t in range(tiles):
            decay = decay_tab[n, :, lanes(t)]
            inner = taps[t][0]
            for tap in taps[t][1:]:
                inner = inner * decay + tap
            out.append(state[n * tiles + t] * jump_tab[n, :, lanes(t)] + inner)
    return tuple(out)


def taps_of(runs_ref, group, stride):
    return [[runs_ref[t, group * stride + i] for i in range(stride)] for t in range(runs_ref.shape[0])]


def segment_ends(state, rate, seg, seqs, seg_ref, end_ref, forward):
    per = SUB // seqs
    tiles = rate.shape[1] // HD
    place = lax.rem(lax.broadcasted_iota(jnp.int32, (SUB, HD), 0), per)
    away = ((per - 1 - place if forward else place) * seg).astype(F32)
    for n in range(NS):
        for t in range(tiles):
            now = state[n * tiles + t]
            seg_ref[n, :, lanes(t)] = now
            part = now * jnp.exp(-rate[n : n + 1, lanes(t)] * away)
            for s in range(seqs):
                end_ref[s, n : n + 1, lanes(t)] = jnp.sum(part[s * per : (s + 1) * per], 0, keepdims=True)


def entry_states(entry_ref, carry_ref, seg_ref, hop, seqs, forward):
    per = SUB // seqs
    for n in range(NS):
        step = hop[n : n + 1, :]
        for s in range(seqs):
            now = carry_ref[s, n : n + 1, :]
            for k in range(per):
                q = s * per + (k if forward else per - 1 - k)
                entry_ref[n, q : q + 1, :] = now
                if k < per - 1:
                    now = now * step + seg_ref[n, q : q + 1, :]


def read_state(ref):
    tiles = ref.shape[2] // HD
    return tuple(ref[n, :, lanes(t)] for n in range(NS) for t in range(tiles))


PACKED = 72
CHUNK = 256


def unpack(pack_ref):
    return (*(pack_ref[k * NS : (k + 1) * NS, :] for k in range(4)), pack_ref[4 * NS : 4 * NS + 1, :], pack_ref[4 * NS + 1 : 4 * NS + 2, :])


def enter_kernel(seqs, stride, info_ref, x_ref, xc_ref, gain_ref, rate_ref, low_ref, inv_ref, runs_ref, seg_ref, fin_ref, flat, decay_tab, jump_tab):
    step, width = x_ref.shape
    tiles, seg = runs_ref.shape[:2]
    piece = CHUNK
    gain = gain_ref[...]
    rate = rate_ref[...]

    @pl.when(pl.program_id(0) == 0)
    def _():
        spread(decay_tab, rate, -1.0)
        spread(jump_tab, rate, -float(stride))

    def norm(i, carry):
        at = pl.ds(pl.multiple_of(i * piece, piece), piece)
        x = x_ref[at, :].astype(F32)
        inv = lax.rsqrt(jnp.sum(x * x, -1, keepdims=True) * (1.0 / width) + EPS)
        low_ref[at, :] = (x * inv * gain).astype(BF16)
        inv_ref[at, :] = inv
        to = pl.ds(pl.multiple_of(pl.program_id(0) * step + i * piece, piece), piece)
        for t in range(tiles):
            flat[t, to, :] = xc_ref[at, lanes(t)].astype(F32) * inv
        return carry

    lax.fori_loop(0, step // piece, norm, 0)

    @pl.when(pl.program_id(0) == pl.num_programs(0) - 1)
    def _():
        def group(g, state):
            taps = []
            for t in range(tiles):
                row = [flat[t, pl.ds(g * stride + i, SUB, stride=seg), :] for i in range(stride)]
                for i in range(stride):
                    runs_ref[t, g * stride + i] = row[i]
                taps.append(row)
            return scan_step(taps, decay_tab, jump_tab, state)

        state = lax.fori_loop(0, seg // stride, group, (jnp.zeros((SUB, HD), F32),) * (NS * tiles))
        segment_ends(state, rate, seg, seqs, seg_ref, fin_ref, True)


def context_kernel(seqs, stride, runs_ref, seg_ref, carry_ref, pack_ref, ctx_ref, entry_ref, decay_tab, jump_tab, out_tab, flat):
    tiles, seg = runs_ref.shape[:2]
    rate, root, s_in, s_out, skip, gain = unpack(pack_ref)
    spread(decay_tab, rate, -1.0)
    spread(jump_tab, rate, -float(stride))
    spread(out_tab, root * s_in * s_out * gain)
    entry_states(entry_ref, carry_ref, seg_ref, jnp.exp(rate * (-float(seg))), seqs, True)
    skip = skip * gain
    groups = seg // stride

    def group(g, state):
        taps = taps_of(runs_ref, g, stride)
        state = scan_step(taps, decay_tab, jump_tab, state)
        for t in range(tiles):
            total = skip[:, lanes(t)] * taps[t][-1]
            for n in range(NS):
                total = total + out_tab[n, :, lanes(t)] * state[n * tiles + t]
            flat[t, pl.ds(g, SUB, stride=groups), :] = total
        return state

    lax.fori_loop(0, groups, group, read_state(entry_ref))
    for t in range(tiles):
        ctx_ref[:, lanes(t)] = flat[t].astype(BF16)


def lead_kernel(seqs, stride, near_ref, far_ref, pack_ref, grads_ref, segb_ref, lead_ref, flat, jump_tab):
    tiles, groups = grads_ref.shape[:2]
    for t in range(tiles):
        flat[t] = near_ref[:, lanes(t)].astype(F32) + far_ref[:, lanes(t)].astype(F32)
    rate = unpack(pack_ref)[0]
    spread(jump_tab, rate, -float(stride))

    def group(i, state):
        g = groups - 1 - i
        grads = [flat[t, pl.ds(g, SUB, stride=groups), :] for t in range(tiles)]
        for t in range(tiles):
            grads_ref[t, g] = grads[t]
        return tuple(state[n * tiles + t] * jump_tab[n, :, lanes(t)] + grads[t] for n in range(NS) for t in range(tiles))

    state = lax.fori_loop(0, groups, group, (jnp.zeros((SUB, HD), F32),) * (NS * tiles))
    segment_ends(state, rate, groups * stride, seqs, segb_ref, lead_ref, False)


def state_back_kernel(
    seqs, stride, runs_ref, grads_ref, entry_ref, segb_ref, carryb_ref, pack_ref, back_ref, packg_ref,
    decay_tab, jump_tab, tap_tab, entryb, states, backs, sums,
):
    tiles, seg = runs_ref.shape[:2]
    groups = seg // stride
    rate, root, s_in, s_out, skip, gain = unpack(pack_ref)
    coeff = root * s_in
    spread(decay_tab, rate, -1.0)
    spread(jump_tab, rate, -float(stride))
    both = coeff * s_out
    for i in range(stride):
        spread(tap_tab.at[i], both * jnp.exp(rate * (-float(stride - 1 - i))))
    entry_states(entryb, carryb_ref, segb_ref, jnp.exp(rate * (-float(seg))), seqs, False)
    zero = jnp.zeros((SUB, HD), F32)

    def forward(g, carry):
        state, totals = carry
        for n in range(NS):
            for t in range(tiles):
                states[g, n, :, lanes(t)] = state[n * tiles + t]
        taps = taps_of(runs_ref, g, stride)
        out = []
        for t in range(tiles):
            grad = grads_ref[t, g]
            out.append(totals[t] + grad * taps[t][-1])
            backs[t, g * stride + stride - 1] = grad * skip[:, lanes(t)]
            for i in range(stride - 1):
                backs[t, g * stride + i] = zero
        return scan_step(taps, decay_tab, jump_tab, state), tuple(out)

    last, totals = lax.fori_loop(0, groups, forward, (read_state(entry_ref), (zero,) * tiles))
    for n in range(NS):
        for t in range(tiles):
            states[groups, n, :, lanes(t)] = last[n * tiles + t]
    for t in range(tiles):
        packg_ref[3 * NS : 3 * NS + 1, lanes(t)] = jnp.sum(totals[t], 0, keepdims=True) * gain[:, lanes(t)]
    lot = 2
    kinds = stride + 2
    for t in range(tiles):
        for first in range(0, NS, lot):
            names = range(first, first + lot)

            def group(i, carry, t=t, names=names):
                g = groups - 1 - i
                adj, acc = carry
                grad = grads_ref[t, g]
                taps = [runs_ref[t, g * stride + i] for i in range(stride)]
                sums_b = [backs[t, g * stride + i] for i in range(stride)]
                new_adj, new_acc = [], []
                for k, n in enumerate(names):
                    now = adj[k] * jump_tab[n, :, lanes(t)] + grad
                    new_adj.append(now)
                    for i in range(stride):
                        sums_b[i] = sums_b[i] + tap_tab[i, n, :, lanes(t)] * now
                        new_acc.append(acc[k * kinds + i] + now * taps[i])
                    new_acc.append(acc[k * kinds + stride] + now * states[g, n, :, lanes(t)])
                    new_acc.append(acc[k * kinds + stride + 1] + grad * states[g + 1, n, :, lanes(t)])
                for i in range(stride):
                    backs[t, g * stride + i] = sums_b[i]
                return tuple(new_adj), tuple(new_acc)

            start = (tuple(entryb[n, :, lanes(t)] for n in names), (zero,) * (lot * kinds))
            _, acc = lax.fori_loop(0, groups, group, start, unroll=4)
            for k, n in enumerate(names):
                for j in range(kinds):
                    sums[j, n : n + 1, lanes(t)] = jnp.sum(acc[k * kinds + j], 0, keepdims=True)

    def spill(g, carry):
        for t in range(tiles):
            for i in range(stride):
                back_ref[t, pl.ds(g * stride + i, SUB, stride=seg), :] = backs[t, g * stride + i]
        return carry

    lax.fori_loop(0, groups, spill, 0)
    decay = jnp.exp(-rate)
    powers = [jnp.ones_like(rate)]
    for _ in range(stride):
        powers.append(powers[-1] * decay)
    coeff_grad = sum(powers[stride - 1 - i] * sums[i] for i in range(stride)) * s_out * gain
    decay_grad = float(stride) * powers[stride - 1] * sums[stride]
    for i in range(stride - 1):
        decay_grad = decay_grad + float(stride - 1 - i) * powers[stride - 2 - i] * sums[i]
    decay_grad = decay_grad * coeff * s_out * gain
    packg_ref[:NS, :] = coeff_grad * s_in * (decay * decay / root) - decay * decay_grad
    packg_ref[NS : 2 * NS, :] = coeff_grad * root
    packg_ref[2 * NS : 3 * NS, :] = coeff * gain * sums[stride + 1]


def carried(value, hop, axis, forward, seen=None):
    count = lax.axis_size(axis)
    mine = lax.axis_index(axis)
    whole = value
    enter = jnp.zeros_like(value)
    for bit in low_bits(count):
        other = swap(whole, axis, bit)
        if seen is not None:
            seen.append(other)
        upper = (mine & bit) != 0
        offset = mine & (bit - 1)
        if not forward:
            upper = jnp.logical_not(upper)
            offset = bit - 1 - offset
        enter = jnp.where(upper, enter + hop(offset) * other, enter)
        span = hop(bit)
        whole = jnp.where(upper, whole + span * other, other + span * whole)
    return enter


def qkv_kernel(x_ref, wq_ref, wk_ref, wv_ref, q_ref, k_ref, v_ref):
    x = x_ref[...]
    q_ref[...] = nn(x, wq_ref[...]).astype(BF16)
    k_ref[...] = nn(x, wk_ref[...]).astype(BF16)
    v_ref[...] = nn(x, wv_ref[...]).astype(BF16)


def masks(first, tile, block, stride):
    row = lax.broadcasted_iota(jnp.int32, (tile, CTX), 0) + first
    col = lax.broadcasted_iota(jnp.int32, (tile, CTX), 1)
    side = stride * col + (stride - 1) <= row
    row = lax.broadcasted_iota(jnp.int32, (tile, block), 0) + first
    col = lax.broadcasted_iota(jnp.int32, (tile, block), 1)
    return side, col <= row


def attend_kernel(parts, scale, idx_ref, q_ref, k_ref, v_ref, wk_ref, wv_ref, *rest):
    ctx_refs, (out_ref, kc_ref, vc_ref, lse_ref) = rest[:parts], rest[parts:]
    block, width = q_ref.shape
    stride = block // CTX
    idx = idx_ref[2]
    key_c = jnp.zeros((CTX, width), F32)
    val_c = jnp.zeros((CTX, width), F32)
    for p in range(parts):
        at = pl.ds(pl.multiple_of((idx ^ p) * width, width), width)
        key_c = key_c + nn(ctx_refs[p][...], wk_ref[at, :])
        val_c = val_c + nn(ctx_refs[p][...], wv_ref[at, :])
    kc_ref[...] = key_c.astype(BF16)
    vc_ref[...] = val_c.astype(BF16)
    tile = min(256, block)
    for h in range(width // HD):
        cols = slice(h * HD, (h + 1) * HD)
        for first in range(0, block, tile):
            seen = first + tile
            rows = slice(first, seen)
            q = q_ref[rows, cols]
            side_ok, own_ok = masks(first, tile, seen, stride)
            side = jnp.where(side_ok, nt(q, kc_ref[:, cols]), -1e30)
            own = jnp.where(own_ok, nt(q, k_ref[:seen, cols]), -1e30)
            top = jnp.maximum(jnp.max(side, -1, keepdims=True), jnp.max(own, -1, keepdims=True))
            side = jnp.exp((side - top) * scale)
            own = jnp.exp((own - top) * scale)
            total = jnp.sum(side, -1, keepdims=True) + jnp.sum(own, -1, keepdims=True)
            share = 1.0 / total
            got = nn((side * share).astype(BF16), vc_ref[:, cols]) + nn((own * share).astype(BF16), v_ref[:seen, cols])
            out_ref[rows, cols] = got.astype(BF16)
            lse_ref[rows, h : h + 1] = top * scale + jnp.log(total)


def attend_back_kernel(
    seq, scale, info_ref, mid_ref, near_ref, far_ref, grad_ref, gain_ref, wo_ref, q_ref, k_ref, v_ref, kc_ref, vc_ref, lse_ref,
    wq_ref, wk_ref, wv_ref,
    low_ref, slice_ref, gaing_ref, dq_ref, dk_ref, dv_ref, dkc_ref, dvc_ref, keep_ref, send_ref,
    n2_ref, full_ref, key_acc, val_acc, skey_acc, sval_acc,
):
    block, width = q_ref.shape
    model = mid_ref.shape[1]
    half = model // 2
    stride = block // CTX
    idx, mine, limit = info_ref[2], info_ref[3], info_ref[4 + seq]
    n2_ref[:, pl.ds(pl.multiple_of(mine * half, half), half)] = near_ref[...]
    n2_ref[:, pl.ds(pl.multiple_of((1 - mine) * half, half), half)] = far_ref[...]
    gain = gain_ref[...]
    step = CHUNK

    def norm(i, total):
        at = pl.ds(pl.multiple_of(i * step, step), step)
        mid = mid_ref[at, :]
        inv = lax.rsqrt(jnp.sum(mid * mid, -1, keepdims=True) * (1.0 / model) + EPS)
        hat = mid * inv
        n2 = n2_ref[at, :].astype(F32)
        prod = n2 * hat
        h2 = n2 * gain
        mean = jnp.sum(h2 * hat, -1, keepdims=True) * (1.0 / model)
        place = lax.broadcasted_iota(jnp.int32, (step, 1), 0) + i * step
        cot = jnp.where(place < limit, grad_ref[at, :].astype(F32), 0.0)
        grad = cot + inv * (h2 - hat * mean)
        full_ref[at, :] = grad
        low_ref[at, :] = grad.astype(BF16)
        return total + jnp.sum(prod, 0, keepdims=True)

    gaing_ref[...] = lax.fori_loop(0, block // step, norm, jnp.zeros((1, model), F32))
    slice_ref[...] = full_ref[:, pl.ds(pl.multiple_of(idx * width, width), width)]
    att_grad = nt(low_ref[...], wo_ref[...]).astype(BF16)
    tile = min(512, block)
    for h in range(width // HD):
        cols = slice(h * HD, (h + 1) * HD)
        for first in range(0, block, tile):
            seen = first + tile
            rows = slice(first, seen)
            q = q_ref[rows, cols]
            grad = att_grad[rows, cols]
            lse = lse_ref[rows, h : h + 1]
            side_ok, own_ok = masks(first, tile, seen, stride)
            kc, k = kc_ref[:, cols], k_ref[:seen, cols]
            side = jnp.exp(jnp.where(side_ok, nt(q, kc) * scale - lse, -1e30))
            own = jnp.exp(jnp.where(own_ok, nt(q, k) * scale - lse, -1e30))
            dside = nt(grad, vc_ref[:, cols])
            down = nt(grad, v_ref[:seen, cols])
            term = jnp.sum(side * dside, -1, keepdims=True) + jnp.sum(own * down, -1, keepdims=True)
            dside = (side * (dside - term)).astype(BF16)
            down = (own * (down - term)).astype(BF16)
            dq_ref[rows, cols] = ((nn(dside, kc) + nn(down, k)) * scale).astype(BF16)
            side = side.astype(BF16)
            own = own.astype(BF16)
            last = first + tile >= block
            fresh = first == 0
            for acc, score, right in (
                (skey_acc, dside, q),
                (sval_acc, side, grad),
            ):
                got = tn(score, right)
                acc[...] = got if fresh else acc[...] + got
            for acc, score, right in (
                (key_acc, down, q),
                (val_acc, own, grad),
            ):
                got = tn(score, right)
                if fresh:
                    acc[:seen, :] = got
                else:
                    acc[:first, :] = acc[:first, :] + got[:first]
                    acc[first:seen, :] = got[first:]
            if last:
                dk_ref[:, cols] = (key_acc[...] * scale).astype(BF16)
                dv_ref[:, cols] = val_acc[...].astype(BF16)
                dkc_ref[:, cols] = (skey_acc[...] * scale).astype(BF16)
                dvc_ref[:, cols] = sval_acc[...].astype(BF16)
    count = model // width
    for p in range(count):
        at = pl.ds(pl.multiple_of((idx ^ p) * width, width), width)
        wk, wv = wk_ref[at, :], wv_ref[at, :]
        ctx = nt(dkc_ref[...], wk) + nt(dvc_ref[...], wv)
        (send_ref if p % 2 else keep_ref)[p // 2, :CTX, :] = ctx.astype(BF16)
    for p in range(count):
        at = pl.ds(pl.multiple_of((idx ^ p) * width, width), width)
        own = nt(dq_ref[...], wq_ref[at, :]) + nt(dk_ref[...], wk_ref[at, :]) + nt(dv_ref[...], wv_ref[at, :])
        (send_ref if p % 2 else keep_ref)[p // 2, CTX:, :] = own.astype(BF16)


def feed_kernel(parts, tile, seq, info_ref, x_ref, grad_ref, gain_ref, up_ref, *rest):
    att_refs, wo_refs = rest[:parts], rest[parts : 2 * parts]
    mid_ref, n2_ref, act_ref, slope_ref, cot_ref = rest[2 * parts :]
    model = x_ref.shape[1]
    limit = info_ref[4 + seq]
    mid = x_ref[...].astype(F32)
    got = nn(att_refs[0][...], wo_refs[0][...])
    for p in range(1, parts):
        got = got + nn(att_refs[p][...], wo_refs[p][...])
    mid = mid + got
    mid_ref[...] = mid
    inv = lax.rsqrt(jnp.sum(mid * mid, -1, keepdims=True) * (1.0 / model) + EPS)
    n2_ref[...] = (mid * inv * gain_ref[...]).astype(BF16)
    place = lax.broadcasted_iota(jnp.int32, (tile, 1), 0) + pl.program_id(0) * tile
    cot_ref[...] = jnp.where(place < limit, grad_ref[...].astype(F32), 0.0).astype(BF16)
    pre = nn(n2_ref[...], up_ref[...])
    cdf = 0.5 * (1.0 + lax.erf(pre * 0.7071067811865476))
    pdf = jnp.exp(pre * pre * -0.5) * 0.3989422804014327
    act_ref[...] = (pre * cdf).astype(BF16)
    slope_ref[...] = (cdf + pre * pdf).astype(BF16)


def halves(info_ref, half):
    mine = info_ref[3]
    return (
        pl.ds(pl.multiple_of(mine * half, half), half),
        pl.ds(pl.multiple_of((1 - mine) * half, half), half),
    )


def feed_back_kernel(info_ref, cot_ref, slope_ref, up_ref, down_ref, pre_ref, keep_ref, send_ref):
    near, far = halves(info_ref, keep_ref.shape[1])
    pull = nt(cot_ref[...], down_ref[...])
    pre_ref[...] = (pull * slope_ref[...].astype(F32)).astype(BF16)
    send_ref[...] = nt(pre_ref[...], up_ref[far, :]).astype(BF16)
    keep_ref[...] = nt(pre_ref[...], up_ref[near, :]).astype(BF16)


def feed_out_kernel(seqs, steps, info_ref, *refs):
    down_ref, keep_ref, send_ref = refs[seqs:]
    near, far = halves(info_ref, keep_ref.shape[1])
    for s in range(seqs):

        @pl.when(pl.program_id(0) // steps == s)
        def _(s=s):
            send_ref[...] = nn(refs[s][...], down_ref[:, far]).astype(BF16)
            keep_ref[...] = nn(refs[s][...], down_ref[:, near]).astype(BF16)


def add_kernel(a_ref, b_ref, out_ref):
    out_ref[...] = (a_ref[...].astype(F32) + b_ref[...].astype(F32)).astype(BF16)


def add_pair_kernel(a_ref, b_ref, out0_ref, out1_ref):
    out0_ref[...] = (a_ref[0].astype(F32) + b_ref[0].astype(F32)).astype(BF16)
    out1_ref[...] = (a_ref[1].astype(F32) + b_ref[1].astype(F32)).astype(BF16)


def add_parts_kernel(pairs, count, start, size, *refs):
    keeps, gots, outs = refs[:count], refs[count : 2 * count], refs[2 * count :]
    at = slice(start, start + size)
    for m in range(pairs):
        for s in range(count):
            outs[m][s * size : (s + 1) * size, :] = (keeps[s][m, at].astype(F32) + gots[s][m, at].astype(F32)).astype(BF16)


def add_out_kernel(seqs, info_ref, *refs):
    mids, (a_ref, b_ref, out_ref) = refs[:seqs], refs[seqs:]
    near, _ = halves(info_ref, out_ref.shape[1])
    block = mids[0].shape[0]
    for s in range(seqs):
        at = slice(s * block, (s + 1) * block)
        total = a_ref[at, :].astype(F32) + b_ref[at, :].astype(F32)
        out_ref[at, :] = (mids[s][:, near] + total).astype(BF16)


def join_kernel(info_ref, near_ref, far_ref, out_ref):
    near, far = halves(info_ref, near_ref.shape[1])
    out_ref[:, near] = near_ref[...]
    out_ref[:, far] = far_ref[...]


def high(a, b, dims):
    return lax.dot_general(a, b, (dims, ((), ())), precision=lax.Precision.HIGHEST, preferred_element_type=F32)


def norm_back_kernel(seqs, near_ref, far_ref, back_ref, x_ref, inv_ref, pack_ref, packg_ref, *refs):
    gains, (h1_ref, small_ref, sums_ref) = refs[:seqs], refs[seqs:]
    tiles, rows = back_ref.shape[:2]
    width = tiles * HD
    gain = unpack(pack_ref)[5]
    step = 128
    ones = jnp.ones((SUB, HD), F32)

    def part(i, total):
        at = pl.ds(pl.multiple_of(i * step, step), step)
        inv = inv_ref[at, :]
        sums, out = 0.0, []
        for t in range(tiles):
            n1 = near_ref[at, lanes(t)].astype(F32) + far_ref[at, lanes(t)].astype(F32) + back_ref[t, at, :]
            hat = x_ref[at, lanes(t)].astype(F32) * inv
            prod = n1 * hat
            h1 = n1 * gain[:, lanes(t)]
            h1_ref[at, lanes(t)] = h1
            out.append(total[t] + jnp.sum(prod, 0, keepdims=True))
            sums = sums + h1 * hat
        sums_ref[:, at] = high(ones, sums, ((1,), (1,)))
        return tuple(out)

    total = lax.fori_loop(0, rows // step, part, (jnp.zeros((1, HD), F32),) * tiles)
    small_ref[...] = jnp.zeros(small_ref.shape, F32)
    small_ref[: 3 * NS + 1, :] = packg_ref[: 3 * NS + 1, :]
    for t in range(tiles):
        small_ref[3 * NS + 1 : 3 * NS + 2, lanes(t)] = total[t]
    gain2 = gains[0][...]
    for s in range(1, seqs):
        gain2 = gain2 + gains[s][...]
    for k in range(gain2.shape[1] // width):
        small_ref[3 * NS + 2 + k : 3 * NS + 3 + k, :] = gain2[:, k * width : (k + 1) * width]


def add_wide_kernel(a_ref, b_ref, out_ref):
    out_ref[...] = a_ref[...] + b_ref[...]


def add_wide(line, a, b):
    return line.run("add", 4, add_wide_kernel, (a, b), [full(a.shape)] * 2, [out_full(a.shape, F32)])[0]


def input_grad_kernel(seqs, model, h1_ref, sums_ref, more_ref, x_ref, inv_ref, *refs):
    mids, out_ref = refs[:seqs], refs[seqs]
    block, width = mids[0].shape
    step = 128
    ones = jnp.full((SUB, HD), 1.0 / (SUB * model), F32)
    for s in range(seqs):

        def part(i, carry, s=s):
            at = pl.ds(pl.multiple_of(s * block + i * step, step), step)
            here = pl.ds(pl.multiple_of(i * step, step), step)
            inv = inv_ref[at, :]
            mean = high(sums_ref[:, at] + more_ref[:, at], ones, ((0,), (0,)))
            for t in range(width // HD):
                hat = x_ref[at, lanes(t)].astype(F32) * inv
                grad = mids[s][here, lanes(t)] + inv * (h1_ref[at, lanes(t)] - hat * mean)
                out_ref[at, lanes(t)] = grad.astype(BF16)
            return carry

        lax.fori_loop(0, block // step, part, 0)


def add_pair(line, a, b):
    return line.run("add_pair", 8, add_pair_kernel, (a, b), [full(a.shape)] * 2, [out_full(a.shape[1:], BF16)] * 2)


def add_parts(line, keeps, gots, start, size):
    pairs, _, width = keeps[0].shape
    count = len(keeps)
    return line.run(
        "add_parts", 12,
        functools.partial(add_parts_kernel, pairs, count, start, size),
        (*keeps, *gots),
        [full(keeps[0].shape)] * (2 * count),
        [out_full((count * size, width), BF16)] * pairs,
    )


def add(line, a, b):
    return line.run("add", 8, add_kernel, (a, b), [full(a.shape)] * 2, [out_full(a.shape, BF16)])[0]


def quarter(info, far, step):
    return (info[0] ^ far) * 2 + (info[1] ^ step)


PIECES = ((0, 0), (0, 1), (1, 0), (1, 1))


def outer_kernel(pairs, info_ref, *refs):
    piece = refs[0].shape[1] // 4
    for far, step in PIECES:
        out_ref = refs[2 * pairs + far].at[step]
        at = pl.ds(pl.multiple_of(quarter(info_ref, far, step) * piece, piece), piece)
        total = tn(refs[0][:, at], refs[pairs][...])
        for p in range(1, pairs):
            total = total + tn(refs[p][:, at], refs[pairs + p][...])
        out_ref[...] = total.astype(BF16)


def outer(line, info, lefts, rights):
    rows, cols = lefts[0].shape[1], rights[0].shape[1]
    return line.run(
        "outer", 20,
        functools.partial(outer_kernel, len(lefts)),
        [*lefts, *rights],
        [full(a.shape) for a in (*lefts, *rights)],
        [out_full((2, rows // 4, cols), BF16)] * 2,
        prefetch=(info,),
    )


def project_grad_kernel(seqs, info_ref, *refs):
    refs = list(refs)

    def take(count):
        got = refs[:count]
        del refs[:count]
        return got

    (low_ref,) = take(1)
    mids = take(seqs)
    (ctx_ref,) = take(1)
    dqs, dks, dvs, dkcs, dvcs, atts = (take(seqs) for _ in range(6))
    block, width = dqs[0].shape
    quart = low_ref.shape[1] // 4 // width
    for far, step in PIECES:
        out_ref = refs[far].at[step]
        for i in range(quart):
            part = quarter(info_ref, far, step) * quart + i
            at = pl.ds(pl.multiple_of(part * width, width), width)
            rows = slice(i * width, (i + 1) * width)
            for k, (grads, more) in enumerate(((dqs, None), (dks, dkcs), (dvs, dvcs))):
                total = 0.0
                for s in range(seqs):
                    total = total + tn(low_ref[s * block : (s + 1) * block, at], grads[s][...])
                    if more is not None:
                        total = total + tn(ctx_ref[part ^ info_ref[2], s * CTX : (s + 1) * CTX, :], more[s][...])
                out_ref[rows, k * width : (k + 1) * width] = total.astype(BF16)
            total = 0.0
            for s in range(seqs):
                total = total + tn(atts[s][...], mids[s][:, at])
            out_ref[rows, 3 * width :] = total.astype(BF16)


def order(p, f):
    return quarter(f, p // 2, p % 2)


def widen_kernel(flags_ref, *refs):
    out_ref = refs[-1]
    for p in range(4):

        @pl.when(pl.program_id(0) == p)
        def _(p=p):
            start = 0
            for ref in refs[p : p + 1] if p < 3 else refs[3:-1]:
                size = ref.shape[0]
                out_ref[start : start + size, :] = ref[...].astype(F32)
                start += size


def widen(line, info, pieces):
    piece, cols = pieces[0].shape
    return line.run(
        "widen", 10,
        widen_kernel,
        pieces,
        [full(p.shape) for p in pieces],
        [((4 * piece, cols), F32, pl.BlockSpec((piece, cols), lambda p, f: (order(p, f), 0)))],
        grid=(4,),
        prefetch=(info,),
    )[0]


def widen_project_kernel(first, count, parts, flags_ref, *refs):
    pieces, outs = refs[:parts], refs[-4:]
    width = pieces[0].shape[1] // 4
    for p in range(count):

        @pl.when(pl.program_id(0) == p)
        def _(p=p):
            start = 0
            for ref in pieces[p : p + 1] if first + p < 3 else pieces[p:]:
                size = ref.shape[0]
                for k in range(3):
                    outs[k][start : start + size, :] = ref[:, k * width : (k + 1) * width].astype(F32)
                step = min(size, width)
                for j in range(0, size, step):
                    row = (start + j) % width
                    to = (start + j) // width * width
                    outs[3][row : row + step, to : to + width] = ref[j : j + step, 3 * width :].astype(F32)
                start += size


def widen_project(line, info, pieces, first, count, before=None):
    rows = pieces[0].shape[0] if first == 0 else sum(p.shape[0] for p in pieces)
    cols = pieces[0].shape[1]
    width = cols // 4
    given = pieces[first : first + count] if first == 0 else pieces
    before = before or []
    return line.run(
        "widen_project", 10,
        functools.partial(widen_project_kernel, first, count, len(given)),
        [*given, *before],
        [full(p.shape) for p in given] + [pl.BlockSpec(memory_space=pl.ANY)] * len(before),
        [((4 * rows, width), F32, pl.BlockSpec((rows, width), lambda p, f: (order(p + first, f), 0)))] * 3
        + [((width, 4 * rows), F32, pl.BlockSpec((width, rows), lambda p, f: (0, order(p + first, f))))],
        grid=(count,),
        prefetch=(info,),
        aliases={1 + len(given) + k: k for k in range(len(before))},
    )


def gather_parts(value, axis):
    parts = [value]
    for bit in reversed(low_bits(lax.axis_size(axis))):
        parts = parts + [None] * 0 + [swap(p, axis, bit) for p in parts]
    count = len(parts)
    order = [0]
    for bit in reversed(low_bits(count)):
        order = order + [k ^ bit for k in order]
    out = [None] * count
    for k, p in zip(order, parts):
        out[k] = p
    return out


def add_low(a, b):
    return (a.astype(F32) + b.astype(F32)).astype(BF16)


def scatter_parts(parts, axis):
    bits = low_bits(lax.axis_size(axis))[1:]
    for bit in bits:
        keep, send = parts[0::2], parts[1::2]
        got = [swap(p, axis, bit) for p in send]
        if bit != bits[-1]:
            parts = [add_low(a, b) for a, b in zip(keep, got)]
    return keep[0], got[0]


(
    AT_PRE, AT_N2_KEEP, AT_N2_SEND, AT_N2_CORE, AT_N2_Y, AT_N2_NEAR, AT_N2_FAR, AT_BACK, AT_GOT, AT_NEAR, AT_Z,
    AT_TOTAL, AT_HOP, AT_QUARTERS, AT_CTX, AT_N1, AT_LEAD, AT_SEEN, AT_CARRY, AT_STATE, AT_OUT_KEEP, AT_OUT_SEND,
    AT_OUT_CORE, AT_OUT_Y, AT_OUT_NEAR, AT_OUT_FAR, AT_OUTPUTS, AT_H1, AT_SMALL, AT_SUMS, AT_MORE, AT_SMALL_GOT,
    AT_INPUT_GRAD, AT_WIDE, DOWN, UP, QUERY, AT_CTX_STACK, VALUE,
) = range(39)
KINDS = {DOWN: 0, UP: 0, QUERY: 4}


def local(
    inputs, out_grad, lengths, norm_gain, query_weight, key_weight, value_weight, out_weight,
    mlp_gain, up_weight, down_weight, decay_rate, state_input, state_output, skip_gain,
):
    seqs, block, model = inputs.shape
    width = query_weight.shape[1]
    units = up_weight.shape[1]
    heads = width // HD
    tiles = width // HD
    stride = block // CTX
    scale = HD ** (-0.5)
    tensor_count = lax.axis_size(TENSOR)
    tensor_bits = low_bits(tensor_count)
    idx = lax.axis_index(TENSOR)
    place = lax.axis_index(SEQ)
    rows = seqs * block
    seg = rows // SUB
    half = model // 2
    pairs = tensor_count // 2
    small_rows = (3 * NS + 2 + tensor_count + 7) // 8 * 8
    seq_bits = low_bits(lax.axis_size(SEQ))
    first, second = seq_bits[:2]
    line = Line()
    info = jnp.concatenate(
        [
            jnp.stack([(place & first) // first, (place & second) // second, idx, idx & 1]).astype(jnp.int32),
            (lengths - place * block).astype(jnp.int32),
        ]
    )

    flat_in = inputs.reshape(rows, model)
    flat_grad = out_grad.reshape(rows, model)
    gain_all = norm_gain.reshape(1, model)
    gain2 = mlp_gain.reshape(1, model)
    gain_chan = lax.dynamic_slice_in_dim(norm_gain, idx * width, width, 0)
    gain_row = gain_chan.reshape(1, width)
    pack = jnp.concatenate(
        [
            decay_rate,
            jnp.sqrt(-jnp.expm1(-2.0 * decay_rate)),
            state_input,
            state_output,
            skip_gain.reshape(1, width),
            gain_row,
            jnp.zeros((PACKED - 4 * NS - 2, width), F32),
        ]
    )
    tab = pltpu.VMEM((NS, SUB, width), F32)
    state_shape = (NS, SUB, width)

    def hop(blocks):
        return jnp.exp(-decay_rate * (jnp.asarray(blocks, F32) * block))[None]

    def rows_of(s):
        return pl.BlockSpec((block, width), lambda *a, s=s: (s, 0))

    wo_parts = gather_parts(out_weight, TENSOR)

    tile = 256
    normed_low, inverse, runs, seg_end, final = line.run(
        "enter", 10,
        functools.partial(enter_kernel, seqs, stride),
        (flat_in, flat_in, gain_all, decay_rate),
        [
            pl.BlockSpec((tile, model), lambda i, f: (i, 0)),
            pl.BlockSpec((tile, width), lambda i, f: (i, f[2])),
            full((1, model)),
            full((NS, width)),
        ],
        [
            ((rows, model), BF16, pl.BlockSpec((tile, model), lambda i, f: (i, 0))),
            ((rows, 1), F32, pl.BlockSpec((tile, 1), lambda i, f: (i, 0)), True),
            (*out_full((tiles, seg, SUB, HD), F32), True),
            (*out_full(state_shape, F32), True),
            out_full((seqs, NS, width), F32),
        ],
        grid=(rows // tile,),
        prefetch=(info,),
        scratch=[pltpu.VMEM((tiles, rows, HD), F32), tab, tab],
        hbm=(2, 3),
    )
    carry_in = carried(final, hop, SEQ, True)

    ctx_low, entry = line.run(
        "context", 6,
        functools.partial(context_kernel, seqs, stride),
        (runs, seg_end, carry_in, pack),
        [full((tiles, seg, SUB, HD)), full(state_shape), full((seqs, NS, width)), full((PACKED, width))],
        [out_full((seqs * CTX, width), BF16), (*out_full(state_shape, F32), True)],
        scratch=[tab, tab, tab, pltpu.VMEM((tiles, seqs * CTX, HD), F32)],
        hbm=(0, 1),
    )
    ctx_parts = gather_parts(ctx_low, TENSOR)

    query, key_self, value_self = line.run(
        "qkv", 10,
        qkv_kernel,
        (normed_low, query_weight, key_weight, value_weight),
        [pl.BlockSpec((tile, model), lambda i: (i, 0))] + [full((model, width))] * 3,
        [((rows, width), BF16, pl.BlockSpec((tile, width), lambda i: (i, 0)))] * 3,
        grid=(rows // tile,),
        after=wo_parts[2] if tensor_count > 2 else None,
    )

    attended, key_ctx, value_ctx, log_sum, att_parts = [], [], [], [], []
    for s in range(seqs):
        a, kc, vc, ls = line.run(
            "attend", 12,
            functools.partial(attend_kernel, tensor_count, scale),
            (query, key_self, value_self, key_weight, value_weight, *ctx_parts),
            [rows_of(s)] * 3
            + [full((model, width))] * 2
            + [pl.BlockSpec((CTX, width), lambda *a, s=s: (s, 0))] * tensor_count,
            [
                out_full((block, width), BF16),
                out_full((CTX, width), BF16),
                out_full((CTX, width), BF16),
                out_full((block, heads), F32),
            ],
            prefetch=(info,),
        )
        attended.append(a)
        key_ctx.append(kc)
        value_ctx.append(vc)
        log_sum.append(ls)
        att_parts.append(gather_parts(a, TENSOR))

    steps = block // tile
    middle, normed2, act, slope, cot = ([] for _ in range(5))
    for s in range(seqs):

        def at(cols, s=s):
            return pl.BlockSpec((tile, cols), lambda i, f, s=s: (s * steps + i, 0))

        def own(cols):
            return pl.BlockSpec((tile, cols), lambda i, f: (i, 0))

        got = line.run(
            "feed", 30,
            functools.partial(feed_kernel, tensor_count, tile, s),
            (flat_in, flat_grad, gain2, up_weight, *att_parts[s], *wo_parts),
            [at(model), at(model), full((1, model)), full((model, units))]
            + [own(width)] * tensor_count
            + [full((width, model))] * tensor_count,
            [((block, c), t, own(c)) for c, t in ((model, F32), (model, BF16), (units, BF16), (units, BF16), (model, BF16))],
            grid=(steps,),
            prefetch=(info,),
        )
        for slot, value in zip((middle, normed2, act, slope, cot), got):
            slot.append(value)

    box = {}

    def feed_back(s):
        got = line.run(
            "feed_back", 18,
            feed_back_kernel,
            (cot[s], slope[s], up_weight, down_weight),
            [pl.BlockSpec((tile, model), lambda i, f: (i, 0)), pl.BlockSpec((tile, units), lambda i, f: (i, 0)), full((model, units)), full((units, model))],
            [((block, c), BF16, pl.BlockSpec((tile, c), lambda i, f: (i, 0))) for c in (units, half, half)],
            grid=(steps,),
            prefetch=(info,),
        )
        box[AT_PRE, s], box[AT_N2_KEEP, s] = got[:2]
        box[AT_N2_SEND, s] = swap(got[2], TENSOR, 1)

    def near_core(s):
        box[AT_N2_CORE, s] = add(line, box[AT_N2_KEEP, s], box[AT_N2_SEND, s])
        box[AT_N2_Y, s] = swap(box[AT_N2_CORE, s], TENSOR, tensor_bits[1])

    def near_y(s):
        total = add(line, box[AT_N2_CORE, s], box[AT_N2_Y, s])
        for bit in tensor_bits[2:]:
            total = add(line, total, swap(total, TENSOR, bit))
        box[AT_N2_NEAR, s] = total
        box[AT_N2_FAR, s] = swap(total, TENSOR, 1)

    def attend_back(s):
        outs = [
            ((block, model), BF16), ((block, width), F32), ((1, model), F32),
            ((block, width), BF16), ((block, width), BF16), ((block, width), BF16),
            ((CTX, width), BF16), ((CTX, width), BF16),
            ((pairs, CTX + block, width), BF16), ((pairs, CTX + block, width), BF16),
        ]
        got = line.run(
            "attend_back", 28,
            functools.partial(attend_back_kernel, s, scale),
            (middle[s], box[AT_N2_NEAR, s], box[AT_N2_FAR, s], flat_grad, gain2, out_weight, query, key_self, value_self, key_ctx[s], value_ctx[s], log_sum[s], query_weight, key_weight, value_weight),
            [full((block, model)), full((block, half)), full((block, half)), pl.BlockSpec((block, model), lambda *a, s=s: (s, 0)), full((1, model)), full((width, model))]
            + [rows_of(s)] * 3
            + [full((CTX, width))] * 2
            + [full((block, heads))]
            + [full((model, width))] * 3,
            [out_full(*o) for o in outs],
            prefetch=(info,),
            scratch=[pltpu.VMEM((block, model), BF16), pltpu.VMEM((block, model), F32)]
            + [pltpu.VMEM((block, HD), F32)] * 2
            + [pltpu.VMEM((CTX, HD), F32)] * 2,
        )

        box[AT_BACK, s] = got
        box[AT_GOT, s] = swap(got[9], TENSOR, 1)

    def backs(k):
        return [box[AT_BACK, s][k] for s in range(seqs)]

    def both(key):
        return [box[key, s] for s in range(seqs)]

    def sum_start(key, pieces):
        box[key] = pieces[0], swap(pieces[1], SEQ, bits_of[key][0])

    def sum_second(key):
        near, far = add_pair(line, *box[key])
        box[key, AT_NEAR], box[key, AT_Z] = near, swap(far, SEQ, bits_of[key][1])

    def sum_third(key):
        total = add(line, box[key, AT_NEAR], box[key, AT_Z])
        for bit in bits_of[key][2:-1]:
            total = add(line, total, swap(total, SEQ, bit))
        box[key, AT_TOTAL] = total
        if len(seq_bits) > 2:
            box[key, AT_HOP] = swap(total, SEQ, bits_of[key][-1])

    def sum_last(key):
        total = box[key, AT_TOTAL]
        if len(seq_bits) > 2:
            total = add(line, total, box[key, AT_HOP])
        one, two = bits_of[key][:2]
        across, along = swap(total, SEQ, two), swap(total, SEQ, one)
        last = KINDS[key] >> 1
        if last == 0:
            far = [swap(across, SEQ, one)]
        elif last == 1:
            far = [swap(along, SEQ, two)]
        else:
            size = total.shape[0] // 2
            far = [swap(across[:size], SEQ, one), swap(along[size:], SEQ, two)]
        box[key, AT_QUARTERS] = [total, across, along, *far]

    def pin(key, k):
        line.held.append(box[key, AT_QUARTERS][k])

    def project():
        mid_low, mid_slice, gain2_part, dq, dk, dv, dkc, dvc = (backs(k) for k in range(8))
        ctx_stack = jnp.stack(ctx_parts)
        ins = (normed_low, *mid_low, ctx_stack, *dq, *dk, *dv, *dkc, *dvc, *attended)
        got = (
            line.run(
                "project_grad", 28,
                functools.partial(project_grad_kernel, seqs),
                ins,
                [full(a.shape) for a in ins],
                [out_full((2, model // 4, 4 * width), BF16)] * 2,
                prefetch=(info,),
                )
        )
        sum_start(QUERY, got)

    def ctx_parts_sum():
        box[AT_CTX] = scatter_parts(add_parts(line, backs(8), both(AT_GOT), 0, CTX), TENSOR)

    def n1_parts_sum():
        box[AT_N1] = scatter_parts(add_parts(line, backs(8), both(AT_GOT), CTX, block), TENSOR)

    def lead_step():
        ctx_near, ctx_far = box[AT_CTX]
        ctx_grads, segb_end, lead = line.run(
            "lead", 4,
            functools.partial(lead_kernel, seqs, stride),
            (ctx_near, ctx_far, pack),
            [vmem()] * 3,
            [(*out_full((tiles, seqs * CTX // SUB, SUB, HD), F32), True), (state_shape, F32, vmem()), ((seqs, NS, width), F32, vmem())],
            scratch=[pltpu.VMEM((tiles, seqs * CTX, HD), F32), tab],
        )
        box[AT_LEAD] = ctx_grads, segb_end
        box[AT_SEEN] = []
        box[AT_CARRY] = carried(lead, hop, SEQ, False, box[AT_SEEN])

    def state_step():
        ctx_grads, segb_end = box[AT_LEAD]
        carry_back = box[AT_CARRY]
        box[AT_STATE] = line.run(
            "state_back", 10,
            functools.partial(state_back_kernel, seqs, stride),
            (runs, ctx_grads, entry, segb_end, carry_back, pack),
            [
                full((tiles, seg, SUB, HD)),
                full((tiles, seqs * CTX // SUB, SUB, HD)),
                full(state_shape),
                full(state_shape),
                full((seqs, NS, width)),
                full((PACKED, width)),
            ],
            [out_full((tiles, rows, HD), F32), out_full((small_rows, width), F32)],
            scratch=[
                tab,
                tab,
                pltpu.VMEM((stride, NS, SUB, width), F32),
                tab,
                pltpu.VMEM((seg // stride + 1, NS, SUB, width), F32),
                pltpu.VMEM((tiles, seg, SUB, HD), F32),
                pltpu.VMEM((stride + 2, NS, width), F32),
            ],
            hbm=(0, 1, 2),
        )

    def feed_out():
        got = line.run(
            "feed_out", 14,
            functools.partial(feed_out_kernel, seqs, steps),
            (*act, down_weight),
            [pl.BlockSpec((tile, units), lambda i, f, s=s: (jnp.clip(i - s * steps, 0, steps - 1), 0)) for s in range(seqs)]
            + [full((units, model))],
            [((rows, half), BF16, pl.BlockSpec((tile, half), lambda i, f: (i, 0)))] * 2,
            grid=(seqs * steps,),
            prefetch=(info,),
        )
        box[AT_OUT_KEEP], box[AT_OUT_SEND] = got[0], swap(got[1], TENSOR, 1)

    def out_core():
        total = add(line, box[AT_OUT_KEEP], box[AT_OUT_SEND])
        for bit in tensor_bits[1:-1]:
            total = add(line, total, swap(total, TENSOR, bit))
        box[AT_OUT_CORE], box[AT_OUT_Y] = total, swap(total, TENSOR, tensor_bits[-1])

    def out_add():
        box[AT_OUT_NEAR] = line.run(
            "add_out", 12,
            functools.partial(add_out_kernel, seqs),
            (*middle, box[AT_OUT_CORE], box[AT_OUT_Y]),
            [full((block, model))] * seqs + [full((rows, half))] * 2,
            [out_full((rows, half), BF16)],
            prefetch=(info,),
        )[0]
        box[AT_OUT_FAR] = swap(box[AT_OUT_NEAR], TENSOR, 1)

    def join():
        box[AT_OUTPUTS] = line.run(
            "join", 6,
            join_kernel,
            (box[AT_OUT_NEAR], box[AT_OUT_FAR]),
            [pl.BlockSpec((tile, half), lambda i, f: (i, 0))] * 2,
            [((rows, model), BF16, pl.BlockSpec((tile, model), lambda i, f: (i, 0)))],
            grid=(rows // tile,),
            prefetch=(info,),
        )[0].reshape(seqs, block, model)

    def norm_back():
        chan_grad, pack_grad = box[AT_STATE]
        h1, small, sums = line.run(
            "norm_back", 12,
            functools.partial(norm_back_kernel, seqs),
            (*box[AT_N1], chan_grad, in_chan, inverse, pack, pack_grad, *backs(2)),
            [full((rows, width))] * 2
            + [full((tiles, rows, HD)), full((rows, width)), full((rows, 1)), full((PACKED, width)), full((small_rows, width))]
            + [full((1, model))] * seqs,
            [out_full((rows, width), F32), out_full((small_rows, width), F32), out_full((SUB, rows), F32)],
        )
        box[AT_H1], box[AT_SMALL] = h1, small
        box[AT_SUMS], box[AT_MORE] = sums, swap(sums, TENSOR, 1)
        box[AT_SMALL_GOT] = swap(small, SEQ, seq_bits[0])

    def row_sums():
        total = add_wide(line, box[AT_SUMS], box[AT_MORE])
        for bit in tensor_bits[1:-1]:
            total = add_wide(line, total, swap(total, TENSOR, bit))
        box[AT_SUMS], box[AT_MORE] = total, swap(total, TENSOR, tensor_bits[-1])

    def input_step():
        box[AT_INPUT_GRAD] = line.run(
            "input_grad", 12,
            functools.partial(input_grad_kernel, seqs, model),
            (box[AT_H1], box[AT_SUMS], box[AT_MORE], in_chan, inverse, *backs(1)),
            [full((rows, width)), full((SUB, rows)), full((SUB, rows)), full((rows, width)), full((rows, 1))]
            + [full((block, width))] * seqs,
            [out_full((rows, width), BF16)],
        )[0]

    def small_step(k):
        total = add_wide(line, box[AT_SMALL], box[AT_SMALL_GOT])
        box[AT_SMALL] = total
        later = seq_bits[k + 1 :]
        if k == 2:
            for bit in later:
                box[AT_SMALL] = add_wide(line, box[AT_SMALL], swap(box[AT_SMALL], SEQ, bit))
        elif later:
            box[AT_SMALL_GOT] = swap(total, SEQ, later[0])

    def flags_of(key):
        return swapped if KINDS[key] & 1 else info

    def widen_step(key):
        pieces = box[key, AT_QUARTERS]
        if key == QUERY:
            early = widen_project(line, flags_of(key), pieces[:3], 0, 3)
            box[key, AT_WIDE] = widen_project(line, flags_of(key), pieces[3:], 3, 1, early)
        else:
            box[key, AT_WIDE] = widen(line, flags_of(key), pieces)

    in_chan = lax.dynamic_slice_in_dim(flat_in, idx * width, width, 1)
    swapped = jnp.concatenate([info[1::-1], info[2:]])
    bits_of = {key: [second, first, *seq_bits[2:]] if kind & 1 else seq_bits for key, kind in KINDS.items()}
    feed_back(0)
    sum_start(DOWN, outer(line, flags_of(DOWN), act, cot))
    near_core(0)
    feed_back(1)
    sum_start(UP, outer(line, flags_of(UP), normed2, both(AT_PRE)))
    near_core(1)
    near_y(0)
    sum_second(DOWN)
    near_y(1)
    attend_back(0)
    sum_third(DOWN)
    attend_back(1)
    sum_second(UP)
    project()
    feed_out()
    ctx_parts_sum()
    lead_step()
    n1_parts_sum()
    sum_last(DOWN)
    sum_third(UP)
    sum_second(QUERY)
    sum_last(UP)
    state_step()
    pin(DOWN, 1)
    pin(UP, 2)
    pin(DOWN, 2)
    out_core()
    sum_third(QUERY)
    norm_back()
    row_sums()
    small_step(0)
    line.held.append(box[AT_SEEN][0])
    widen_step(DOWN)
    small_step(1)
    sum_last(QUERY)
    widen_step(UP)
    pin(UP, 3)
    input_step()
    pin(DOWN, 3)
    line.held.append(box[AT_SEEN][2])
    line.held.append(box[AT_SEEN][1])
    pin(QUERY, 2)
    small_step(2)
    out_add()
    join()
    widen_step(QUERY)
    outputs, down_grad, up_grad = box[AT_OUTPUTS], box[DOWN, AT_WIDE], box[UP, AT_WIDE]
    query_grad, key_grad, value_grad, out_grad_w = box[QUERY, AT_WIDE]
    input_grad = box[AT_INPUT_GRAD].reshape(seqs, block, width)
    small = box[AT_SMALL]
    return (
        outputs,
        input_grad,
        small[3 * NS + 1],
        query_grad,
        key_grad,
        value_grad,
        out_grad_w,
        small[3 * NS + 2 : 3 * NS + 2 + model // width].reshape(model),
        up_grad,
        down_grad,
        small[:NS],
        small[NS : 2 * NS],
        small[2 * NS : 3 * NS],
        small[3 * NS],
    )


def solution(mesh):
    in_specs = (
        P(None, SEQ, None),
        P(None, SEQ, None),
        P(),
        P(),
        P(None, TENSOR),
        P(None, TENSOR),
        P(None, TENSOR),
        P(TENSOR, None),
        P(),
        P(None, TENSOR),
        P(TENSOR, None),
        P(None, TENSOR),
        P(None, TENSOR),
        P(None, TENSOR),
        P(TENSOR),
    )
    out_specs = (
        P(None, SEQ, None),
        P(None, SEQ, TENSOR),
        P(TENSOR),
        P(None, TENSOR),
        P(None, TENSOR),
        P(None, TENSOR),
        P(TENSOR, None),
        P(),
        P(None, TENSOR),
        P(TENSOR, None),
        P(None, TENSOR),
        P(None, TENSOR),
        P(None, TENSOR),
        P(TENSOR),
    )
    return jax.shard_map(local, mesh=mesh, in_specs=in_specs, out_specs=out_specs, check_vma=False)
```

```python
import functools

import jax
import jax.numpy as jnp
from jax import lax
from jax.experimental import pallas as pl
from jax.experimental.pallas import tpu as pltpu
from jax.sharding import PartitionSpec as P

SEQ, TENSOR = "seq", "tensor"
HD = 128
NS = 16
CTX = 128
SUB = 8
EPS = 1e-06
F32 = jnp.float32
BF16 = jnp.bfloat16
MIB = 1 << 20


def nn(a, b):
    return lax.dot_general(a, b, (((1,), (0,)), ((), ())), preferred_element_type=F32)


def nt(a, b):
    return lax.dot_general(a, b, (((1,), (1,)), ((), ())), preferred_element_type=F32)


def tn(a, b):
    return lax.dot_general(a, b, (((0,), (0,)), ((), ())), preferred_element_type=F32)


def swap(value, axis, bit):
    count = lax.axis_size(axis)
    return lax.ppermute(value, axis, [(i, i ^ bit) for i in range(count)])


def low_bits(count):
    bit, out = 1, []
    while bit < count:
        out.append(bit)
        bit *= 2
    return out


def sds(shape, dtype):
    return jax.ShapeDtypeStruct(shape, dtype)


def vmem():
    return pl.BlockSpec(memory_space=pltpu.VMEM)


def smem():
    return pl.BlockSpec(memory_space=pltpu.SMEM)


class Line:
    def __init__(self):
        self.mark = None
        self.held = []

    def run(self, name, limit, kernel, args, in_specs, outs, grid=None, prefetch=(), scratch=(), after=None, hbm=(), aliases=None):
        args = [pltpu.with_memory_space_constraint(a, pltpu.HBM) if k in hbm else a for k, a in enumerate(args)]
        in_specs = list(in_specs)
        marks = [] if self.mark is None else [pltpu.with_memory_space_constraint(self.mark, pltpu.HBM)]
        others = [t for t in (after, *self.held) if t is not None]
        self.held = []
        count, extra = len(prefetch) + len(args), len(marks) + len(others)

        def body(*refs):
            return kernel(*refs[:count], *refs[count + extra : count + extra + len(outs)], *refs[count + extra + len(outs) + 1 :])

        in_specs += [pl.BlockSpec(memory_space=pltpu.HBM)] * len(marks) + [pl.BlockSpec(memory_space=pl.ANY)] * len(others)
        *got, self.mark = pl.pallas_call(
            body,
            grid_spec=pltpu.PrefetchScalarGridSpec(
                num_scalar_prefetch=len(prefetch),
                grid=grid or (1,),
                in_specs=in_specs,
                out_specs=[o[2] for o in outs] + [pl.BlockSpec(memory_space=pltpu.HBM)],
                scratch_shapes=list(scratch),
            ),
            out_shape=[pltpu.HBM(o[0], o[1]) if len(o) > 3 else sds(o[0], o[1]) for o in outs] + [pltpu.HBM((SUB, HD), F32)],
            compiler_params=pltpu.CompilerParams(vmem_limit_bytes=limit * MIB),
            cost_estimate=pl.CostEstimate(flops=1, bytes_accessed=1, transcendentals=0),
            input_output_aliases=aliases or {},
            name=name,
        )(*prefetch, *args, *marks, *others)
        return got


def full(shape):
    return pl.BlockSpec(shape, lambda *a: (0,) * len(shape))


def out_full(shape, dtype):
    return (shape, dtype, full(shape))


def lanes(tile):
    return slice(tile * HD, (tile + 1) * HD)


def spread(table, rows, factor=None):
    for n in range(NS):
        row = rows[n : n + 1, :]
        if factor is not None:
            row = jnp.exp(row * factor)
        table[n] = jnp.broadcast_to(row, table.shape[1:])


def scan_step(taps, decay_tab, jump_tab, state):
    tiles = len(taps)
    out = []
    for n in range(NS):
        for t in range(tiles):
            decay = decay_tab[n, :, lanes(t)]
            inner = taps[t][0]
            for tap in taps[t][1:]:
                inner = inner * decay + tap
            out.append(state[n * tiles + t] * jump_tab[n, :, lanes(t)] + inner)
    return tuple(out)


def taps_of(runs_ref, group, stride):
    return [[runs_ref[t, group * stride + i] for i in range(stride)] for t in range(runs_ref.shape[0])]


def segment_ends(state, rate, seg, seqs, seg_ref, end_ref, forward):
    per = SUB // seqs
    tiles = rate.shape[1] // HD
    place = lax.rem(lax.broadcasted_iota(jnp.int32, (SUB, HD), 0), per)
    away = ((per - 1 - place if forward else place) * seg).astype(F32)
    for n in range(NS):
        for t in range(tiles):
            now = state[n * tiles + t]
            seg_ref[n, :, lanes(t)] = now
            part = now * jnp.exp(-rate[n : n + 1, lanes(t)] * away)
            for s in range(seqs):
                end_ref[s, n : n + 1, lanes(t)] = jnp.sum(part[s * per : (s + 1) * per], 0, keepdims=True)


def entry_states(entry_ref, carry_ref, seg_ref, hop, seqs, forward):
    per = SUB // seqs
    for n in range(NS):
        step = hop[n : n + 1, :]
        for s in range(seqs):
            now = carry_ref[s, n : n + 1, :]
            for k in range(per):
                q = s * per + (k if forward else per - 1 - k)
                entry_ref[n, q : q + 1, :] = now
                if k < per - 1:
                    now = now * step + seg_ref[n, q : q + 1, :]


def read_state(ref):
    tiles = ref.shape[2] // HD
    return tuple(ref[n, :, lanes(t)] for n in range(NS) for t in range(tiles))


PACKED = 72
CHUNK = 256


def unpack(pack_ref):
    return (*(pack_ref[k * NS : (k + 1) * NS, :] for k in range(4)), pack_ref[4 * NS : 4 * NS + 1, :], pack_ref[4 * NS + 1 : 4 * NS + 2, :])


def enter_kernel(seqs, stride, info_ref, x_ref, xc_ref, gain_ref, rate_ref, low_ref, inv_ref, runs_ref, seg_ref, fin_ref, flat, decay_tab, jump_tab):
    step, width = x_ref.shape
    tiles, seg = runs_ref.shape[:2]
    piece = CHUNK
    gain = gain_ref[...]
    rate = rate_ref[...]

    @pl.when(pl.program_id(0) == 0)
    def _():
        spread(decay_tab, rate, -1.0)
        spread(jump_tab, rate, -float(stride))

    def norm(i, carry):
        at = pl.ds(pl.multiple_of(i * piece, piece), piece)
        x = x_ref[at, :].astype(F32)
        inv = lax.rsqrt(jnp.sum(x * x, -1, keepdims=True) * (1.0 / width) + EPS)
        low_ref[at, :] = (x * inv * gain).astype(BF16)
        inv_ref[at, :] = inv
        to = pl.ds(pl.multiple_of(pl.program_id(0) * step + i * piece, piece), piece)
        for t in range(tiles):
            flat[t, to, :] = xc_ref[at, lanes(t)].astype(F32) * inv
        return carry

    lax.fori_loop(0, step // piece, norm, 0)

    @pl.when(pl.program_id(0) == pl.num_programs(0) - 1)
    def _():
        def group(g, state):
            taps = []
            for t in range(tiles):
                row = [flat[t, pl.ds(g * stride + i, SUB, stride=seg), :] for i in range(stride)]
                for i in range(stride):
                    runs_ref[t, g * stride + i] = row[i]
                taps.append(row)
            return scan_step(taps, decay_tab, jump_tab, state)

        state = lax.fori_loop(0, seg // stride, group, (jnp.zeros((SUB, HD), F32),) * (NS * tiles))
        segment_ends(state, rate, seg, seqs, seg_ref, fin_ref, True)


def context_kernel(seqs, stride, runs_ref, seg_ref, carry_ref, pack_ref, ctx_ref, entry_ref, decay_tab, jump_tab, out_tab, flat):
    tiles, seg = runs_ref.shape[:2]
    rate, root, s_in, s_out, skip, gain = unpack(pack_ref)
    spread(decay_tab, rate, -1.0)
    spread(jump_tab, rate, -float(stride))
    spread(out_tab, root * s_in * s_out * gain)
    entry_states(entry_ref, carry_ref, seg_ref, jnp.exp(rate * (-float(seg))), seqs, True)
    skip = skip * gain
    groups = seg // stride

    def group(g, state):
        taps = taps_of(runs_ref, g, stride)
        state = scan_step(taps, decay_tab, jump_tab, state)
        for t in range(tiles):
            total = skip[:, lanes(t)] * taps[t][-1]
            for n in range(NS):
                total = total + out_tab[n, :, lanes(t)] * state[n * tiles + t]
            flat[t, pl.ds(g, SUB, stride=groups), :] = total
        return state

    lax.fori_loop(0, groups, group, read_state(entry_ref))
    for t in range(tiles):
        ctx_ref[:, lanes(t)] = flat[t].astype(BF16)


def lead_kernel(seqs, stride, near_ref, far_ref, pack_ref, grads_ref, segb_ref, lead_ref, flat, jump_tab):
    tiles, groups = grads_ref.shape[:2]
    for t in range(tiles):
        flat[t] = near_ref[:, lanes(t)].astype(F32) + far_ref[:, lanes(t)].astype(F32)
    rate = unpack(pack_ref)[0]
    spread(jump_tab, rate, -float(stride))

    def group(i, state):
        g = groups - 1 - i
        grads = [flat[t, pl.ds(g, SUB, stride=groups), :] for t in range(tiles)]
        for t in range(tiles):
            grads_ref[t, g] = grads[t]
        return tuple(state[n * tiles + t] * jump_tab[n, :, lanes(t)] + grads[t] for n in range(NS) for t in range(tiles))

    state = lax.fori_loop(0, groups, group, (jnp.zeros((SUB, HD), F32),) * (NS * tiles))
    segment_ends(state, rate, groups * stride, seqs, segb_ref, lead_ref, False)


def state_back_kernel(
    seqs, stride, runs_ref, grads_ref, entry_ref, segb_ref, carryb_ref, pack_ref, back_ref, packg_ref,
    decay_tab, jump_tab, tap_tab, entryb, states, backs, sums,
):
    tiles, seg = runs_ref.shape[:2]
    groups = seg // stride
    rate, root, s_in, s_out, skip, gain = unpack(pack_ref)
    coeff = root * s_in
    spread(decay_tab, rate, -1.0)
    spread(jump_tab, rate, -float(stride))
    both = coeff * s_out
    for i in range(stride):
        spread(tap_tab.at[i], both * jnp.exp(rate * (-float(stride - 1 - i))))
    entry_states(entryb, carryb_ref, segb_ref, jnp.exp(rate * (-float(seg))), seqs, False)
    zero = jnp.zeros((SUB, HD), F32)

    def forward(g, carry):
        state, totals = carry
        for n in range(NS):
            for t in range(tiles):
                states[g, n, :, lanes(t)] = state[n * tiles + t]
        taps = taps_of(runs_ref, g, stride)
        out = []
        for t in range(tiles):
            grad = grads_ref[t, g]
            out.append(totals[t] + grad * taps[t][-1])
            backs[t, g * stride + stride - 1] = grad * skip[:, lanes(t)]
            for i in range(stride - 1):
                backs[t, g * stride + i] = zero
        return scan_step(taps, decay_tab, jump_tab, state), tuple(out)

    last, totals = lax.fori_loop(0, groups, forward, (read_state(entry_ref), (zero,) * tiles))
    for n in range(NS):
        for t in range(tiles):
            states[groups, n, :, lanes(t)] = last[n * tiles + t]
    for t in range(tiles):
        packg_ref[3 * NS : 3 * NS + 1, lanes(t)] = jnp.sum(totals[t], 0, keepdims=True) * gain[:, lanes(t)]
    lot = 2
    kinds = stride + 2
    for t in range(tiles):
        for first in range(0, NS, lot):
            names = range(first, first + lot)

            def group(i, carry, t=t, names=names):
                g = groups - 1 - i
                adj, acc = carry
                grad = grads_ref[t, g]
                taps = [runs_ref[t, g * stride + i] for i in range(stride)]
                sums_b = [backs[t, g * stride + i] for i in range(stride)]
                new_adj, new_acc = [], []
                for k, n in enumerate(names):
                    now = adj[k] * jump_tab[n, :, lanes(t)] + grad
                    new_adj.append(now)
                    for i in range(stride):
                        sums_b[i] = sums_b[i] + tap_tab[i, n, :, lanes(t)] * now
                        new_acc.append(acc[k * kinds + i] + now * taps[i])
                    new_acc.append(acc[k * kinds + stride] + now * states[g, n, :, lanes(t)])
                    new_acc.append(acc[k * kinds + stride + 1] + grad * states[g + 1, n, :, lanes(t)])
                for i in range(stride):
                    backs[t, g * stride + i] = sums_b[i]
                return tuple(new_adj), tuple(new_acc)

            start = (tuple(entryb[n, :, lanes(t)] for n in names), (zero,) * (lot * kinds))
            _, acc = lax.fori_loop(0, groups, group, start, unroll=4)
            for k, n in enumerate(names):
                for j in range(kinds):
                    sums[j, n : n + 1, lanes(t)] = jnp.sum(acc[k * kinds + j], 0, keepdims=True)

    def spill(g, carry):
        for t in range(tiles):
            for i in range(stride):
                back_ref[t, pl.ds(g * stride + i, SUB, stride=seg), :] = backs[t, g * stride + i]
        return carry

    lax.fori_loop(0, groups, spill, 0)
    decay = jnp.exp(-rate)
    powers = [jnp.ones_like(rate)]
    for _ in range(stride):
        powers.append(powers[-1] * decay)
    coeff_grad = sum(powers[stride - 1 - i] * sums[i] for i in range(stride)) * s_out * gain
    decay_grad = float(stride) * powers[stride - 1] * sums[stride]
    for i in range(stride - 1):
        decay_grad = decay_grad + float(stride - 1 - i) * powers[stride - 2 - i] * sums[i]
    decay_grad = decay_grad * coeff * s_out * gain
    packg_ref[:NS, :] = coeff_grad * s_in * (decay * decay / root) - decay * decay_grad
    packg_ref[NS : 2 * NS, :] = coeff_grad * root
    packg_ref[2 * NS : 3 * NS, :] = coeff * gain * sums[stride + 1]


def carried(value, hop, axis, forward, seen=None):
    count = lax.axis_size(axis)
    mine = lax.axis_index(axis)
    whole = value
    enter = jnp.zeros_like(value)
    for bit in low_bits(count):
        other = swap(whole, axis, bit)
        if seen is not None:
            seen.append(other)
        upper = (mine & bit) != 0
        offset = mine & (bit - 1)
        if not forward:
            upper = jnp.logical_not(upper)
            offset = bit - 1 - offset
        enter = jnp.where(upper, enter + hop(offset) * other, enter)
        span = hop(bit)
        whole = jnp.where(upper, whole + span * other, other + span * whole)
    return enter


def qkv_kernel(x_ref, wq_ref, wk_ref, wv_ref, q_ref, k_ref, v_ref):
    x = x_ref[...]
    q_ref[...] = nn(x, wq_ref[...]).astype(BF16)
    k_ref[...] = nn(x, wk_ref[...]).astype(BF16)
    v_ref[...] = nn(x, wv_ref[...]).astype(BF16)


def masks(first, tile, block, stride):
    row = lax.broadcasted_iota(jnp.int32, (tile, CTX), 0) + first
    col = lax.broadcasted_iota(jnp.int32, (tile, CTX), 1)
    side = stride * col + (stride - 1) <= row
    row = lax.broadcasted_iota(jnp.int32, (tile, block), 0) + first
    col = lax.broadcasted_iota(jnp.int32, (tile, block), 1)
    return side, col <= row


def attend_kernel(parts, scale, idx_ref, q_ref, k_ref, v_ref, wk_ref, wv_ref, *rest):
    ctx_refs, (out_ref, kc_ref, vc_ref, lse_ref) = rest[:parts], rest[parts:]
    block, width = q_ref.shape
    stride = block // CTX
    idx = idx_ref[2]
    key_c = jnp.zeros((CTX, width), F32)
    val_c = jnp.zeros((CTX, width), F32)
    for p in range(parts):
        at = pl.ds(pl.multiple_of((idx ^ p) * width, width), width)
        key_c = key_c + nn(ctx_refs[p][...], wk_ref[at, :])
        val_c = val_c + nn(ctx_refs[p][...], wv_ref[at, :])
    kc_ref[...] = key_c.astype(BF16)
    vc_ref[...] = val_c.astype(BF16)
    tile = min(512, block)
    for h in range(width // HD):
        cols = slice(h * HD, (h + 1) * HD)
        for first in range(0, block, tile):
            seen = first + tile
            rows = slice(first, seen)
            q = q_ref[rows, cols]
            side_ok, own_ok = masks(first, tile, seen, stride)
            side = jnp.where(side_ok, nt(q, kc_ref[:, cols]), -1e30)
            own = jnp.where(own_ok, nt(q, k_ref[:seen, cols]), -1e30)
            top = jnp.maximum(jnp.max(side, -1, keepdims=True), jnp.max(own, -1, keepdims=True))
            side = jnp.exp((side - top) * scale)
            own = jnp.exp((own - top) * scale)
            total = jnp.sum(side, -1, keepdims=True) + jnp.sum(own, -1, keepdims=True)
            share = 1.0 / total
            got = nn((side * share).astype(BF16), vc_ref[:, cols]) + nn((own * share).astype(BF16), v_ref[:seen, cols])
            out_ref[rows, cols] = got.astype(BF16)
            lse_ref[rows, h : h + 1] = top * scale + jnp.log(total)


def attend_back_kernel(
    seq, scale, info_ref, mid_ref, near_ref, far_ref, grad_ref, gain_ref, wo_ref, q_ref, k_ref, v_ref, kc_ref, vc_ref, lse_ref,
    wq_ref, wk_ref, wv_ref,
    low_ref, slice_ref, gaing_ref, dq_ref, dk_ref, dv_ref, dkc_ref, dvc_ref, keep_ref, send_ref,
    n2_ref, full_ref, key_acc, val_acc, skey_acc, sval_acc,
):
    block, width = q_ref.shape
    model = mid_ref.shape[1]
    half = model // 2
    stride = block // CTX
    idx, mine, limit = info_ref[2], info_ref[3], info_ref[4 + seq]
    n2_ref[:, pl.ds(pl.multiple_of(mine * half, half), half)] = near_ref[...]
    n2_ref[:, pl.ds(pl.multiple_of((1 - mine) * half, half), half)] = far_ref[...]
    gain = gain_ref[...]
    step = CHUNK

    def norm(i, total):
        at = pl.ds(pl.multiple_of(i * step, step), step)
        mid = mid_ref[at, :]
        inv = lax.rsqrt(jnp.sum(mid * mid, -1, keepdims=True) * (1.0 / model) + EPS)
        hat = mid * inv
        n2 = n2_ref[at, :].astype(F32)
        prod = n2 * hat
        h2 = n2 * gain
        mean = jnp.sum(h2 * hat, -1, keepdims=True) * (1.0 / model)
        place = lax.broadcasted_iota(jnp.int32, (step, 1), 0) + i * step
        cot = jnp.where(place < limit, grad_ref[at, :].astype(F32), 0.0)
        grad = cot + inv * (h2 - hat * mean)
        full_ref[at, :] = grad
        low_ref[at, :] = grad.astype(BF16)
        return total + jnp.sum(prod, 0, keepdims=True)

    gaing_ref[...] = lax.fori_loop(0, block // step, norm, jnp.zeros((1, model), F32))
    slice_ref[...] = full_ref[:, pl.ds(pl.multiple_of(idx * width, width), width)]
    att_grad = nt(low_ref[...], wo_ref[...]).astype(BF16)
    tile = min(512, block)
    for h in range(width // HD):
        cols = slice(h * HD, (h + 1) * HD)
        for first in range(0, block, tile):
            seen = first + tile
            rows = slice(first, seen)
            q = q_ref[rows, cols]
            grad = att_grad[rows, cols]
            lse = lse_ref[rows, h : h + 1]
            side_ok, own_ok = masks(first, tile, seen, stride)
            kc, k = kc_ref[:, cols], k_ref[:seen, cols]
            side = jnp.exp(jnp.where(side_ok, nt(q, kc) * scale - lse, -1e30))
            own = jnp.exp(jnp.where(own_ok, nt(q, k) * scale - lse, -1e30))
            dside = nt(grad, vc_ref[:, cols])
            down = nt(grad, v_ref[:seen, cols])
            term = jnp.sum(side * dside, -1, keepdims=True) + jnp.sum(own * down, -1, keepdims=True)
            dside = (side * (dside - term)).astype(BF16)
            down = (own * (down - term)).astype(BF16)
            dq_ref[rows, cols] = ((nn(dside, kc) + nn(down, k)) * scale).astype(BF16)
            side = side.astype(BF16)
            own = own.astype(BF16)
            last = first + tile >= block
            fresh = first == 0
            for acc, score, right in (
                (skey_acc, dside, q),
                (sval_acc, side, grad),
            ):
                got = tn(score, right)
                acc[...] = got if fresh else acc[...] + got
            for acc, score, right in (
                (key_acc, down, q),
                (val_acc, own, grad),
            ):
                got = tn(score, right)
                if fresh:
                    acc[:seen, :] = got
                else:
                    acc[:first, :] = acc[:first, :] + got[:first]
                    acc[first:seen, :] = got[first:]
            if last:
                dk_ref[:, cols] = (key_acc[...] * scale).astype(BF16)
                dv_ref[:, cols] = val_acc[...].astype(BF16)
                dkc_ref[:, cols] = (skey_acc[...] * scale).astype(BF16)
                dvc_ref[:, cols] = sval_acc[...].astype(BF16)
    count = model // width
    for p in range(count):
        at = pl.ds(pl.multiple_of((idx ^ p) * width, width), width)
        wk, wv = wk_ref[at, :], wv_ref[at, :]
        ctx = nt(dkc_ref[...], wk) + nt(dvc_ref[...], wv)
        (send_ref if p % 2 else keep_ref)[p // 2, :CTX, :] = ctx.astype(BF16)
    for p in range(count):
        at = pl.ds(pl.multiple_of((idx ^ p) * width, width), width)
        own = nt(dq_ref[...], wq_ref[at, :]) + nt(dk_ref[...], wk_ref[at, :]) + nt(dv_ref[...], wv_ref[at, :])
        (send_ref if p % 2 else keep_ref)[p // 2, CTX:, :] = own.astype(BF16)


def feed_kernel(parts, tile, seq, info_ref, x_ref, grad_ref, gain_ref, up_ref, *rest):
    att_refs, wo_refs = rest[:parts], rest[parts : 2 * parts]
    mid_ref, n2_ref, act_ref, slope_ref, cot_ref = rest[2 * parts :]
    model = x_ref.shape[1]
    limit = info_ref[4 + seq]
    mid = x_ref[...].astype(F32)
    got = nn(att_refs[0][...], wo_refs[0][...])
    for p in range(1, parts):
        got = got + nn(att_refs[p][...], wo_refs[p][...])
    mid = mid + got
    mid_ref[...] = mid
    inv = lax.rsqrt(jnp.sum(mid * mid, -1, keepdims=True) * (1.0 / model) + EPS)
    n2_ref[...] = (mid * inv * gain_ref[...]).astype(BF16)
    place = lax.broadcasted_iota(jnp.int32, (tile, 1), 0) + pl.program_id(0) * tile
    cot_ref[...] = jnp.where(place < limit, grad_ref[...].astype(F32), 0.0).astype(BF16)
    pre = nn(n2_ref[...], up_ref[...])
    cdf = 0.5 * (1.0 + lax.erf(pre * 0.7071067811865476))
    pdf = jnp.exp(pre * pre * -0.5) * 0.3989422804014327
    act_ref[...] = (pre * cdf).astype(BF16)
    slope_ref[...] = (cdf + pre * pdf).astype(BF16)


def halves(info_ref, half):
    mine = info_ref[3]
    return (
        pl.ds(pl.multiple_of(mine * half, half), half),
        pl.ds(pl.multiple_of((1 - mine) * half, half), half),
    )


def feed_back_kernel(info_ref, cot_ref, slope_ref, up_ref, down_ref, pre_ref, keep_ref, send_ref):
    near, far = halves(info_ref, keep_ref.shape[1])
    pull = nt(cot_ref[...], down_ref[...])
    pre_ref[...] = (pull * slope_ref[...].astype(F32)).astype(BF16)
    send_ref[...] = nt(pre_ref[...], up_ref[far, :]).astype(BF16)
    keep_ref[...] = nt(pre_ref[...], up_ref[near, :]).astype(BF16)


def feed_out_kernel(seqs, steps, info_ref, *refs):
    down_ref, keep_ref, send_ref = refs[seqs:]
    near, far = halves(info_ref, keep_ref.shape[1])
    for s in range(seqs):

        @pl.when(pl.program_id(0) // steps == s)
        def _(s=s):
            send_ref[...] = nn(refs[s][...], down_ref[:, far]).astype(BF16)
            keep_ref[...] = nn(refs[s][...], down_ref[:, near]).astype(BF16)


def add_kernel(a_ref, b_ref, out_ref):
    out_ref[...] = (a_ref[...].astype(F32) + b_ref[...].astype(F32)).astype(BF16)


def add_pair_kernel(a_ref, b_ref, out0_ref, out1_ref):
    out0_ref[...] = (a_ref[0].astype(F32) + b_ref[0].astype(F32)).astype(BF16)
    out1_ref[...] = (a_ref[1].astype(F32) + b_ref[1].astype(F32)).astype(BF16)


def add_parts_kernel(pairs, count, start, size, *refs):
    keeps, gots, outs = refs[:count], refs[count : 2 * count], refs[2 * count :]
    at = slice(start, start + size)
    for m in range(pairs):
        for s in range(count):
            outs[m][s * size : (s + 1) * size, :] = (keeps[s][m, at].astype(F32) + gots[s][m, at].astype(F32)).astype(BF16)


def add_out_kernel(seqs, info_ref, *refs):
    mids, (a_ref, b_ref, out_ref) = refs[:seqs], refs[seqs:]
    near, _ = halves(info_ref, out_ref.shape[1])
    block = mids[0].shape[0]
    for s in range(seqs):
        at = slice(s * block, (s + 1) * block)
        total = a_ref[at, :].astype(F32) + b_ref[at, :].astype(F32)
        out_ref[at, :] = (mids[s][:, near] + total).astype(BF16)


def join_kernel(info_ref, near_ref, far_ref, out_ref):
    near, far = halves(info_ref, near_ref.shape[1])
    out_ref[:, near] = near_ref[...]
    out_ref[:, far] = far_ref[...]


def high(a, b, dims):
    return lax.dot_general(a, b, (dims, ((), ())), precision=lax.Precision.HIGHEST, preferred_element_type=F32)


def norm_back_kernel(seqs, near_ref, far_ref, back_ref, x_ref, inv_ref, pack_ref, packg_ref, *refs):
    gains, (h1_ref, small_ref, sums_ref) = refs[:seqs], refs[seqs:]
    tiles, rows = back_ref.shape[:2]
    width = tiles * HD
    gain = unpack(pack_ref)[5]
    step = 128
    ones = jnp.ones((SUB, HD), F32)

    def part(i, total):
        at = pl.ds(pl.multiple_of(i * step, step), step)
        inv = inv_ref[at, :]
        sums, out = 0.0, []
        for t in range(tiles):
            n1 = near_ref[at, lanes(t)].astype(F32) + far_ref[at, lanes(t)].astype(F32) + back_ref[t, at, :]
            hat = x_ref[at, lanes(t)].astype(F32) * inv
            prod = n1 * hat
            h1 = n1 * gain[:, lanes(t)]
            h1_ref[at, lanes(t)] = h1
            out.append(total[t] + jnp.sum(prod, 0, keepdims=True))
            sums = sums + h1 * hat
        sums_ref[:, at] = high(ones, sums, ((1,), (1,)))
        return tuple(out)

    total = lax.fori_loop(0, rows // step, part, (jnp.zeros((1, HD), F32),) * tiles)
    small_ref[...] = jnp.zeros(small_ref.shape, F32)
    small_ref[: 3 * NS + 1, :] = packg_ref[: 3 * NS + 1, :]
    for t in range(tiles):
        small_ref[3 * NS + 1 : 3 * NS + 2, lanes(t)] = total[t]
    gain2 = gains[0][...]
    for s in range(1, seqs):
        gain2 = gain2 + gains[s][...]
    for k in range(gain2.shape[1] // width):
        small_ref[3 * NS + 2 + k : 3 * NS + 3 + k, :] = gain2[:, k * width : (k + 1) * width]


def add_wide_kernel(a_ref, b_ref, out_ref):
    out_ref[...] = a_ref[...] + b_ref[...]


def add_wide(line, a, b):
    return line.run("add", 4, add_wide_kernel, (a, b), [full(a.shape)] * 2, [out_full(a.shape, F32)])[0]


def input_grad_kernel(seqs, model, h1_ref, sums_ref, more_ref, x_ref, inv_ref, *refs):
    mids, out_ref = refs[:seqs], refs[seqs]
    block, width = mids[0].shape
    step = 128
    ones = jnp.full((SUB, HD), 1.0 / (SUB * model), F32)
    for s in range(seqs):

        def part(i, carry, s=s):
            at = pl.ds(pl.multiple_of(s * block + i * step, step), step)
            here = pl.ds(pl.multiple_of(i * step, step), step)
            inv = inv_ref[at, :]
            mean = high(sums_ref[:, at] + more_ref[:, at], ones, ((0,), (0,)))
            for t in range(width // HD):
                hat = x_ref[at, lanes(t)].astype(F32) * inv
                grad = mids[s][here, lanes(t)] + inv * (h1_ref[at, lanes(t)] - hat * mean)
                out_ref[at, lanes(t)] = grad.astype(BF16)
            return carry

        lax.fori_loop(0, block // step, part, 0)


def add_pair(line, a, b):
    return line.run("add_pair", 8, add_pair_kernel, (a, b), [full(a.shape)] * 2, [out_full(a.shape[1:], BF16)] * 2)


def add_parts(line, keeps, gots, start, size):
    pairs, _, width = keeps[0].shape
    count = len(keeps)
    return line.run(
        "add_parts", 12,
        functools.partial(add_parts_kernel, pairs, count, start, size),
        (*keeps, *gots),
        [full(keeps[0].shape)] * (2 * count),
        [out_full((count * size, width), BF16)] * pairs,
    )


def add(line, a, b):
    return line.run("add", 8, add_kernel, (a, b), [full(a.shape)] * 2, [out_full(a.shape, BF16)])[0]


def quarter(info, far, step):
    return (info[0] ^ far) * 2 + (info[1] ^ step)


PIECES = ((0, 0), (0, 1), (1, 0), (1, 1))


def outer_kernel(pairs, info_ref, *refs):
    piece = refs[0].shape[1] // 4
    for far, step in PIECES:
        out_ref = refs[2 * pairs + far].at[step]
        at = pl.ds(pl.multiple_of(quarter(info_ref, far, step) * piece, piece), piece)
        total = tn(refs[0][:, at], refs[pairs][...])
        for p in range(1, pairs):
            total = total + tn(refs[p][:, at], refs[pairs + p][...])
        out_ref[...] = total.astype(BF16)


def outer(line, info, lefts, rights):
    rows, cols = lefts[0].shape[1], rights[0].shape[1]
    return line.run(
        "outer", 20,
        functools.partial(outer_kernel, len(lefts)),
        [*lefts, *rights],
        [full(a.shape) for a in (*lefts, *rights)],
        [out_full((2, rows // 4, cols), BF16)] * 2,
        prefetch=(info,),
    )


def project_grad_kernel(seqs, info_ref, *refs):
    refs = list(refs)

    def take(count):
        got = refs[:count]
        del refs[:count]
        return got

    (low_ref,) = take(1)
    mids = take(seqs)
    (ctx_ref,) = take(1)
    dqs, dks, dvs, dkcs, dvcs, atts = (take(seqs) for _ in range(6))
    block, width = dqs[0].shape
    quart = low_ref.shape[1] // 4 // width
    for far, step in PIECES:
        out_ref = refs[far].at[step]
        for i in range(quart):
            part = quarter(info_ref, far, step) * quart + i
            at = pl.ds(pl.multiple_of(part * width, width), width)
            rows = slice(i * width, (i + 1) * width)
            for k, (grads, more) in enumerate(((dqs, None), (dks, dkcs), (dvs, dvcs))):
                total = 0.0
                for s in range(seqs):
                    total = total + tn(low_ref[s * block : (s + 1) * block, at], grads[s][...])
                    if more is not None:
                        total = total + tn(ctx_ref[part ^ info_ref[2], s * CTX : (s + 1) * CTX, :], more[s][...])
                out_ref[rows, k * width : (k + 1) * width] = total.astype(BF16)
            total = 0.0
            for s in range(seqs):
                total = total + tn(atts[s][...], mids[s][:, at])
            out_ref[rows, 3 * width :] = total.astype(BF16)


def order(p, f):
    return quarter(f, p // 2, p % 2)


def widen_kernel(flags_ref, *refs):
    out_ref = refs[-1]
    for p in range(4):

        @pl.when(pl.program_id(0) == p)
        def _(p=p):
            start = 0
            for ref in refs[p : p + 1] if p < 3 else refs[3:-1]:
                size = ref.shape[0]
                out_ref[start : start + size, :] = ref[...].astype(F32)
                start += size


def widen(line, info, pieces):
    piece, cols = pieces[0].shape
    return line.run(
        "widen", 10,
        widen_kernel,
        pieces,
        [full(p.shape) for p in pieces],
        [((4 * piece, cols), F32, pl.BlockSpec((piece, cols), lambda p, f: (order(p, f), 0)))],
        grid=(4,),
        prefetch=(info,),
    )[0]


def widen_project_kernel(first, count, parts, flags_ref, *refs):
    pieces, outs = refs[:parts], refs[-4:]
    width = pieces[0].shape[1] // 4
    for p in range(count):

        @pl.when(pl.program_id(0) == p)
        def _(p=p):
            start = 0
            for ref in pieces[p : p + 1] if first + p < 3 else pieces[p:]:
                size = ref.shape[0]
                for k in range(3):
                    outs[k][start : start + size, :] = ref[:, k * width : (k + 1) * width].astype(F32)
                step = min(size, width)
                for j in range(0, size, step):
                    row = (start + j) % width
                    to = (start + j) // width * width
                    outs[3][row : row + step, to : to + width] = ref[j : j + step, 3 * width :].astype(F32)
                start += size


def widen_project(line, info, pieces, first, count, before=None):
    rows = pieces[0].shape[0] if first == 0 else sum(p.shape[0] for p in pieces)
    cols = pieces[0].shape[1]
    width = cols // 4
    given = pieces[first : first + count] if first == 0 else pieces
    before = before or []
    return line.run(
        "widen_project", 10,
        functools.partial(widen_project_kernel, first, count, len(given)),
        [*given, *before],
        [full(p.shape) for p in given] + [pl.BlockSpec(memory_space=pl.ANY)] * len(before),
        [((4 * rows, width), F32, pl.BlockSpec((rows, width), lambda p, f: (order(p + first, f), 0)))] * 3
        + [((width, 4 * rows), F32, pl.BlockSpec((width, rows), lambda p, f: (0, order(p + first, f))))],
        grid=(count,),
        prefetch=(info,),
        aliases={1 + len(given) + k: k for k in range(len(before))},
    )


def gather_parts(value, axis):
    parts = [value]
    for bit in reversed(low_bits(lax.axis_size(axis))):
        parts = parts + [None] * 0 + [swap(p, axis, bit) for p in parts]
    count = len(parts)
    order = [0]
    for bit in reversed(low_bits(count)):
        order = order + [k ^ bit for k in order]
    out = [None] * count
    for k, p in zip(order, parts):
        out[k] = p
    return out


def add_low(a, b):
    return (a.astype(F32) + b.astype(F32)).astype(BF16)


def scatter_parts(parts, axis):
    bits = low_bits(lax.axis_size(axis))[1:]
    for bit in bits:
        keep, send = parts[0::2], parts[1::2]
        got = [swap(p, axis, bit) for p in send]
        if bit != bits[-1]:
            parts = [add_low(a, b) for a, b in zip(keep, got)]
    return keep[0], got[0]


(
    AT_PRE, AT_N2_KEEP, AT_N2_SEND, AT_N2_CORE, AT_N2_Y, AT_N2_NEAR, AT_N2_FAR, AT_BACK, AT_GOT, AT_NEAR, AT_Z,
    AT_TOTAL, AT_HOP, AT_QUARTERS, AT_CTX, AT_N1, AT_LEAD, AT_SEEN, AT_CARRY, AT_STATE, AT_OUT_KEEP, AT_OUT_SEND,
    AT_OUT_CORE, AT_OUT_Y, AT_OUT_NEAR, AT_OUT_FAR, AT_OUTPUTS, AT_H1, AT_SMALL, AT_SUMS, AT_MORE, AT_SMALL_GOT,
    AT_INPUT_GRAD, AT_WIDE, DOWN, UP, QUERY, AT_CTX_STACK, VALUE,
) = range(39)
KINDS = {DOWN: 0, UP: 0, QUERY: 4}


def local(
    inputs, out_grad, lengths, norm_gain, query_weight, key_weight, value_weight, out_weight,
    mlp_gain, up_weight, down_weight, decay_rate, state_input, state_output, skip_gain,
):
    seqs, block, model = inputs.shape
    width = query_weight.shape[1]
    units = up_weight.shape[1]
    heads = width // HD
    tiles = width // HD
    stride = block // CTX
    scale = HD ** (-0.5)
    tensor_count = lax.axis_size(TENSOR)
    tensor_bits = low_bits(tensor_count)
    idx = lax.axis_index(TENSOR)
    place = lax.axis_index(SEQ)
    rows = seqs * block
    seg = rows // SUB
    half = model // 2
    pairs = tensor_count // 2
    small_rows = (3 * NS + 2 + tensor_count + 7) // 8 * 8
    seq_bits = low_bits(lax.axis_size(SEQ))
    first, second = seq_bits[:2]
    line = Line()
    info = jnp.concatenate(
        [
            jnp.stack([(place & first) // first, (place & second) // second, idx, idx & 1]).astype(jnp.int32),
            (lengths - place * block).astype(jnp.int32),
        ]
    )

    flat_in = inputs.reshape(rows, model)
    flat_grad = out_grad.reshape(rows, model)
    gain_all = norm_gain.reshape(1, model)
    gain2 = mlp_gain.reshape(1, model)
    gain_chan = lax.dynamic_slice_in_dim(norm_gain, idx * width, width, 0)
    gain_row = gain_chan.reshape(1, width)
    pack = jnp.concatenate(
        [
            decay_rate,
            jnp.sqrt(-jnp.expm1(-2.0 * decay_rate)),
            state_input,
            state_output,
            skip_gain.reshape(1, width),
            gain_row,
            jnp.zeros((PACKED - 4 * NS - 2, width), F32),
        ]
    )
    tab = pltpu.VMEM((NS, SUB, width), F32)
    state_shape = (NS, SUB, width)

    def hop(blocks):
        return jnp.exp(-decay_rate * (jnp.asarray(blocks, F32) * block))[None]

    def rows_of(s):
        return pl.BlockSpec((block, width), lambda *a, s=s: (s, 0))

    wo_parts = gather_parts(out_weight, TENSOR)

    tile = 256
    normed_low, inverse, runs, seg_end, final = line.run(
        "enter", 10,
        functools.partial(enter_kernel, seqs, stride),
        (flat_in, flat_in, gain_all, decay_rate),
        [
            pl.BlockSpec((256, model), lambda i, f: (i, 0)),
            pl.BlockSpec((256, width), lambda i, f: (i, f[2])),
            full((1, model)),
            full((NS, width)),
        ],
        [
            ((rows, model), BF16, pl.BlockSpec((256, model), lambda i, f: (i, 0))),
            ((rows, 1), F32, pl.BlockSpec((256, 1), lambda i, f: (i, 0)), True),
            (*out_full((tiles, seg, SUB, HD), F32), True),
            (*out_full(state_shape, F32), True),
            out_full((seqs, NS, width), F32),
        ],
        grid=(rows // 256,),
        prefetch=(info,),
        scratch=[pltpu.VMEM((tiles, rows, HD), F32), tab, tab],
        hbm=(0, 1, 2, 3),
    )
    carry_in = carried(final, hop, SEQ, True)

    ctx_low, entry = line.run(
        "context", 6,
        functools.partial(context_kernel, seqs, stride),
        (runs, seg_end, carry_in, pack),
        [full((tiles, seg, SUB, HD)), full(state_shape), full((seqs, NS, width)), full((PACKED, width))],
        [out_full((seqs * CTX, width), BF16), (*out_full(state_shape, F32), True)],
        scratch=[tab, tab, tab, pltpu.VMEM((tiles, seqs * CTX, HD), F32)],
        hbm=(0, 1),
    )
    ctx_parts = gather_parts(ctx_low, TENSOR)

    query, key_self, value_self = line.run(
        "qkv", 10,
        qkv_kernel,
        (normed_low, query_weight, key_weight, value_weight),
        [pl.BlockSpec((tile, model), lambda i: (i, 0))] + [full((model, width))] * 3,
        [((rows, width), BF16, pl.BlockSpec((tile, width), lambda i: (i, 0)))] * 3,
        grid=(rows // tile,),
        after=wo_parts[2] if tensor_count > 2 else None,
    )

    attended, key_ctx, value_ctx, log_sum, att_parts = [], [], [], [], []
    for s in range(seqs):
        a, kc, vc, ls = line.run(
            "attend", 12,
            functools.partial(attend_kernel, tensor_count, scale),
            (query, key_self, value_self, key_weight, value_weight, *ctx_parts),
            [rows_of(s)] * 3
            + [full((model, width))] * 2
            + [pl.BlockSpec((CTX, width), lambda *a, s=s: (s, 0))] * tensor_count,
            [
                out_full((block, width), BF16),
                out_full((CTX, width), BF16),
                out_full((CTX, width), BF16),
                out_full((block, heads), F32),
            ],
            prefetch=(info,),
        )
        attended.append(a)
        key_ctx.append(kc)
        value_ctx.append(vc)
        log_sum.append(ls)
        att_parts.append(gather_parts(a, TENSOR))

    steps = block // tile
    middle, normed2, act, slope, cot = ([] for _ in range(5))
    for s in range(seqs):

        def at(cols, s=s):
            return pl.BlockSpec((tile, cols), lambda i, f, s=s: (s * steps + i, 0))

        def own(cols):
            return pl.BlockSpec((tile, cols), lambda i, f: (i, 0))

        got = line.run(
            "feed", 30,
            functools.partial(feed_kernel, tensor_count, tile, s),
            (flat_in, flat_grad, gain2, up_weight, *att_parts[s], *wo_parts),
            [at(model), at(model), full((1, model)), full((model, units))]
            + [own(width)] * tensor_count
            + [full((width, model))] * tensor_count,
            [((block, c), t, own(c)) for c, t in ((model, F32), (model, BF16), (units, BF16), (units, BF16), (model, BF16))],
            grid=(steps,),
            prefetch=(info,),
        )
        for slot, value in zip((middle, normed2, act, slope, cot), got):
            slot.append(value)

    box = {}

    def feed_back(s):
        got = line.run(
            "feed_back", 18,
            feed_back_kernel,
            (cot[s], slope[s], up_weight, down_weight),
            [pl.BlockSpec((tile, model), lambda i, f: (i, 0)), pl.BlockSpec((tile, units), lambda i, f: (i, 0)), full((model, units)), full((units, model))],
            [((block, c), BF16, pl.BlockSpec((tile, c), lambda i, f: (i, 0))) for c in (units, half, half)],
            grid=(steps,),
            prefetch=(info,),
        )
        box[AT_PRE, s], box[AT_N2_KEEP, s] = got[:2]
        box[AT_N2_SEND, s] = swap(got[2], TENSOR, 1)

    def near_core(s):
        box[AT_N2_CORE, s] = add(line, box[AT_N2_KEEP, s], box[AT_N2_SEND, s])
        box[AT_N2_Y, s] = swap(box[AT_N2_CORE, s], TENSOR, tensor_bits[1])

    def near_y(s):
        total = add(line, box[AT_N2_CORE, s], box[AT_N2_Y, s])
        for bit in tensor_bits[2:]:
            total = add(line, total, swap(total, TENSOR, bit))
        box[AT_N2_NEAR, s] = total
        box[AT_N2_FAR, s] = swap(total, TENSOR, 1)

    def attend_back(s):
        outs = [
            ((block, model), BF16), ((block, width), F32), ((1, model), F32),
            ((block, width), BF16), ((block, width), BF16), ((block, width), BF16),
            ((CTX, width), BF16), ((CTX, width), BF16),
            ((pairs, CTX + block, width), BF16), ((pairs, CTX + block, width), BF16),
        ]
        got = line.run(
            "attend_back", 28,
            functools.partial(attend_back_kernel, s, scale),
            (middle[s], box[AT_N2_NEAR, s], box[AT_N2_FAR, s], flat_grad, gain2, out_weight, query, key_self, value_self, key_ctx[s], value_ctx[s], log_sum[s], query_weight, key_weight, value_weight),
            [full((block, model)), full((block, half)), full((block, half)), pl.BlockSpec((block, model), lambda *a, s=s: (s, 0)), full((1, model)), full((width, model))]
            + [rows_of(s)] * 3
            + [full((CTX, width))] * 2
            + [full((block, heads))]
            + [full((model, width))] * 3,
            [out_full(*o) for o in outs],
            prefetch=(info,),
            scratch=[pltpu.VMEM((block, model), BF16), pltpu.VMEM((block, model), F32)]
            + [pltpu.VMEM((block, HD), F32)] * 2
            + [pltpu.VMEM((CTX, HD), F32)] * 2,
        )

        box[AT_BACK, s] = got
        box[AT_GOT, s] = swap(got[9], TENSOR, 1)

    def backs(k):
        return [box[AT_BACK, s][k] for s in range(seqs)]

    def both(key):
        return [box[key, s] for s in range(seqs)]

    def sum_start(key, pieces):
        box[key] = pieces[0], swap(pieces[1], SEQ, bits_of[key][0])

    def sum_second(key):
        near, far = add_pair(line, *box[key])
        box[key, AT_NEAR], box[key, AT_Z] = near, swap(far, SEQ, bits_of[key][1])

    def sum_third(key):
        total = add(line, box[key, AT_NEAR], box[key, AT_Z])
        for bit in bits_of[key][2:-1]:
            total = add(line, total, swap(total, SEQ, bit))
        box[key, AT_TOTAL] = total
        if len(seq_bits) > 2:
            box[key, AT_HOP] = swap(total, SEQ, bits_of[key][-1])

    def sum_last(key):
        total = box[key, AT_TOTAL]
        if len(seq_bits) > 2:
            total = add(line, total, box[key, AT_HOP])
        one, two = bits_of[key][:2]
        across, along = swap(total, SEQ, two), swap(total, SEQ, one)
        last = KINDS[key] >> 1
        if last == 0:
            far = [swap(across, SEQ, one)]
        elif last == 1:
            far = [swap(along, SEQ, two)]
        else:
            size = total.shape[0] // 2
            far = [swap(across[:size], SEQ, one), swap(along[size:], SEQ, two)]
        box[key, AT_QUARTERS] = [total, across, along, *far]

    def pin(key, k):
        line.held.append(box[key, AT_QUARTERS][k])

    def project():
        mid_low, mid_slice, gain2_part, dq, dk, dv, dkc, dvc = (backs(k) for k in range(8))
        ctx_stack = jnp.stack(ctx_parts)
        ins = (normed_low, *mid_low, ctx_stack, *dq, *dk, *dv, *dkc, *dvc, *attended)
        got = (
            line.run(
                "project_grad", 28,
                functools.partial(project_grad_kernel, seqs),
                ins,
                [full(a.shape) for a in ins],
                [out_full((2, model // 4, 4 * width), BF16)] * 2,
                prefetch=(info,),
                )
        )
        sum_start(QUERY, got)

    def ctx_parts_sum():
        box[AT_CTX] = scatter_parts(add_parts(line, backs(8), both(AT_GOT), 0, CTX), TENSOR)

    def n1_parts_sum():
        box[AT_N1] = scatter_parts(add_parts(line, backs(8), both(AT_GOT), CTX, block), TENSOR)

    def lead_step():
        ctx_near, ctx_far = box[AT_CTX]
        ctx_grads, segb_end, lead = line.run(
            "lead", 4,
            functools.partial(lead_kernel, seqs, stride),
            (ctx_near, ctx_far, pack),
            [vmem()] * 3,
            [(*out_full((tiles, seqs * CTX // SUB, SUB, HD), F32), True), (state_shape, F32, vmem()), ((seqs, NS, width), F32, vmem())],
            scratch=[pltpu.VMEM((tiles, seqs * CTX, HD), F32), tab],
        )
        box[AT_LEAD] = ctx_grads, segb_end
        box[AT_SEEN] = []
        box[AT_CARRY] = carried(lead, hop, SEQ, False, box[AT_SEEN])

    def state_step():
        ctx_grads, segb_end = box[AT_LEAD]
        carry_back = box[AT_CARRY]
        box[AT_STATE] = line.run(
            "state_back", 10,
            functools.partial(state_back_kernel, seqs, stride),
            (runs, ctx_grads, entry, segb_end, carry_back, pack),
            [
                full((tiles, seg, SUB, HD)),
                full((tiles, seqs * CTX // SUB, SUB, HD)),
                full(state_shape),
                full(state_shape),
                full((seqs, NS, width)),
                full((PACKED, width)),
            ],
            [out_full((tiles, rows, HD), F32), out_full((small_rows, width), F32)],
            scratch=[
                tab,
                tab,
                pltpu.VMEM((stride, NS, SUB, width), F32),
                tab,
                pltpu.VMEM((seg // stride + 1, NS, SUB, width), F32),
                pltpu.VMEM((tiles, seg, SUB, HD), F32),
                pltpu.VMEM((stride + 2, NS, width), F32),
            ],
            hbm=(0, 1, 2),
        )

    def feed_out():
        got = line.run(
            "feed_out", 14,
            functools.partial(feed_out_kernel, seqs, steps),
            (*act, down_weight),
            [pl.BlockSpec((tile, units), lambda i, f, s=s: (jnp.clip(i - s * steps, 0, steps - 1), 0)) for s in range(seqs)]
            + [full((units, model))],
            [((rows, half), BF16, pl.BlockSpec((tile, half), lambda i, f: (i, 0)))] * 2,
            grid=(seqs * steps,),
            prefetch=(info,),
        )
        box[AT_OUT_KEEP], box[AT_OUT_SEND] = got[0], swap(got[1], TENSOR, 1)

    def out_core():
        total = add(line, box[AT_OUT_KEEP], box[AT_OUT_SEND])
        for bit in tensor_bits[1:-1]:
            total = add(line, total, swap(total, TENSOR, bit))
        box[AT_OUT_CORE], box[AT_OUT_Y] = total, swap(total, TENSOR, tensor_bits[-1])

    def out_add():
        box[AT_OUT_NEAR] = line.run(
            "add_out", 12,
            functools.partial(add_out_kernel, seqs),
            (*middle, box[AT_OUT_CORE], box[AT_OUT_Y]),
            [full((block, model))] * seqs + [full((rows, half))] * 2,
            [out_full((rows, half), BF16)],
            prefetch=(info,),
        )[0]
        box[AT_OUT_FAR] = swap(box[AT_OUT_NEAR], TENSOR, 1)

    def join():
        box[AT_OUTPUTS] = line.run(
            "join", 6,
            join_kernel,
            (box[AT_OUT_NEAR], box[AT_OUT_FAR]),
            [pl.BlockSpec((tile, half), lambda i, f: (i, 0))] * 2,
            [((rows, model), BF16, pl.BlockSpec((tile, model), lambda i, f: (i, 0)))],
            grid=(rows // tile,),
            prefetch=(info,),
        )[0].reshape(seqs, block, model)

    def norm_back():
        chan_grad, pack_grad = box[AT_STATE]
        h1, small, sums = line.run(
            "norm_back", 12,
            functools.partial(norm_back_kernel, seqs),
            (*box[AT_N1], chan_grad, in_chan, inverse, pack, pack_grad, *backs(2)),
            [full((rows, width))] * 2
            + [full((tiles, rows, HD)), full((rows, width)), full((rows, 1)), full((PACKED, width)), full((small_rows, width))]
            + [full((1, model))] * seqs,
            [out_full((rows, width), F32), out_full((small_rows, width), F32), out_full((SUB, rows), F32)],
        )
        box[AT_H1], box[AT_SMALL] = h1, small
        box[AT_SUMS], box[AT_MORE] = sums, swap(sums, TENSOR, 1)
        box[AT_SMALL_GOT] = swap(small, SEQ, seq_bits[0])

    def row_sums():
        total = add_wide(line, box[AT_SUMS], box[AT_MORE])
        for bit in tensor_bits[1:-1]:
            total = add_wide(line, total, swap(total, TENSOR, bit))
        box[AT_SUMS], box[AT_MORE] = total, swap(total, TENSOR, tensor_bits[-1])

    def input_step():
        box[AT_INPUT_GRAD] = line.run(
            "input_grad", 12,
            functools.partial(input_grad_kernel, seqs, model),
            (box[AT_H1], box[AT_SUMS], box[AT_MORE], in_chan, inverse, *backs(1)),
            [full((rows, width)), full((SUB, rows)), full((SUB, rows)), full((rows, width)), full((rows, 1))]
            + [full((block, width))] * seqs,
            [out_full((rows, width), BF16)],
        )[0]

    def small_step(k):
        total = add_wide(line, box[AT_SMALL], box[AT_SMALL_GOT])
        box[AT_SMALL] = total
        later = seq_bits[k + 1 :]
        if k == 2:
            for bit in later:
                box[AT_SMALL] = add_wide(line, box[AT_SMALL], swap(box[AT_SMALL], SEQ, bit))
        elif later:
            box[AT_SMALL_GOT] = swap(total, SEQ, later[0])

    def flags_of(key):
        return swapped if KINDS[key] & 1 else info

    def widen_step(key):
        pieces = box[key, AT_QUARTERS]
        if key == QUERY:
            early = widen_project(line, flags_of(key), pieces[:3], 0, 3)
            box[key, AT_WIDE] = widen_project(line, flags_of(key), pieces[3:], 3, 1, early)
        else:
            box[key, AT_WIDE] = widen(line, flags_of(key), pieces)

    in_chan = lax.dynamic_slice_in_dim(flat_in, idx * width, width, 1)
    swapped = jnp.concatenate([info[1::-1], info[2:]])
    bits_of = {key: [second, first, *seq_bits[2:]] if kind & 1 else seq_bits for key, kind in KINDS.items()}
    feed_back(0)
    sum_start(DOWN, outer(line, flags_of(DOWN), act, cot))
    near_core(0)
    feed_back(1)
    sum_start(UP, outer(line, flags_of(UP), normed2, both(AT_PRE)))
    near_core(1)
    near_y(0)
    sum_second(DOWN)
    near_y(1)
    attend_back(0)
    sum_third(DOWN)
    attend_back(1)
    sum_second(UP)
    project()
    feed_out()
    ctx_parts_sum()
    lead_step()
    n1_parts_sum()
    sum_last(DOWN)
    sum_third(UP)
    sum_second(QUERY)
    sum_last(UP)
    state_step()
    pin(DOWN, 1)
    pin(UP, 2)
    pin(DOWN, 2)
    out_core()
    sum_third(QUERY)
    norm_back()
    row_sums()
    small_step(0)
    line.held.append(box[AT_SEEN][0])
    widen_step(DOWN)
    small_step(1)
    sum_last(QUERY)
    widen_step(UP)
    pin(UP, 3)
    input_step()
    pin(DOWN, 3)
    line.held.append(box[AT_SEEN][2])
    line.held.append(box[AT_SEEN][1])
    pin(QUERY, 2)
    small_step(2)
    out_add()
    join()
    widen_step(QUERY)
    outputs, down_grad, up_grad = box[AT_OUTPUTS], box[DOWN, AT_WIDE], box[UP, AT_WIDE]
    query_grad, key_grad, value_grad, out_grad_w = box[QUERY, AT_WIDE]
    input_grad = box[AT_INPUT_GRAD].reshape(seqs, block, width)
    small = box[AT_SMALL]
    return (
        outputs,
        input_grad,
        small[3 * NS + 1],
        query_grad,
        key_grad,
        value_grad,
        out_grad_w,
        small[3 * NS + 2 : 3 * NS + 2 + model // width].reshape(model),
        up_grad,
        down_grad,
        small[:NS],
        small[NS : 2 * NS],
        small[2 * NS : 3 * NS],
        small[3 * NS],
    )


def solution(mesh):
    in_specs = (
        P(None, SEQ, None),
        P(None, SEQ, None),
        P(),
        P(),
        P(None, TENSOR),
        P(None, TENSOR),
        P(None, TENSOR),
        P(TENSOR, None),
        P(),
        P(None, TENSOR),
        P(TENSOR, None),
        P(None, TENSOR),
        P(None, TENSOR),
        P(None, TENSOR),
        P(TENSOR),
    )
    out_specs = (
        P(None, SEQ, None),
        P(None, SEQ, TENSOR),
        P(TENSOR),
        P(None, TENSOR),
        P(None, TENSOR),
        P(None, TENSOR),
        P(TENSOR, None),
        P(),
        P(None, TENSOR),
        P(TENSOR, None),
        P(None, TENSOR),
        P(None, TENSOR),
        P(None, TENSOR),
        P(TENSOR),
    )
    return jax.shard_map(local, mesh=mesh, in_specs=in_specs, out_specs=out_specs, check_vma=False)
```

```python
import functools

import jax
import jax.numpy as jnp
from jax import lax
from jax.experimental import pallas as pl
from jax.experimental.pallas import tpu as pltpu
from jax.sharding import PartitionSpec as P

SEQ, TENSOR = "seq", "tensor"
HD = 128
NS = 16
CTX = 128
SUB = 8
EPS = 1e-06
F32 = jnp.float32
BF16 = jnp.bfloat16
MIB = 1 << 20


def nn(a, b):
    return lax.dot_general(a, b, (((1,), (0,)), ((), ())), preferred_element_type=F32)


def nt(a, b):
    return lax.dot_general(a, b, (((1,), (1,)), ((), ())), preferred_element_type=F32)


def tn(a, b):
    return lax.dot_general(a, b, (((0,), (0,)), ((), ())), preferred_element_type=F32)


def swap(value, axis, bit):
    count = lax.axis_size(axis)
    return lax.ppermute(value, axis, [(i, i ^ bit) for i in range(count)])


def low_bits(count):
    bit, out = 1, []
    while bit < count:
        out.append(bit)
        bit *= 2
    return out


def sds(shape, dtype):
    return jax.ShapeDtypeStruct(shape, dtype)


def vmem():
    return pl.BlockSpec(memory_space=pltpu.VMEM)


def smem():
    return pl.BlockSpec(memory_space=pltpu.SMEM)


class Line:
    def __init__(self):
        self.mark = None
        self.held = []

    def run(self, name, limit, kernel, args, in_specs, outs, grid=None, prefetch=(), scratch=(), after=None, hbm=(), aliases=None):
        args = [pltpu.with_memory_space_constraint(a, pltpu.HBM) if k in hbm else a for k, a in enumerate(args)]
        in_specs = list(in_specs)
        marks = [] if self.mark is None else [pltpu.with_memory_space_constraint(self.mark, pltpu.HBM)]
        others = [pltpu.with_memory_space_constraint(t, pltpu.HBM) for t in (after, *self.held) if t is not None]
        self.held = []
        count, extra = len(prefetch) + len(args), len(marks) + len(others)

        def body(*refs):
            return kernel(*refs[:count], *refs[count + extra : count + extra + len(outs)], *refs[count + extra + len(outs) + 1 :])

        in_specs += [pl.BlockSpec(memory_space=pltpu.HBM)] * len(marks) + [pl.BlockSpec(memory_space=pl.ANY)] * len(others)
        *got, self.mark = pl.pallas_call(
            body,
            grid_spec=pltpu.PrefetchScalarGridSpec(
                num_scalar_prefetch=len(prefetch),
                grid=grid or (1,),
                in_specs=in_specs,
                out_specs=[o[2] for o in outs] + [pl.BlockSpec(memory_space=pltpu.HBM)],
                scratch_shapes=list(scratch),
            ),
            out_shape=[pltpu.HBM(o[0], o[1]) if len(o) > 3 else sds(o[0], o[1]) for o in outs] + [pltpu.HBM((SUB, HD), F32)],
            compiler_params=pltpu.CompilerParams(vmem_limit_bytes=limit * MIB),
            cost_estimate=pl.CostEstimate(flops=1, bytes_accessed=1, transcendentals=0),
            input_output_aliases=aliases or {},
            name=name,
        )(*prefetch, *args, *marks, *others)
        return got


def full(shape):
    return pl.BlockSpec(shape, lambda *a: (0,) * len(shape))


def out_full(shape, dtype):
    return (shape, dtype, full(shape))


def lanes(tile):
    return slice(tile * HD, (tile + 1) * HD)


def spread(table, rows, factor=None):
    for n in range(NS):
        row = rows[n : n + 1, :]
        if factor is not None:
            row = jnp.exp(row * factor)
        table[n] = jnp.broadcast_to(row, table.shape[1:])


def scan_step(taps, decay_tab, jump_tab, state):
    tiles = len(taps)
    out = []
    for n in range(NS):
        for t in range(tiles):
            decay = decay_tab[n, :, lanes(t)]
            inner = taps[t][0]
            for tap in taps[t][1:]:
                inner = inner * decay + tap
            out.append(state[n * tiles + t] * jump_tab[n, :, lanes(t)] + inner)
    return tuple(out)


def taps_of(runs_ref, group, stride):
    return [[runs_ref[t, group * stride + i] for i in range(stride)] for t in range(runs_ref.shape[0])]


def segment_ends(state, rate, seg, seqs, seg_ref, end_ref, forward):
    per = SUB // seqs
    tiles = rate.shape[1] // HD
    place = lax.rem(lax.broadcasted_iota(jnp.int32, (SUB, HD), 0), per)
    away = ((per - 1 - place if forward else place) * seg).astype(F32)
    for n in range(NS):
        for t in range(tiles):
            now = state[n * tiles + t]
            seg_ref[n, :, lanes(t)] = now
            part = now * jnp.exp(-rate[n : n + 1, lanes(t)] * away)
            for s in range(seqs):
                end_ref[s, n : n + 1, lanes(t)] = jnp.sum(part[s * per : (s + 1) * per], 0, keepdims=True)


def entry_states(entry_ref, carry_ref, seg_ref, hop, seqs, forward):
    per = SUB // seqs
    for n in range(NS):
        step = hop[n : n + 1, :]
        for s in range(seqs):
            now = carry_ref[s, n : n + 1, :]
            for k in range(per):
                q = s * per + (k if forward else per - 1 - k)
                entry_ref[n, q : q + 1, :] = now
                if k < per - 1:
                    now = now * step + seg_ref[n, q : q + 1, :]


def read_state(ref):
    tiles = ref.shape[2] // HD
    return tuple(ref[n, :, lanes(t)] for n in range(NS) for t in range(tiles))


PACKED = 72
CHUNK = 256


def unpack(pack_ref):
    return (*(pack_ref[k * NS : (k + 1) * NS, :] for k in range(4)), pack_ref[4 * NS : 4 * NS + 1, :], pack_ref[4 * NS + 1 : 4 * NS + 2, :])


def enter_kernel(seqs, stride, info_ref, x_ref, xc_ref, gain_ref, rate_ref, low_ref, inv_ref, runs_ref, seg_ref, fin_ref, flat, decay_tab, jump_tab):
    step, width = x_ref.shape
    tiles, seg = runs_ref.shape[:2]
    piece = CHUNK
    gain = gain_ref[...]
    rate = rate_ref[...]

    @pl.when(pl.program_id(0) == 0)
    def _():
        spread(decay_tab, rate, -1.0)
        spread(jump_tab, rate, -float(stride))

    def norm(i, carry):
        at = pl.ds(pl.multiple_of(i * piece, piece), piece)
        x = x_ref[at, :].astype(F32)
        inv = lax.rsqrt(jnp.sum(x * x, -1, keepdims=True) * (1.0 / width) + EPS)
        low_ref[at, :] = (x * inv * gain).astype(BF16)
        inv_ref[at, :] = inv
        to = pl.ds(pl.multiple_of(pl.program_id(0) * step + i * piece, piece), piece)
        for t in range(tiles):
            flat[t, to, :] = xc_ref[at, lanes(t)].astype(F32) * inv
        return carry

    lax.fori_loop(0, step // piece, norm, 0)

    @pl.when(pl.program_id(0) == pl.num_programs(0) - 1)
    def _():
        def group(g, state):
            taps = []
            for t in range(tiles):
                row = [flat[t, pl.ds(g * stride + i, SUB, stride=seg), :] for i in range(stride)]
                for i in range(stride):
                    runs_ref[t, g * stride + i] = row[i]
                taps.append(row)
            return scan_step(taps, decay_tab, jump_tab, state)

        state = lax.fori_loop(0, seg // stride, group, (jnp.zeros((SUB, HD), F32),) * (NS * tiles))
        segment_ends(state, rate, seg, seqs, seg_ref, fin_ref, True)


def context_kernel(seqs, stride, runs_ref, seg_ref, carry_ref, pack_ref, ctx_ref, entry_ref, decay_tab, jump_tab, out_tab, flat):
    tiles, seg = runs_ref.shape[:2]
    rate, root, s_in, s_out, skip, gain = unpack(pack_ref)
    spread(decay_tab, rate, -1.0)
    spread(jump_tab, rate, -float(stride))
    spread(out_tab, root * s_in * s_out * gain)
    entry_states(entry_ref, carry_ref, seg_ref, jnp.exp(rate * (-float(seg))), seqs, True)
    skip = skip * gain
    groups = seg // stride

    def group(g, state):
        taps = taps_of(runs_ref, g, stride)
        state = scan_step(taps, decay_tab, jump_tab, state)
        for t in range(tiles):
            total = skip[:, lanes(t)] * taps[t][-1]
            for n in range(NS):
                total = total + out_tab[n, :, lanes(t)] * state[n * tiles + t]
            flat[t, pl.ds(g, SUB, stride=groups), :] = total
        return state

    lax.fori_loop(0, groups, group, read_state(entry_ref))
    for t in range(tiles):
        ctx_ref[:, lanes(t)] = flat[t].astype(BF16)


def lead_kernel(seqs, stride, near_ref, far_ref, pack_ref, grads_ref, segb_ref, lead_ref, flat, jump_tab):
    tiles, groups = grads_ref.shape[:2]
    for t in range(tiles):
        flat[t] = near_ref[:, lanes(t)].astype(F32) + far_ref[:, lanes(t)].astype(F32)
    rate = unpack(pack_ref)[0]
    spread(jump_tab, rate, -float(stride))

    def group(i, state):
        g = groups - 1 - i
        grads = [flat[t, pl.ds(g, SUB, stride=groups), :] for t in range(tiles)]
        for t in range(tiles):
            grads_ref[t, g] = grads[t]
        return tuple(state[n * tiles + t] * jump_tab[n, :, lanes(t)] + grads[t] for n in range(NS) for t in range(tiles))

    state = lax.fori_loop(0, groups, group, (jnp.zeros((SUB, HD), F32),) * (NS * tiles))
    segment_ends(state, rate, groups * stride, seqs, segb_ref, lead_ref, False)


def state_back_kernel(
    seqs, stride, runs_ref, grads_ref, entry_ref, segb_ref, carryb_ref, pack_ref, back_ref, packg_ref,
    decay_tab, jump_tab, tap_tab, entryb, states, backs, sums,
):
    tiles, seg = runs_ref.shape[:2]
    groups = seg // stride
    rate, root, s_in, s_out, skip, gain = unpack(pack_ref)
    coeff = root * s_in
    spread(decay_tab, rate, -1.0)
    spread(jump_tab, rate, -float(stride))
    both = coeff * s_out
    for i in range(stride):
        spread(tap_tab.at[i], both * jnp.exp(rate * (-float(stride - 1 - i))))
    entry_states(entryb, carryb_ref, segb_ref, jnp.exp(rate * (-float(seg))), seqs, False)
    zero = jnp.zeros((SUB, HD), F32)

    def forward(g, carry):
        state, totals = carry
        for n in range(NS):
            for t in range(tiles):
                states[g, n, :, lanes(t)] = state[n * tiles + t]
        taps = taps_of(runs_ref, g, stride)
        out = []
        for t in range(tiles):
            grad = grads_ref[t, g]
            out.append(totals[t] + grad * taps[t][-1])
            backs[t, g * stride + stride - 1] = grad * skip[:, lanes(t)]
            for i in range(stride - 1):
                backs[t, g * stride + i] = zero
        return scan_step(taps, decay_tab, jump_tab, state), tuple(out)

    last, totals = lax.fori_loop(0, groups, forward, (read_state(entry_ref), (zero,) * tiles))
    for n in range(NS):
        for t in range(tiles):
            states[groups, n, :, lanes(t)] = last[n * tiles + t]
    for t in range(tiles):
        packg_ref[3 * NS : 3 * NS + 1, lanes(t)] = jnp.sum(totals[t], 0, keepdims=True) * gain[:, lanes(t)]
    lot = 2
    kinds = stride + 2
    for t in range(tiles):
        for first in range(0, NS, lot):
            names = range(first, first + lot)

            def group(i, carry, t=t, names=names):
                g = groups - 1 - i
                adj, acc = carry
                grad = grads_ref[t, g]
                taps = [runs_ref[t, g * stride + i] for i in range(stride)]
                sums_b = [backs[t, g * stride + i] for i in range(stride)]
                new_adj, new_acc = [], []
                for k, n in enumerate(names):
                    now = adj[k] * jump_tab[n, :, lanes(t)] + grad
                    new_adj.append(now)
                    for i in range(stride):
                        sums_b[i] = sums_b[i] + tap_tab[i, n, :, lanes(t)] * now
                        new_acc.append(acc[k * kinds + i] + now * taps[i])
                    new_acc.append(acc[k * kinds + stride] + now * states[g, n, :, lanes(t)])
                    new_acc.append(acc[k * kinds + stride + 1] + grad * states[g + 1, n, :, lanes(t)])
                for i in range(stride):
                    backs[t, g * stride + i] = sums_b[i]
                return tuple(new_adj), tuple(new_acc)

            start = (tuple(entryb[n, :, lanes(t)] for n in names), (zero,) * (lot * kinds))
            _, acc = lax.fori_loop(0, groups, group, start, unroll=4)
            for k, n in enumerate(names):
                for j in range(kinds):
                    sums[j, n : n + 1, lanes(t)] = jnp.sum(acc[k * kinds + j], 0, keepdims=True)

    def spill(g, carry):
        for t in range(tiles):
            for i in range(stride):
                back_ref[t, pl.ds(g * stride + i, SUB, stride=seg), :] = backs[t, g * stride + i]
        return carry

    lax.fori_loop(0, groups, spill, 0)
    decay = jnp.exp(-rate)
    powers = [jnp.ones_like(rate)]
    for _ in range(stride):
        powers.append(powers[-1] * decay)
    coeff_grad = sum(powers[stride - 1 - i] * sums[i] for i in range(stride)) * s_out * gain
    decay_grad = float(stride) * powers[stride - 1] * sums[stride]
    for i in range(stride - 1):
        decay_grad = decay_grad + float(stride - 1 - i) * powers[stride - 2 - i] * sums[i]
    decay_grad = decay_grad * coeff * s_out * gain
    packg_ref[:NS, :] = coeff_grad * s_in * (decay * decay / root) - decay * decay_grad
    packg_ref[NS : 2 * NS, :] = coeff_grad * root
    packg_ref[2 * NS : 3 * NS, :] = coeff * gain * sums[stride + 1]


def carried(value, hop, axis, forward, seen=None):
    count = lax.axis_size(axis)
    mine = lax.axis_index(axis)
    whole = value
    enter = jnp.zeros_like(value)
    for bit in low_bits(count):
        other = swap(whole, axis, bit)
        if seen is not None:
            seen.append(other)
        upper = (mine & bit) != 0
        offset = mine & (bit - 1)
        if not forward:
            upper = jnp.logical_not(upper)
            offset = bit - 1 - offset
        enter = jnp.where(upper, enter + hop(offset) * other, enter)
        span = hop(bit)
        whole = jnp.where(upper, whole + span * other, other + span * whole)
    return enter


def qkv_kernel(x_ref, wq_ref, wk_ref, wv_ref, q_ref, k_ref, v_ref):
    x = x_ref[...]
    q_ref[...] = nn(x, wq_ref[...]).astype(BF16)
    k_ref[...] = nn(x, wk_ref[...]).astype(BF16)
    v_ref[...] = nn(x, wv_ref[...]).astype(BF16)


def masks(first, tile, block, stride):
    row = lax.broadcasted_iota(jnp.int32, (tile, CTX), 0) + first
    col = lax.broadcasted_iota(jnp.int32, (tile, CTX), 1)
    side = stride * col + (stride - 1) <= row
    row = lax.broadcasted_iota(jnp.int32, (tile, block), 0) + first
    col = lax.broadcasted_iota(jnp.int32, (tile, block), 1)
    return side, col <= row


def attend_kernel(parts, scale, idx_ref, q_ref, k_ref, v_ref, wk_ref, wv_ref, *rest):
    ctx_refs, (out_ref, kc_ref, vc_ref, lse_ref) = rest[:parts], rest[parts:]
    block, width = q_ref.shape
    stride = block // CTX
    idx = idx_ref[2]
    key_c = jnp.zeros((CTX, width), F32)
    val_c = jnp.zeros((CTX, width), F32)
    for p in range(parts):
        at = pl.ds(pl.multiple_of((idx ^ p) * width, width), width)
        key_c = key_c + nn(ctx_refs[p][...], wk_ref[at, :])
        val_c = val_c + nn(ctx_refs[p][...], wv_ref[at, :])
    kc_ref[...] = key_c.astype(BF16)
    vc_ref[...] = val_c.astype(BF16)
    tile = min(512, block)
    for h in range(width // HD):
        cols = slice(h * HD, (h + 1) * HD)
        for first in range(0, block, tile):
            seen = first + tile
            rows = slice(first, seen)
            q = q_ref[rows, cols]
            side_ok, own_ok = masks(first, tile, seen, stride)
            side = jnp.where(side_ok, nt(q, kc_ref[:, cols]), -1e30)
            own = jnp.where(own_ok, nt(q, k_ref[:seen, cols]), -1e30)
            top = jnp.maximum(jnp.max(side, -1, keepdims=True), jnp.max(own, -1, keepdims=True))
            side = jnp.exp((side - top) * scale)
            own = jnp.exp((own - top) * scale)
            total = jnp.sum(side, -1, keepdims=True) + jnp.sum(own, -1, keepdims=True)
            share = 1.0 / total
            got = nn((side * share).astype(BF16), vc_ref[:, cols]) + nn((own * share).astype(BF16), v_ref[:seen, cols])
            out_ref[rows, cols] = got.astype(BF16)
            lse_ref[rows, h : h + 1] = top * scale + jnp.log(total)


def attend_back_kernel(
    seq, scale, info_ref, mid_ref, near_ref, far_ref, grad_ref, gain_ref, wo_ref, q_ref, k_ref, v_ref, kc_ref, vc_ref, lse_ref,
    wq_ref, wk_ref, wv_ref,
    low_ref, slice_ref, gaing_ref, dq_ref, dk_ref, dv_ref, dkc_ref, dvc_ref, keep_ref, send_ref,
    n2_ref, full_ref, key_acc, val_acc, skey_acc, sval_acc,
):
    block, width = q_ref.shape
    model = mid_ref.shape[1]
    half = model // 2
    stride = block // CTX
    idx, mine, limit = info_ref[2], info_ref[3], info_ref[4 + seq]
    n2_ref[:, pl.ds(pl.multiple_of(mine * half, half), half)] = near_ref[...]
    n2_ref[:, pl.ds(pl.multiple_of((1 - mine) * half, half), half)] = far_ref[...]
    gain = gain_ref[...]
    step = CHUNK

    def norm(i, total):
        at = pl.ds(pl.multiple_of(i * step, step), step)
        mid = mid_ref[at, :]
        inv = lax.rsqrt(jnp.sum(mid * mid, -1, keepdims=True) * (1.0 / model) + EPS)
        hat = mid * inv
        n2 = n2_ref[at, :].astype(F32)
        prod = n2 * hat
        h2 = n2 * gain
        mean = jnp.sum(h2 * hat, -1, keepdims=True) * (1.0 / model)
        place = lax.broadcasted_iota(jnp.int32, (step, 1), 0) + i * step
        cot = jnp.where(place < limit, grad_ref[at, :].astype(F32), 0.0)
        grad = cot + inv * (h2 - hat * mean)
        full_ref[at, :] = grad
        low_ref[at, :] = grad.astype(BF16)
        return total + jnp.sum(prod, 0, keepdims=True)

    gaing_ref[...] = lax.fori_loop(0, block // step, norm, jnp.zeros((1, model), F32))
    slice_ref[...] = full_ref[:, pl.ds(pl.multiple_of(idx * width, width), width)]
    att_grad = nt(low_ref[...], wo_ref[...]).astype(BF16)
    tile = min(512, block)
    for h in range(width // HD):
        cols = slice(h * HD, (h + 1) * HD)
        for first in range(0, block, tile):
            seen = first + tile
            rows = slice(first, seen)
            q = q_ref[rows, cols]
            grad = att_grad[rows, cols]
            lse = lse_ref[rows, h : h + 1]
            side_ok, own_ok = masks(first, tile, seen, stride)
            kc, k = kc_ref[:, cols], k_ref[:seen, cols]
            side = jnp.exp(jnp.where(side_ok, nt(q, kc) * scale - lse, -1e30))
            own = jnp.exp(jnp.where(own_ok, nt(q, k) * scale - lse, -1e30))
            dside = nt(grad, vc_ref[:, cols])
            down = nt(grad, v_ref[:seen, cols])
            term = jnp.sum(side * dside, -1, keepdims=True) + jnp.sum(own * down, -1, keepdims=True)
            dside = (side * (dside - term)).astype(BF16)
            down = (own * (down - term)).astype(BF16)
            dq_ref[rows, cols] = ((nn(dside, kc) + nn(down, k)) * scale).astype(BF16)
            side = side.astype(BF16)
            own = own.astype(BF16)
            last = first + tile >= block
            fresh = first == 0
            for acc, score, right in (
                (skey_acc, dside, q),
                (sval_acc, side, grad),
            ):
                got = tn(score, right)
                acc[...] = got if fresh else acc[...] + got
            for acc, score, right in (
                (key_acc, down, q),
                (val_acc, own, grad),
            ):
                got = tn(score, right)
                if fresh:
                    acc[:seen, :] = got
                else:
                    acc[:first, :] = acc[:first, :] + got[:first]
                    acc[first:seen, :] = got[first:]
            if last:
                dk_ref[:, cols] = (key_acc[...] * scale).astype(BF16)
                dv_ref[:, cols] = val_acc[...].astype(BF16)
                dkc_ref[:, cols] = (skey_acc[...] * scale).astype(BF16)
                dvc_ref[:, cols] = sval_acc[...].astype(BF16)
    count = model // width
    for p in range(count):
        at = pl.ds(pl.multiple_of((idx ^ p) * width, width), width)
        wk, wv = wk_ref[at, :], wv_ref[at, :]
        ctx = nt(dkc_ref[...], wk) + nt(dvc_ref[...], wv)
        (send_ref if p % 2 else keep_ref)[p // 2, :CTX, :] = ctx.astype(BF16)
    for p in range(count):
        at = pl.ds(pl.multiple_of((idx ^ p) * width, width), width)
        own = nt(dq_ref[...], wq_ref[at, :]) + nt(dk_ref[...], wk_ref[at, :]) + nt(dv_ref[...], wv_ref[at, :])
        (send_ref if p % 2 else keep_ref)[p // 2, CTX:, :] = own.astype(BF16)


def feed_kernel(parts, tile, seq, info_ref, x_ref, grad_ref, gain_ref, up_ref, *rest):
    att_refs, wo_refs = rest[:parts], rest[parts : 2 * parts]
    mid_ref, n2_ref, act_ref, slope_ref, cot_ref = rest[2 * parts :]
    model = x_ref.shape[1]
    limit = info_ref[4 + seq]
    mid = x_ref[...].astype(F32)
    got = nn(att_refs[0][...], wo_refs[0][...])
    for p in range(1, parts):
        got = got + nn(att_refs[p][...], wo_refs[p][...])
    mid = mid + got
    mid_ref[...] = mid
    inv = lax.rsqrt(jnp.sum(mid * mid, -1, keepdims=True) * (1.0 / model) + EPS)
    n2_ref[...] = (mid * inv * gain_ref[...]).astype(BF16)
    place = lax.broadcasted_iota(jnp.int32, (tile, 1), 0) + pl.program_id(0) * tile
    cot_ref[...] = jnp.where(place < limit, grad_ref[...].astype(F32), 0.0).astype(BF16)
    pre = nn(n2_ref[...], up_ref[...])
    cdf = 0.5 * (1.0 + lax.erf(pre * 0.7071067811865476))
    pdf = jnp.exp(pre * pre * -0.5) * 0.3989422804014327
    act_ref[...] = (pre * cdf).astype(BF16)
    slope_ref[...] = (cdf + pre * pdf).astype(BF16)


def halves(info_ref, half):
    mine = info_ref[3]
    return (
        pl.ds(pl.multiple_of(mine * half, half), half),
        pl.ds(pl.multiple_of((1 - mine) * half, half), half),
    )


def feed_back_kernel(info_ref, cot_ref, slope_ref, up_ref, down_ref, pre_ref, keep_ref, send_ref):
    near, far = halves(info_ref, keep_ref.shape[1])
    pull = nt(cot_ref[...], down_ref[...])
    pre_ref[...] = (pull * slope_ref[...].astype(F32)).astype(BF16)
    send_ref[...] = nt(pre_ref[...], up_ref[far, :]).astype(BF16)
    keep_ref[...] = nt(pre_ref[...], up_ref[near, :]).astype(BF16)


def feed_out_kernel(seqs, steps, info_ref, *refs):
    down_ref, keep_ref, send_ref = refs[seqs:]
    near, far = halves(info_ref, keep_ref.shape[1])
    for s in range(seqs):

        @pl.when(pl.program_id(0) // steps == s)
        def _(s=s):
            send_ref[...] = nn(refs[s][...], down_ref[:, far]).astype(BF16)
            keep_ref[...] = nn(refs[s][...], down_ref[:, near]).astype(BF16)


def add_kernel(a_ref, b_ref, out_ref):
    out_ref[...] = (a_ref[...].astype(F32) + b_ref[...].astype(F32)).astype(BF16)


def add_pair_kernel(a_ref, b_ref, out0_ref, out1_ref):
    out0_ref[...] = (a_ref[0].astype(F32) + b_ref[0].astype(F32)).astype(BF16)
    out1_ref[...] = (a_ref[1].astype(F32) + b_ref[1].astype(F32)).astype(BF16)


def add_parts_kernel(pairs, count, start, size, *refs):
    keeps, gots, outs = refs[:count], refs[count : 2 * count], refs[2 * count :]
    at = slice(start, start + size)
    for m in range(pairs):
        for s in range(count):
            outs[m][s * size : (s + 1) * size, :] = (keeps[s][m, at].astype(F32) + gots[s][m, at].astype(F32)).astype(BF16)


def add_out_kernel(seqs, info_ref, *refs):
    mids, (a_ref, b_ref, out_ref) = refs[:seqs], refs[seqs:]
    near, _ = halves(info_ref, out_ref.shape[1])
    block = mids[0].shape[0]
    for s in range(seqs):
        at = slice(s * block, (s + 1) * block)
        total = a_ref[at, :].astype(F32) + b_ref[at, :].astype(F32)
        out_ref[at, :] = (mids[s][:, near] + total).astype(BF16)


def join_kernel(info_ref, near_ref, far_ref, out_ref):
    near, far = halves(info_ref, near_ref.shape[1])
    out_ref[:, near] = near_ref[...]
    out_ref[:, far] = far_ref[...]


def high(a, b, dims):
    return lax.dot_general(a, b, (dims, ((), ())), precision=lax.Precision.HIGHEST, preferred_element_type=F32)


def norm_back_kernel(seqs, near_ref, far_ref, back_ref, x_ref, inv_ref, pack_ref, packg_ref, *refs):
    gains, (h1_ref, small_ref, sums_ref) = refs[:seqs], refs[seqs:]
    tiles, rows = back_ref.shape[:2]
    width = tiles * HD
    gain = unpack(pack_ref)[5]
    step = 128
    ones = jnp.ones((SUB, HD), F32)

    def part(i, total):
        at = pl.ds(pl.multiple_of(i * step, step), step)
        inv = inv_ref[at, :]
        sums, out = 0.0, []
        for t in range(tiles):
            n1 = near_ref[at, lanes(t)].astype(F32) + far_ref[at, lanes(t)].astype(F32) + back_ref[t, at, :]
            hat = x_ref[at, lanes(t)].astype(F32) * inv
            prod = n1 * hat
            h1 = n1 * gain[:, lanes(t)]
            h1_ref[at, lanes(t)] = h1
            out.append(total[t] + jnp.sum(prod, 0, keepdims=True))
            sums = sums + h1 * hat
        sums_ref[:, at] = high(ones, sums, ((1,), (1,)))
        return tuple(out)

    total = lax.fori_loop(0, rows // step, part, (jnp.zeros((1, HD), F32),) * tiles)
    small_ref[...] = jnp.zeros(small_ref.shape, F32)
    small_ref[: 3 * NS + 1, :] = packg_ref[: 3 * NS + 1, :]
    for t in range(tiles):
        small_ref[3 * NS + 1 : 3 * NS + 2, lanes(t)] = total[t]
    gain2 = gains[0][...]
    for s in range(1, seqs):
        gain2 = gain2 + gains[s][...]
    for k in range(gain2.shape[1] // width):
        small_ref[3 * NS + 2 + k : 3 * NS + 3 + k, :] = gain2[:, k * width : (k + 1) * width]


def add_wide_kernel(a_ref, b_ref, out_ref):
    out_ref[...] = a_ref[...] + b_ref[...]


def add_wide(line, a, b):
    return line.run("add", 4, add_wide_kernel, (a, b), [full(a.shape)] * 2, [out_full(a.shape, F32)])[0]


def input_grad_kernel(seqs, model, h1_ref, sums_ref, more_ref, x_ref, inv_ref, *refs):
    mids, out_ref = refs[:seqs], refs[seqs]
    block, width = mids[0].shape
    step = 128
    ones = jnp.full((SUB, HD), 1.0 / (SUB * model), F32)
    for s in range(seqs):

        def part(i, carry, s=s):
            at = pl.ds(pl.multiple_of(s * block + i * step, step), step)
            here = pl.ds(pl.multiple_of(i * step, step), step)
            inv = inv_ref[at, :]
            mean = high(sums_ref[:, at] + more_ref[:, at], ones, ((0,), (0,)))
            for t in range(width // HD):
                hat = x_ref[at, lanes(t)].astype(F32) * inv
                grad = mids[s][here, lanes(t)] + inv * (h1_ref[at, lanes(t)] - hat * mean)
                out_ref[at, lanes(t)] = grad.astype(BF16)
            return carry

        lax.fori_loop(0, block // step, part, 0)


def add_pair(line, a, b):
    return line.run("add_pair", 8, add_pair_kernel, (a, b), [full(a.shape)] * 2, [out_full(a.shape[1:], BF16)] * 2)


def add_parts(line, keeps, gots, start, size):
    pairs, _, width = keeps[0].shape
    count = len(keeps)
    return line.run(
        "add_parts", 12,
        functools.partial(add_parts_kernel, pairs, count, start, size),
        (*keeps, *gots),
        [full(keeps[0].shape)] * (2 * count),
        [out_full((count * size, width), BF16)] * pairs,
    )


def add(line, a, b):
    return line.run("add", 8, add_kernel, (a, b), [full(a.shape)] * 2, [out_full(a.shape, BF16)])[0]


def quarter(info, far, step):
    return (info[0] ^ far) * 2 + (info[1] ^ step)


PIECES = ((0, 0), (0, 1), (1, 0), (1, 1))


def outer_kernel(pairs, info_ref, *refs):
    piece = refs[0].shape[1] // 4
    for far, step in PIECES:
        out_ref = refs[2 * pairs + far].at[step]
        at = pl.ds(pl.multiple_of(quarter(info_ref, far, step) * piece, piece), piece)
        total = tn(refs[0][:, at], refs[pairs][...])
        for p in range(1, pairs):
            total = total + tn(refs[p][:, at], refs[pairs + p][...])
        out_ref[...] = total.astype(BF16)


def outer(line, info, lefts, rights):
    rows, cols = lefts[0].shape[1], rights[0].shape[1]
    return line.run(
        "outer", 20,
        functools.partial(outer_kernel, len(lefts)),
        [*lefts, *rights],
        [full(a.shape) for a in (*lefts, *rights)],
        [out_full((2, rows // 4, cols), BF16)] * 2,
        prefetch=(info,),
    )


def project_grad_kernel(seqs, info_ref, *refs):
    refs = list(refs)

    def take(count):
        got = refs[:count]
        del refs[:count]
        return got

    (low_ref,) = take(1)
    mids = take(seqs)
    (ctx_ref,) = take(1)
    dqs, dks, dvs, dkcs, dvcs, atts = (take(seqs) for _ in range(6))
    block, width = dqs[0].shape
    quart = low_ref.shape[1] // 4 // width
    for far, step in PIECES:
        out_ref = refs[far].at[step]
        for i in range(quart):
            part = quarter(info_ref, far, step) * quart + i
            at = pl.ds(pl.multiple_of(part * width, width), width)
            rows = slice(i * width, (i + 1) * width)
            for k, (grads, more) in enumerate(((dqs, None), (dks, dkcs), (dvs, dvcs))):
                total = 0.0
                for s in range(seqs):
                    total = total + tn(low_ref[s * block : (s + 1) * block, at], grads[s][...])
                    if more is not None:
                        total = total + tn(ctx_ref[part ^ info_ref[2], s * CTX : (s + 1) * CTX, :], more[s][...])
                out_ref[rows, k * width : (k + 1) * width] = total.astype(BF16)
            total = 0.0
            for s in range(seqs):
                total = total + tn(atts[s][...], mids[s][:, at])
            out_ref[rows, 3 * width :] = total.astype(BF16)


def order(p, f):
    return quarter(f, p // 2, p % 2)


def widen_kernel(flags_ref, *refs):
    out_ref = refs[-1]
    for p in range(4):

        @pl.when(pl.program_id(0) == p)
        def _(p=p):
            start = 0
            for ref in refs[p : p + 1] if p < 3 else refs[3:-1]:
                size = ref.shape[0]
                out_ref[start : start + size, :] = ref[...].astype(F32)
                start += size


def widen(line, info, pieces):
    piece, cols = pieces[0].shape
    return line.run(
        "widen", 10,
        widen_kernel,
        pieces,
        [full(p.shape) for p in pieces],
        [((4 * piece, cols), F32, pl.BlockSpec((piece, cols), lambda p, f: (order(p, f), 0)))],
        grid=(4,),
        prefetch=(info,),
    )[0]


def widen_project_kernel(first, count, parts, flags_ref, *refs):
    pieces, outs = refs[:parts], refs[-4:]
    width = pieces[0].shape[1] // 4
    for p in range(count):

        @pl.when(pl.program_id(0) == p)
        def _(p=p):
            start = 0
            for ref in pieces[p : p + 1] if first + p < 3 else pieces[p:]:
                size = ref.shape[0]
                for k in range(3):
                    outs[k][start : start + size, :] = ref[:, k * width : (k + 1) * width].astype(F32)
                step = min(size, width)
                for j in range(0, size, step):
                    row = (start + j) % width
                    to = (start + j) // width * width
                    outs[3][row : row + step, to : to + width] = ref[j : j + step, 3 * width :].astype(F32)
                start += size


def widen_project(line, info, pieces, first, count, before=None):
    rows = pieces[0].shape[0] if first == 0 else sum(p.shape[0] for p in pieces)
    cols = pieces[0].shape[1]
    width = cols // 4
    given = pieces[first : first + count] if first == 0 else pieces
    before = before or []
    return line.run(
        "widen_project", 10,
        functools.partial(widen_project_kernel, first, count, len(given)),
        [*given, *before],
        [full(p.shape) for p in given] + [pl.BlockSpec(memory_space=pl.ANY)] * len(before),
        [((4 * rows, width), F32, pl.BlockSpec((rows, width), lambda p, f: (order(p + first, f), 0)))] * 3
        + [((width, 4 * rows), F32, pl.BlockSpec((width, rows), lambda p, f: (0, order(p + first, f))))],
        grid=(count,),
        prefetch=(info,),
        aliases={1 + len(given) + k: k for k in range(len(before))},
    )


def gather_parts(value, axis):
    parts = [value]
    for bit in reversed(low_bits(lax.axis_size(axis))):
        parts = parts + [None] * 0 + [swap(p, axis, bit) for p in parts]
    count = len(parts)
    order = [0]
    for bit in reversed(low_bits(count)):
        order = order + [k ^ bit for k in order]
    out = [None] * count
    for k, p in zip(order, parts):
        out[k] = p
    return out


def add_low(a, b):
    return (a.astype(F32) + b.astype(F32)).astype(BF16)


def scatter_parts(parts, axis):
    bits = low_bits(lax.axis_size(axis))[1:]
    for bit in bits:
        keep, send = parts[0::2], parts[1::2]
        got = [swap(p, axis, bit) for p in send]
        if bit != bits[-1]:
            parts = [add_low(a, b) for a, b in zip(keep, got)]
    return keep[0], got[0]


(
    AT_PRE, AT_N2_KEEP, AT_N2_SEND, AT_N2_CORE, AT_N2_Y, AT_N2_NEAR, AT_N2_FAR, AT_BACK, AT_GOT, AT_NEAR, AT_Z,
    AT_TOTAL, AT_HOP, AT_QUARTERS, AT_CTX, AT_N1, AT_LEAD, AT_SEEN, AT_CARRY, AT_STATE, AT_OUT_KEEP, AT_OUT_SEND,
    AT_OUT_CORE, AT_OUT_Y, AT_OUT_NEAR, AT_OUT_FAR, AT_OUTPUTS, AT_H1, AT_SMALL, AT_SUMS, AT_MORE, AT_SMALL_GOT,
    AT_INPUT_GRAD, AT_WIDE, DOWN, UP, QUERY, AT_CTX_STACK, VALUE,
) = range(39)
KINDS = {DOWN: 0, UP: 0, QUERY: 4}


def local(
    inputs, out_grad, lengths, norm_gain, query_weight, key_weight, value_weight, out_weight,
    mlp_gain, up_weight, down_weight, decay_rate, state_input, state_output, skip_gain,
):
    seqs, block, model = inputs.shape
    width = query_weight.shape[1]
    units = up_weight.shape[1]
    heads = width // HD
    tiles = width // HD
    stride = block // CTX
    scale = HD ** (-0.5)
    tensor_count = lax.axis_size(TENSOR)
    tensor_bits = low_bits(tensor_count)
    idx = lax.axis_index(TENSOR)
    place = lax.axis_index(SEQ)
    rows = seqs * block
    seg = rows // SUB
    half = model // 2
    pairs = tensor_count // 2
    small_rows = (3 * NS + 2 + tensor_count + 7) // 8 * 8
    seq_bits = low_bits(lax.axis_size(SEQ))
    first, second = seq_bits[:2]
    line = Line()
    info = jnp.concatenate(
        [
            jnp.stack([(place & first) // first, (place & second) // second, idx, idx & 1]).astype(jnp.int32),
            (lengths - place * block).astype(jnp.int32),
        ]
    )

    flat_in = inputs.reshape(rows, model)
    flat_grad = out_grad.reshape(rows, model)
    gain_all = norm_gain.reshape(1, model)
    gain2 = mlp_gain.reshape(1, model)
    gain_chan = lax.dynamic_slice_in_dim(norm_gain, idx * width, width, 0)
    gain_row = gain_chan.reshape(1, width)
    pack = jnp.concatenate(
        [
            decay_rate,
            jnp.sqrt(-jnp.expm1(-2.0 * decay_rate)),
            state_input,
            state_output,
            skip_gain.reshape(1, width),
            gain_row,
            jnp.zeros((PACKED - 4 * NS - 2, width), F32),
        ]
    )
    tab = pltpu.VMEM((NS, SUB, width), F32)
    state_shape = (NS, SUB, width)

    def hop(blocks):
        return jnp.exp(-decay_rate * (jnp.asarray(blocks, F32) * block))[None]

    def rows_of(s):
        return pl.BlockSpec((block, width), lambda *a, s=s: (s, 0))

    wo_parts = gather_parts(out_weight, TENSOR)

    tile = 256
    normed_low, inverse, runs, seg_end, final = line.run(
        "enter", 10,
        functools.partial(enter_kernel, seqs, stride),
        (flat_in, flat_in, gain_all, decay_rate),
        [
            pl.BlockSpec((256, model), lambda i, f: (i, 0)),
            pl.BlockSpec((256, width), lambda i, f: (i, f[2])),
            full((1, model)),
            full((NS, width)),
        ],
        [
            ((rows, model), BF16, pl.BlockSpec((256, model), lambda i, f: (i, 0))),
            ((rows, 1), F32, pl.BlockSpec((256, 1), lambda i, f: (i, 0)), True),
            (*out_full((tiles, seg, SUB, HD), F32), True),
            (*out_full(state_shape, F32), True),
            out_full((seqs, NS, width), F32),
        ],
        grid=(rows // 256,),
        prefetch=(info,),
        scratch=[pltpu.VMEM((tiles, rows, HD), F32), tab, tab],
        hbm=(0, 1, 2, 3),
    )
    carry_in = carried(final, hop, SEQ, True)

    ctx_low, entry = line.run(
        "context", 6,
        functools.partial(context_kernel, seqs, stride),
        (runs, seg_end, carry_in, pack),
        [full((tiles, seg, SUB, HD)), full(state_shape), full((seqs, NS, width)), full((PACKED, width))],
        [out_full((seqs * CTX, width), BF16), (*out_full(state_shape, F32), True)],
        scratch=[tab, tab, tab, pltpu.VMEM((tiles, seqs * CTX, HD), F32)],
        hbm=(0, 1),
    )
    ctx_parts = gather_parts(ctx_low, TENSOR)

    query, key_self, value_self = line.run(
        "qkv", 10,
        qkv_kernel,
        (normed_low, query_weight, key_weight, value_weight),
        [pl.BlockSpec((tile, model), lambda i: (i, 0))] + [full((model, width))] * 3,
        [((rows, width), BF16, pl.BlockSpec((tile, width), lambda i: (i, 0)))] * 3,
        grid=(rows // tile,),
        after=wo_parts[2] if tensor_count > 2 else None,
    )

    attended, key_ctx, value_ctx, log_sum, att_parts = [], [], [], [], []
    for s in range(seqs):
        a, kc, vc, ls = line.run(
            "attend", 12,
            functools.partial(attend_kernel, tensor_count, scale),
            (query, key_self, value_self, key_weight, value_weight, *ctx_parts),
            [rows_of(s)] * 3
            + [full((model, width))] * 2
            + [pl.BlockSpec((CTX, width), lambda *a, s=s: (s, 0))] * tensor_count,
            [
                out_full((block, width), BF16),
                out_full((CTX, width), BF16),
                out_full((CTX, width), BF16),
                out_full((block, heads), F32),
            ],
            prefetch=(info,),
        )
        attended.append(a)
        key_ctx.append(kc)
        value_ctx.append(vc)
        log_sum.append(ls)
        att_parts.append(gather_parts(a, TENSOR))

    steps = block // tile
    middle, normed2, act, slope, cot = ([] for _ in range(5))
    for s in range(seqs):

        def at(cols, s=s):
            return pl.BlockSpec((tile, cols), lambda i, f, s=s: (s * steps + i, 0))

        def own(cols):
            return pl.BlockSpec((tile, cols), lambda i, f: (i, 0))

        got = line.run(
            "feed", 30,
            functools.partial(feed_kernel, tensor_count, tile, s),
            (flat_in, flat_grad, gain2, up_weight, *att_parts[s], *wo_parts),
            [at(model), at(model), full((1, model)), full((model, units))]
            + [own(width)] * tensor_count
            + [full((width, model))] * tensor_count,
            [((block, c), t, own(c)) for c, t in ((model, F32), (model, BF16), (units, BF16), (units, BF16), (model, BF16))],
            grid=(steps,),
            prefetch=(info,),
        )
        for slot, value in zip((middle, normed2, act, slope, cot), got):
            slot.append(value)

    box = {}

    def feed_back(s):
        got = line.run(
            "feed_back", 18,
            feed_back_kernel,
            (cot[s], slope[s], up_weight, down_weight),
            [pl.BlockSpec((tile, model), lambda i, f: (i, 0)), pl.BlockSpec((tile, units), lambda i, f: (i, 0)), full((model, units)), full((units, model))],
            [((block, c), BF16, pl.BlockSpec((tile, c), lambda i, f: (i, 0))) for c in (units, half, half)],
            grid=(steps,),
            prefetch=(info,),
        )
        box[AT_PRE, s], box[AT_N2_KEEP, s] = got[:2]
        box[AT_N2_SEND, s] = swap(got[2], TENSOR, 1)

    def near_core(s):
        box[AT_N2_CORE, s] = add(line, box[AT_N2_KEEP, s], box[AT_N2_SEND, s])
        box[AT_N2_Y, s] = swap(box[AT_N2_CORE, s], TENSOR, tensor_bits[1])

    def near_y(s):
        total = add(line, box[AT_N2_CORE, s], box[AT_N2_Y, s])
        for bit in tensor_bits[2:]:
            total = add(line, total, swap(total, TENSOR, bit))
        box[AT_N2_NEAR, s] = total
        box[AT_N2_FAR, s] = swap(total, TENSOR, 1)

    def attend_back(s):
        outs = [
            ((block, model), BF16), ((block, width), F32), ((1, model), F32),
            ((block, width), BF16), ((block, width), BF16), ((block, width), BF16),
            ((CTX, width), BF16), ((CTX, width), BF16),
            ((pairs, CTX + block, width), BF16), ((pairs, CTX + block, width), BF16),
        ]
        got = line.run(
            "attend_back", 28,
            functools.partial(attend_back_kernel, s, scale),
            (middle[s], box[AT_N2_NEAR, s], box[AT_N2_FAR, s], flat_grad, gain2, out_weight, query, key_self, value_self, key_ctx[s], value_ctx[s], log_sum[s], query_weight, key_weight, value_weight),
            [full((block, model)), full((block, half)), full((block, half)), pl.BlockSpec((block, model), lambda *a, s=s: (s, 0)), full((1, model)), full((width, model))]
            + [rows_of(s)] * 3
            + [full((CTX, width))] * 2
            + [full((block, heads))]
            + [full((model, width))] * 3,
            [out_full(*o) for o in outs],
            prefetch=(info,),
            scratch=[pltpu.VMEM((block, model), BF16), pltpu.VMEM((block, model), F32)]
            + [pltpu.VMEM((block, HD), F32)] * 2
            + [pltpu.VMEM((CTX, HD), F32)] * 2,
        )

        box[AT_BACK, s] = got
        box[AT_GOT, s] = swap(got[9], TENSOR, 1)

    def backs(k):
        return [box[AT_BACK, s][k] for s in range(seqs)]

    def both(key):
        return [box[key, s] for s in range(seqs)]

    def sum_start(key, pieces):
        box[key] = pieces[0], swap(pieces[1], SEQ, bits_of[key][0])

    def sum_second(key):
        near, far = add_pair(line, *box[key])
        box[key, AT_NEAR], box[key, AT_Z] = near, swap(far, SEQ, bits_of[key][1])

    def sum_third(key):
        total = add(line, box[key, AT_NEAR], box[key, AT_Z])
        for bit in bits_of[key][2:-1]:
            total = add(line, total, swap(total, SEQ, bit))
        box[key, AT_TOTAL] = total
        if len(seq_bits) > 2:
            box[key, AT_HOP] = swap(total, SEQ, bits_of[key][-1])

    def sum_last(key):
        total = box[key, AT_TOTAL]
        if len(seq_bits) > 2:
            total = add(line, total, box[key, AT_HOP])
        one, two = bits_of[key][:2]
        across, along = swap(total, SEQ, two), swap(total, SEQ, one)
        last = KINDS[key] >> 1
        if last == 0:
            far = [swap(across, SEQ, one)]
        elif last == 1:
            far = [swap(along, SEQ, two)]
        else:
            size = total.shape[0] // 2
            far = [swap(across[:size], SEQ, one), swap(along[size:], SEQ, two)]
        box[key, AT_QUARTERS] = [total, across, along, *far]

    def pin(key, k):
        line.held.append(box[key, AT_QUARTERS][k])

    def project():
        mid_low, mid_slice, gain2_part, dq, dk, dv, dkc, dvc = (backs(k) for k in range(8))
        ctx_stack = jnp.stack(ctx_parts)
        ins = (normed_low, *mid_low, ctx_stack, *dq, *dk, *dv, *dkc, *dvc, *attended)
        got = (
            line.run(
                "project_grad", 28,
                functools.partial(project_grad_kernel, seqs),
                ins,
                [full(a.shape) for a in ins],
                [out_full((2, model // 4, 4 * width), BF16)] * 2,
                prefetch=(info,),
                )
        )
        sum_start(QUERY, got)

    def ctx_parts_sum():
        box[AT_CTX] = scatter_parts(add_parts(line, backs(8), both(AT_GOT), 0, CTX), TENSOR)

    def n1_parts_sum():
        box[AT_N1] = scatter_parts(add_parts(line, backs(8), both(AT_GOT), CTX, block), TENSOR)

    def lead_step():
        ctx_near, ctx_far = box[AT_CTX]
        ctx_grads, segb_end, lead = line.run(
            "lead", 4,
            functools.partial(lead_kernel, seqs, stride),
            (ctx_near, ctx_far, pack),
            [vmem()] * 3,
            [(*out_full((tiles, seqs * CTX // SUB, SUB, HD), F32), True), (state_shape, F32, vmem()), ((seqs, NS, width), F32, vmem())],
            scratch=[pltpu.VMEM((tiles, seqs * CTX, HD), F32), tab],
        )
        box[AT_LEAD] = ctx_grads, segb_end
        box[AT_SEEN] = []
        box[AT_CARRY] = carried(lead, hop, SEQ, False, box[AT_SEEN])

    def state_step():
        ctx_grads, segb_end = box[AT_LEAD]
        carry_back = box[AT_CARRY]
        box[AT_STATE] = line.run(
            "state_back", 10,
            functools.partial(state_back_kernel, seqs, stride),
            (runs, ctx_grads, entry, segb_end, carry_back, pack),
            [
                full((tiles, seg, SUB, HD)),
                full((tiles, seqs * CTX // SUB, SUB, HD)),
                full(state_shape),
                full(state_shape),
                full((seqs, NS, width)),
                full((PACKED, width)),
            ],
            [out_full((tiles, rows, HD), F32), out_full((small_rows, width), F32)],
            scratch=[
                tab,
                tab,
                pltpu.VMEM((stride, NS, SUB, width), F32),
                tab,
                pltpu.VMEM((seg // stride + 1, NS, SUB, width), F32),
                pltpu.VMEM((tiles, seg, SUB, HD), F32),
                pltpu.VMEM((stride + 2, NS, width), F32),
            ],
            hbm=(0, 1, 2),
        )

    def feed_out():
        got = line.run(
            "feed_out", 14,
            functools.partial(feed_out_kernel, seqs, steps),
            (*act, down_weight),
            [pl.BlockSpec((tile, units), lambda i, f, s=s: (jnp.clip(i - s * steps, 0, steps - 1), 0)) for s in range(seqs)]
            + [full((units, model))],
            [((rows, half), BF16, pl.BlockSpec((tile, half), lambda i, f: (i, 0)))] * 2,
            grid=(seqs * steps,),
            prefetch=(info,),
        )
        box[AT_OUT_KEEP], box[AT_OUT_SEND] = got[0], swap(got[1], TENSOR, 1)

    def out_core():
        total = add(line, box[AT_OUT_KEEP], box[AT_OUT_SEND])
        for bit in tensor_bits[1:-1]:
            total = add(line, total, swap(total, TENSOR, bit))
        box[AT_OUT_CORE], box[AT_OUT_Y] = total, swap(total, TENSOR, tensor_bits[-1])

    def out_add():
        box[AT_OUT_NEAR] = line.run(
            "add_out", 12,
            functools.partial(add_out_kernel, seqs),
            (*middle, box[AT_OUT_CORE], box[AT_OUT_Y]),
            [full((block, model))] * seqs + [full((rows, half))] * 2,
            [out_full((rows, half), BF16)],
            prefetch=(info,),
        )[0]
        box[AT_OUT_FAR] = swap(box[AT_OUT_NEAR], TENSOR, 1)

    def join():
        box[AT_OUTPUTS] = line.run(
            "join", 6,
            join_kernel,
            (box[AT_OUT_NEAR], box[AT_OUT_FAR]),
            [pl.BlockSpec((tile, half), lambda i, f: (i, 0))] * 2,
            [((rows, model), BF16, pl.BlockSpec((tile, model), lambda i, f: (i, 0)))],
            grid=(rows // tile,),
            prefetch=(info,),
        )[0].reshape(seqs, block, model)

    def norm_back():
        chan_grad, pack_grad = box[AT_STATE]
        h1, small, sums = line.run(
            "norm_back", 12,
            functools.partial(norm_back_kernel, seqs),
            (*box[AT_N1], chan_grad, in_chan, inverse, pack, pack_grad, *backs(2)),
            [full((rows, width))] * 2
            + [full((tiles, rows, HD)), full((rows, width)), full((rows, 1)), full((PACKED, width)), full((small_rows, width))]
            + [full((1, model))] * seqs,
            [out_full((rows, width), F32), out_full((small_rows, width), F32), out_full((SUB, rows), F32)],
        )
        box[AT_H1], box[AT_SMALL] = h1, small
        box[AT_SUMS], box[AT_MORE] = sums, swap(sums, TENSOR, 1)
        box[AT_SMALL_GOT] = swap(small, SEQ, seq_bits[0])

    def row_sums():
        total = add_wide(line, box[AT_SUMS], box[AT_MORE])
        for bit in tensor_bits[1:-1]:
            total = add_wide(line, total, swap(total, TENSOR, bit))
        box[AT_SUMS], box[AT_MORE] = total, swap(total, TENSOR, tensor_bits[-1])

    def input_step():
        box[AT_INPUT_GRAD] = line.run(
            "input_grad", 12,
            functools.partial(input_grad_kernel, seqs, model),
            (box[AT_H1], box[AT_SUMS], box[AT_MORE], in_chan, inverse, *backs(1)),
            [full((rows, width)), full((SUB, rows)), full((SUB, rows)), full((rows, width)), full((rows, 1))]
            + [full((block, width))] * seqs,
            [out_full((rows, width), BF16)],
        )[0]

    def small_step(k):
        total = add_wide(line, box[AT_SMALL], box[AT_SMALL_GOT])
        box[AT_SMALL] = total
        later = seq_bits[k + 1 :]
        if k == 2:
            for bit in later:
                box[AT_SMALL] = add_wide(line, box[AT_SMALL], swap(box[AT_SMALL], SEQ, bit))
        elif later:
            box[AT_SMALL_GOT] = swap(total, SEQ, later[0])

    def flags_of(key):
        return swapped if KINDS[key] & 1 else info

    def widen_step(key):
        pieces = box[key, AT_QUARTERS]
        if key == QUERY:
            early = widen_project(line, flags_of(key), pieces[:3], 0, 3)
            box[key, AT_WIDE] = widen_project(line, flags_of(key), pieces[3:], 3, 1, early)
        else:
            box[key, AT_WIDE] = widen(line, flags_of(key), pieces)

    in_chan = lax.dynamic_slice_in_dim(flat_in, idx * width, width, 1)
    swapped = jnp.concatenate([info[1::-1], info[2:]])
    bits_of = {key: [second, first, *seq_bits[2:]] if kind & 1 else seq_bits for key, kind in KINDS.items()}
    feed_back(0)
    sum_start(DOWN, outer(line, flags_of(DOWN), act, cot))
    near_core(0)
    feed_back(1)
    sum_start(UP, outer(line, flags_of(UP), normed2, both(AT_PRE)))
    near_core(1)
    near_y(0)
    sum_second(DOWN)
    near_y(1)
    attend_back(0)
    sum_third(DOWN)
    attend_back(1)
    sum_second(UP)
    project()
    feed_out()
    ctx_parts_sum()
    lead_step()
    n1_parts_sum()
    sum_last(DOWN)
    sum_third(UP)
    sum_second(QUERY)
    sum_last(UP)
    state_step()
    pin(DOWN, 1)
    pin(UP, 2)
    pin(DOWN, 2)
    out_core()
    sum_third(QUERY)
    norm_back()
    row_sums()
    small_step(0)
    line.held.append(box[AT_SEEN][0])
    widen_step(DOWN)
    small_step(1)
    sum_last(QUERY)
    widen_step(UP)
    pin(UP, 3)
    input_step()
    pin(DOWN, 3)
    line.held.append(box[AT_SEEN][2])
    line.held.append(box[AT_SEEN][1])
    pin(QUERY, 2)
    small_step(2)
    out_add()
    join()
    widen_step(QUERY)
    outputs, down_grad, up_grad = box[AT_OUTPUTS], box[DOWN, AT_WIDE], box[UP, AT_WIDE]
    query_grad, key_grad, value_grad, out_grad_w = box[QUERY, AT_WIDE]
    input_grad = box[AT_INPUT_GRAD].reshape(seqs, block, width)
    small = box[AT_SMALL]
    return (
        outputs,
        input_grad,
        small[3 * NS + 1],
        query_grad,
        key_grad,
        value_grad,
        out_grad_w,
        small[3 * NS + 2 : 3 * NS + 2 + model // width].reshape(model),
        up_grad,
        down_grad,
        small[:NS],
        small[NS : 2 * NS],
        small[2 * NS : 3 * NS],
        small[3 * NS],
    )


def solution(mesh):
    in_specs = (
        P(None, SEQ, None),
        P(None, SEQ, None),
        P(),
        P(),
        P(None, TENSOR),
        P(None, TENSOR),
        P(None, TENSOR),
        P(TENSOR, None),
        P(),
        P(None, TENSOR),
        P(TENSOR, None),
        P(None, TENSOR),
        P(None, TENSOR),
        P(None, TENSOR),
        P(TENSOR),
    )
    out_specs = (
        P(None, SEQ, None),
        P(None, SEQ, TENSOR),
        P(TENSOR),
        P(None, TENSOR),
        P(None, TENSOR),
        P(None, TENSOR),
        P(TENSOR, None),
        P(),
        P(None, TENSOR),
        P(TENSOR, None),
        P(None, TENSOR),
        P(None, TENSOR),
        P(None, TENSOR),
        P(TENSOR),
    )
    return jax.shard_map(local, mesh=mesh, in_specs=in_specs, out_specs=out_specs, check_vma=False)
```
